32 devices in a mesh: wide: 16 (over z, x, core), narrow: 2 (over y).
Axes of the slice: x: 2, y: 2, z: 4, core: 2. Of those that a mesh axis runs over, the one named last changes fastest.
Arguments:
- initial: float32 [16, 2, 128, 2048], P('wide', 'narrow'), may hold values from -6 to 6
- block_values: bfloat16 [16, 12, 128, 128], replicated, may hold values from -0.0546875 to 0.0546875
- block_index: int32 [16, 12], replicated, may hold values from 0 to 15, as said below
- bond_sites: int32 [12, 2], replicated, may hold values from 0 to 6, as said below
- bond_coupling: float32 [12], replicated, may hold values from -0.25 to 0.25
- pin_sites: int32 [8], replicated, may hold values from 0 to 6
- pin_partner: int32 [8], replicated, may hold values from 0 to 13
- pinned_spins: int32 [14], replicated, may hold values from 0 to 1
- pin_coupling: float32 [8], replicated, may hold values from -0.2 to 0.2
- cross_sites: int32 [4], replicated, may hold values from 0 to 6
- cross_coupling: float32 [4], replicated, may hold values from 0.2 to 0.4
Outputs:
- previous_vector: float32 [16, 2, 128, 2048], P('wide', 'narrow')
- chebyshev_vector: float32 [16, 2, 128, 2048], P('wide', 'narrow')
The draws below stay inside these ranges and needn't reach their ends.
Inputs may be any that keep to these rules, and one draw needn't show every extreme that they name: `block_index`: each row names 12 different block columns. `bond_sites`: the two spins of a bond differ.
All inputs are finite; a program needn't handle non-finite values.
Results may differ from the reference program's by a relative error of at most 0.0031.
Values may be sent and summed in bfloat16 or wider, within the bound.
No kernel may reach another device: no remote copies, remote signals or barrier semaphores. Data moves between devices by JAX's collectives and lax.ppermute only.
A program may use at most 128 MiB of HBM per device.

```python
import jax
import jax.numpy as jnp
from jax import lax

BLOCK = 128
KBLOCKS = 12
BROWS = 16
LOWDIM = 2048
CBITS = 7
COLUMNS = 128
BONDS = 12
PBONDS = 8
PINNED = 14
CROSS = 4
STEPS = 4
WSLABS = 16
NSLABS = 2


def draw_block_index(key, part):
    row_keys = jax.random.split(jax.random.fold_in(key, 11), BROWS)
    orders = jax.vmap(lambda one_key: jax.random.permutation(one_key, BROWS))(row_keys)
    return orders[:, :KBLOCKS].astype(jnp.int32)


def draw_bond_sites(key, part):
    first_key, second_key = jax.random.split(jax.random.fold_in(key, 23))
    site_one = jax.random.randint(first_key, (BONDS,), 0, CBITS)
    offset = jax.random.randint(second_key, (BONDS,), 1, CBITS)
    site_two = (site_one + offset) % CBITS
    return jnp.stack([site_one, site_two], axis=1).astype(jnp.int32)


def plant(result, own_key, low, largest):
    dims = result.shape
    index_at = [jax.random.randint(jax.random.fold_in(own_key, axis), (), 0, dims[axis]) for axis in range(len(dims))]
    result = result.at[tuple(index_at)].set(low)
    longest = dims.index(max(dims))
    index_at[longest] = (index_at[longest] + 1) % dims[longest]
    return result.at[tuple(index_at)].set(largest)


def levels(stream_key, shape, pieces, low, largest):
    level = 1.0
    for axis_at, shards_of in pieces:
        steps = jax.random.uniform(jax.random.fold_in(jax.random.fold_in(stream_key, 6), axis_at), (shards_of,), jnp.float32, low / len(pieces), largest / len(pieces))
        level = level * jnp.repeat(jnp.exp(steps), shape[axis_at] // shards_of).reshape((-1,) + (1,) * (len(shape) - 1 - axis_at))
    return level


def normal_values(own_key, extent, width, most, shards=(), held_as=jnp.bfloat16):
    drawn = jax.random.normal(own_key, extent, jnp.float32) * width
    if len(shards) > 0:
        drawn = levels(own_key, extent, shards, -0.22, 0.18) * drawn
    return jnp.clip(drawn, min=-most, max=most).astype(held_as)


def setup_inputs(seed: int = 0) -> dict:
    keys = jax.random.split(jax.random.key(seed), 12)
    return {
        "initial": normal_values(keys[0], (WSLABS, NSLABS, COLUMNS, LOWDIM), 1.0, 6.0, ((0, 16), (1, 2)), jnp.float32),
        "block_values": normal_values(keys[1], (BROWS, KBLOCKS, BLOCK, BLOCK), (8 * KBLOCKS * BLOCK) ** -0.5, 0.0546875),
        "block_index": draw_block_index(jax.random.fold_in(keys[11], 71), 0),
        "bond_sites": draw_bond_sites(jax.random.fold_in(keys[11], 71), 0),
        "bond_coupling": jnp.clip(jax.random.uniform(keys[4], (BONDS,), jnp.float32, -0.25, 0.25), -0.25, 0.25),
        "pin_sites": plant(jax.random.randint(keys[5], (PBONDS,), 0, CBITS), jax.random.fold_in(keys[5], 1), 0, CBITS - 1).astype(jnp.int32),
        "pin_partner": plant(jax.random.randint(keys[6], (PBONDS,), 0, PINNED), jax.random.fold_in(keys[6], 1), 0, PINNED - 1).astype(jnp.int32),
        "pinned_spins": plant(jax.random.randint(keys[7], (PINNED,), 0, 2), jax.random.fold_in(keys[7], 1), 0, 1).astype(jnp.int32),
        "pin_coupling": jnp.clip(jax.random.uniform(keys[8], (PBONDS,), jnp.float32, -0.2, 0.2), -0.2, 0.2),
        "cross_sites": plant(jax.random.randint(keys[9], (CROSS,), 0, CBITS), jax.random.fold_in(keys[9], 1), 0, CBITS - 1).astype(jnp.int32),
        "cross_coupling": jnp.clip(jax.random.uniform(keys[10], (CROSS,), jnp.float32, 0.2, 0.4), 0.2, 0.4),
    }


def bit_at(values, position):
    return jnp.bitwise_and(jnp.right_shift(values, position), 1)


def column_operator(bond_sites, bond_coupling, pin_sites, pin_partner, pinned_spins, pin_coupling):
    columns = jnp.arange(COLUMNS, dtype=jnp.int32)
    site_one = bit_at(columns[None, :], bond_sites[:, 0:1])
    site_two = bit_at(columns[None, :], bond_sites[:, 1:2])
    differ = (site_one != site_two).astype(jnp.float32)
    flip_bits = jnp.bitwise_xor(jnp.left_shift(jnp.int32(1), bond_sites[:, 0:1]), jnp.left_shift(jnp.int32(1), bond_sites[:, 1:2]))
    target = jnp.bitwise_xor(columns[None, :], flip_bits)
    hopping = (target[:, :, None] == columns[None, None, :]).astype(jnp.float32)
    hopping_part = jnp.sum((bond_coupling[:, None] * differ * 0.5)[:, :, None] * hopping, axis=0)
    diagonal = jnp.sum(bond_coupling[:, None] * (1.0 - 2.0 * differ) * 0.25, axis=0)
    chosen = pin_partner[:, None] == jnp.arange(PINNED, dtype=jnp.int32)[None, :]
    pinned = jnp.sum(jnp.where(chosen, pinned_spins[None, :], 0), axis=1).astype(jnp.int32)
    pin_bits = bit_at(columns[None, :], pin_sites[:, None])
    aligned = jnp.bitwise_xor(pin_bits, pinned[:, None]).astype(jnp.float32)
    pin_field = jnp.sum(pin_coupling[:, None] * (1.0 - 2.0 * aligned) * 0.25, axis=0)
    return hopping_part + jnp.diag(diagonal + pin_field)


def apply_whole(state, matrix, values_wide, block_index, cross_sites, cross_coupling):
    rounded = state.astype(jnp.bfloat16)
    flat = rounded.reshape(WSLABS * NSLABS, COLUMNS, BROWS, BLOCK)

    def one_slab(slab):
        blocks = jnp.take(slab, block_index, axis=1).astype(jnp.float32)
        return jnp.einsum("crkp,rkpq->crq", blocks, values_wide, precision=lax.Precision.HIGHEST)

    low_part = lax.map(one_slab, flat).reshape(state.shape)
    column_part = jnp.einsum("cd,wndl->wncl", matrix, state, precision=lax.Precision.HIGHEST)
    summed = low_part + column_part
    wide_log = WSLABS.bit_length() - 1
    narrow_log = NSLABS.bit_length() - 1
    columns = jnp.arange(COLUMNS, dtype=jnp.int32)
    for bond_slot, slab_axis, position, slab_count in ((0, 0, wide_log - 1, WSLABS), (1, 0, 0, WSLABS), (2, 1, narrow_log - 1, NSLABS), (3, 1, 0, NSLABS)):
        slab_ids = jnp.arange(slab_count, dtype=jnp.int32)
        own_bits = bit_at(slab_ids, position)
        partner_ids = jnp.bitwise_xor(slab_ids, 1 << position).astype(jnp.int32)
        partner = jnp.take(rounded, partner_ids, axis=slab_axis)
        cross_site = cross_sites[bond_slot]
        column_bit = bit_at(columns, cross_site)
        flipped_ids = jnp.bitwise_xor(columns, jnp.left_shift(jnp.int32(1), cross_site)).astype(jnp.int32)
        flipped = jnp.take(partner, flipped_ids, axis=2).astype(jnp.float32)
        if slab_axis == 0:
            own_shaped = own_bits.reshape((-1, 1, 1, 1))
        else:
            own_shaped = own_bits.reshape((1, -1, 1, 1))
        parity = jnp.bitwise_xor(own_shaped, column_bit.reshape((1, 1, -1, 1))).astype(jnp.float32)
        summed = summed + cross_coupling[bond_slot] * ((1.0 - 2.0 * parity) * 0.25 * state + parity * 0.5 * flipped)
    return summed


def reference(initial, block_values, block_index, bond_sites, bond_coupling, pin_sites, pin_partner, pinned_spins, pin_coupling, cross_sites, cross_coupling):
    matrix = column_operator(bond_sites, bond_coupling, pin_sites, pin_partner, pinned_spins, pin_coupling)
    values_wide = block_values.astype(jnp.float32)
    previous = initial
    current = apply_whole(previous, matrix, values_wide, block_index, cross_sites, cross_coupling)
    for repeat in range(STEPS - 1):
        following = 2.0 * apply_whole(current, matrix, values_wide, block_index, cross_sites, cross_coupling) - previous
        previous, current = current, following
    return previous, current
```

```python
import functools

import jax
import jax.numpy as jnp
from jax import lax
from jax.experimental import pallas as pl
from jax.experimental.pallas import tpu as pltpu
from jax.sharding import PartitionSpec as P

CHUNKS = 4
TILE = 256
F32 = jnp.float32
BF16 = jnp.bfloat16


def partner(block, axis, position):
    count = lax.axis_size(axis)
    return lax.ppermute(block, axis, [(at, at ^ (1 << position)) for at in range(count)])


def split(value):
    high = value.astype(BF16)
    return high, (value - high.astype(F32)).astype(BF16)


def dot(left, right):
    return jnp.dot(left, right, preferred_element_type=F32)


def low_kernel(index_ref, values_ref, state_ref, dense_ref, product_ref):
    tile = pl.program_id(0)
    rows, kept, size, _ = values_ref.shape
    dense_ref[...] = jnp.zeros(dense_ref.shape, BF16)
    for row in range(rows):
        for slot in range(kept):
            start = pl.multiple_of(index_ref[tile * rows + row, slot] * size, size)
            dense_ref[0, pl.ds(start, size), row * size : (row + 1) * size] = values_ref[row, slot]
    product_ref[...] = dot(state_ref[...], dense_ref[0])


def low_operator(block_values, block_index, rounded):
    brows, kept, size, _ = block_values.shape
    width = brows * size
    rows = TILE // size
    columns = rounded.shape[0]
    return pl.pallas_call(
        low_kernel,
        grid=(brows // rows,),
        in_specs=[
            pl.BlockSpec(memory_space=pltpu.SMEM),
            pl.BlockSpec((rows, kept, size, size), lambda t: (t, 0, 0, 0)),
            pl.BlockSpec((columns, width), lambda t: (0, 0)),
        ],
        out_specs=[
            pl.BlockSpec((1, width, TILE), lambda t: (t, 0, 0)),
            pl.BlockSpec((columns, TILE), lambda t: (0, t)),
        ],
        out_shape=[
            jax.ShapeDtypeStruct((width // TILE, width, TILE), BF16),
            jax.ShapeDtypeStruct((columns, width), F32),
        ],
        compiler_params=pltpu.CompilerParams(vmem_limit_bytes=24 * 2**20),
        name="low_operator",
    )(block_index, block_values, rounded)


def bit_of(values, position):
    return jnp.bitwise_and(jnp.right_shift(values, position), 1)


def polynomial_kernel(
    spin_of_bond,
    sites_ref,
    coupling_ref,
    pin_sites_ref,
    pin_partner_ref,
    pinned_ref,
    pin_coupling_ref,
    cross_sites_ref,
    cross_coupling_ref,
    own_ref,
    high_ref,
    low_ref,
    op_high,
    op_low,
    rows_ref,
):
    size = rows_ref.shape[1]
    whole = rows_ref.shape[2]
    blocks = whole // size
    row = lax.broadcasted_iota(jnp.int32, (size, size), 0)
    col = lax.broadcasted_iota(jnp.int32, (size, size), 1)
    same = row == col
    zero = jnp.zeros((size, size), F32)
    matrix = zero
    field = zero
    for bond in range(sites_ref.shape[0]):
        one, two = sites_ref[bond, 0], sites_ref[bond, 1]
        strength = coupling_ref[bond]
        differ = jnp.bitwise_xor(bit_of(row, one), bit_of(row, two)).astype(F32)
        flips = jnp.bitwise_xor(
            jnp.left_shift(jnp.int32(1), one), jnp.left_shift(jnp.int32(1), two)
        )
        matrix += jnp.where(col == jnp.bitwise_xor(row, flips), strength * 0.5 * differ, 0.0)
        field += strength * (1.0 - 2.0 * differ) * 0.25
    for pin in range(pin_sites_ref.shape[0]):
        pinned = pinned_ref[pin_partner_ref[pin]]
        aligned = jnp.bitwise_xor(bit_of(row, pin_sites_ref[pin]), pinned).astype(F32)
        field += pin_coupling_ref[pin] * (1.0 - 2.0 * aligned) * 0.25
    spins = max(spin_of_bond) + 1
    fields = [[zero, zero] for _ in range(spins)]
    hops = [[zero, zero] for _ in range(spins)]
    for bond, spin in enumerate(spin_of_bond):
        site = cross_sites_ref[bond]
        strength = cross_coupling_ref[bond]
        target = jnp.bitwise_xor(row, jnp.left_shift(jnp.int32(1), site))
        for turned in range(2):
            own = jnp.bitwise_xor(own_ref[spin], turned)
            parity = jnp.bitwise_xor(bit_of(row, site), own).astype(F32)
            fields[spin][turned] += strength * (1.0 - 2.0 * parity) * 0.25
            hops[spin][turned] += jnp.where(col == target, strength * 0.5 * parity, 0.0)
    hop_parts = [[split(hops[spin][turned]) for turned in range(2)] for spin in range(spins)]
    op_high[...] = jnp.zeros(op_high.shape, BF16)
    op_low[...] = jnp.zeros(op_low.shape, BF16)
    rows_ref[0] = jnp.zeros((size, whole), F32)
    rows_ref[1] = jnp.zeros((size, whole), F32)
    rows_ref[0, :, :size] = jnp.where(same, 1.0, 0.0)
    for block in range(blocks):
        at = slice(block * size, (block + 1) * size)
        own_field = field
        for spin in range(spins):
            turned = block >> spin & 1
            own_field = own_field + fields[spin][turned]
            other = block ^ 1 << spin
            high, low = hop_parts[spin][turned]
            op_high[at, other * size : (other + 1) * size] = high
            op_low[at, other * size : (other + 1) * size] = low
            if block == 0:
                rows_ref[1, :, other * size : (other + 1) * size] = hops[spin][turned]
        diagonal = matrix + jnp.where(same, own_field, 0.0)
        high, low = split(diagonal)
        op_high[at, at] = high
        op_low[at, at] = low
        if block == 0:
            rows_ref[1, :, at] = diagonal
    orders = high_ref.shape[0] // size
    tile = min(TILE, whole)
    for order in range(1, orders + 1):
        high, low = split(rows_ref[order])
        high_ref[(order - 1) * size : order * size, :] = high
        low_ref[(order - 1) * size : order * size, :] = low
        if order == orders:
            break
        both = jnp.concatenate([high, low], axis=0)
        for start in range(0, whole, tile):
            at = slice(start, start + tile)
            product = dot(both, op_high[:, at])
            product = product[:size] + product[size:] + dot(high, op_low[:, at])
            rows_ref[order + 1, :, at] = 2.0 * product - rows_ref[order - 1, :, at]


def polynomial_rows(
    columns, spin_of_bond, orders, sites, coupling, pin_sites, pin_partner, pinned, pin_coupling, cross_sites, cross_coupling, own_bits
):
    whole = columns << (max(spin_of_bond) + 1)
    operands = (sites, coupling, pin_sites, pin_partner, pinned, pin_coupling, cross_sites, cross_coupling, own_bits)
    out = jax.ShapeDtypeStruct((orders * columns, whole), BF16)
    return pl.pallas_call(
        functools.partial(polynomial_kernel, spin_of_bond),
        in_specs=[pl.BlockSpec(memory_space=pltpu.SMEM)] * len(operands),
        out_specs=[pl.BlockSpec(memory_space=pltpu.VMEM)] * 2,
        out_shape=[out, out],
        scratch_shapes=[
            pltpu.VMEM((whole, whole), BF16),
            pltpu.VMEM((whole, whole), BF16),
            pltpu.VMEM((orders + 1, columns, whole), F32),
        ],
        compiler_params=pltpu.CompilerParams(vmem_limit_bytes=40 * 2**20),
        name="polynomial_rows",
    )(*operands)


def chunk_kernel(pieces, *refs):
    state_ref, product_ref, high_ref, low_ref = refs[:4]
    piece_refs = refs[4 : 4 + pieces]
    start_ref, terms_ref = refs[-2:]
    size, width = state_ref.shape
    tile = min(TILE, width)
    for start in range(0, width, tile):
        at = slice(start, start + tile)
        state = state_ref[:, at]
        own, rest = split(state)
        gathered = jnp.concatenate([own] + [ref[:, at] for ref in piece_refs], axis=0)
        powers = dot(high_ref[...], gathered) + dot(low_ref[...], gathered)
        powers += dot(high_ref[:, :size], rest)
        one, two, three, four = (powers[k * size : (k + 1) * size] for k in range(4))
        product = product_ref[:, at]
        start_ref[:size, at] = (8.0 * product + 32.0 * one).astype(BF16)
        start_ref[size:, at] = (4.0 * product + 12.0 * one).astype(BF16)
        terms_ref[0, :, at] = 24.0 * two + 16.0 * state
        terms_ref[1, :, at] = 6.0 * two + 3.0 * state
        terms_ref[2, :, at] = 8.0 * (three + one)
        terms_ref[3, :, at] = three
        terms_ref[4, :, at] = four


def chunk_terms(chunk, width, state, product, high, low, pieces, held):
    columns, states = state.shape
    block = pl.BlockSpec((columns, width), lambda t: (0, chunk))
    full = pl.BlockSpec(memory_space=pltpu.VMEM)
    piece_specs = [
        pl.BlockSpec((columns, width), (lambda t: (0, 0)) if piece.shape[1] == width else (lambda t: (0, chunk)))
        for piece in pieces
    ]
    operands = [state, product, high, low, *pieces]
    specs = [block, block, full, full, *piece_specs]
    aliases = {}
    if held is not None:
        aliases = {len(operands): 0, len(operands) + 1: 1}
        operands += held
        specs += [pl.BlockSpec(memory_space=pl.ANY)] * 2
    return pl.pallas_call(
        functools.partial(chunk_kernel, len(pieces)),
        grid=(1,),
        in_specs=specs,
        out_specs=[
            pl.BlockSpec((2 * columns, width), lambda t: (0, chunk)),
            pl.BlockSpec((5, columns, width), lambda t: (0, 0, chunk)),
        ],
        out_shape=[
            jax.ShapeDtypeStruct((2 * columns, states), BF16),
            jax.ShapeDtypeStruct((5, columns, states), F32),
        ],
        input_output_aliases=aliases,
        compiler_params=pltpu.CompilerParams(vmem_limit_bytes=24 * 2**20),
        name="chunk_terms",
    )(*operands)


def final_kernel(
    start_hbm, terms_hbm, dense_hbm, third_ref, fourth_ref, left, second, last, dense, terms, dense_sems, term_sems, start_sem
):
    tiles, states, tile = dense.shape
    size = third_ref.shape[0]

    def dense_copy(t):
        return pltpu.make_async_copy(dense_hbm.at[t], dense.at[t], dense_sems.at[t])

    def term_copy(slot):
        return pltpu.make_async_copy(terms_hbm.at[slot], terms.at[slot], term_sems.at[slot])

    start_copy = pltpu.make_async_copy(start_hbm, left, start_sem)
    start_copy.start()
    dense_copy(0).start()
    term_copy(0).start()
    term_copy(1).start()
    for t in range(1, tiles):
        dense_copy(t).start()
    for slot in range(2, 5):
        term_copy(slot).start()
    start_copy.wait()
    term_copy(0).wait()
    term_copy(1).wait()

    def columns(t):
        return pl.ds(pl.multiple_of(t * tile, tile), tile)

    @pl.loop(0, tiles)
    def _(t):
        dense_copy(t).wait()
        at = columns(t)
        product = dot(left[...], dense[t])
        second[:size, at] = (product[:size] + terms[0, :, at]).astype(BF16)
        second[size:, at] = (product[size:] + terms[1, :, at]).astype(BF16)

    for slot in range(2, 5):
        term_copy(slot).wait()

    @pl.loop(0, tiles)
    def _(t):
        at = columns(t)
        product = dot(second[...], dense[t])
        high, low = split(product[:size] + terms[2, :, at])
        last[:size, at] = high
        last[size:, at] = low
        third_ref[:, at] = product[size:] + terms[3, :, at]

    @pl.loop(0, tiles)
    def _(t):
        at = columns(t)
        product = dot(last[...], dense[t])
        fourth_ref[:, at] = product[:size] + product[size:] + terms[4, :, at]


def final_vectors(start, terms, dense):
    slots, columns, states = terms.shape
    tiles, _, tile = dense.shape
    out = jax.ShapeDtypeStruct((columns, states), F32)
    return pl.pallas_call(
        final_kernel,
        in_specs=[pl.BlockSpec(memory_space=pl.ANY)] * 3,
        out_specs=[pl.BlockSpec(memory_space=pltpu.VMEM)] * 2,
        out_shape=[out, out],
        scratch_shapes=[
            pltpu.VMEM((2 * columns, states), BF16),
            pltpu.VMEM((2 * columns, states), BF16),
            pltpu.VMEM((2 * columns, states), BF16),
            pltpu.VMEM((tiles, states, tile), BF16),
            pltpu.VMEM((slots, columns, states), F32),
            pltpu.SemaphoreType.DMA((tiles,)),
            pltpu.SemaphoreType.DMA((slots,)),
            pltpu.SemaphoreType.DMA,
        ],
        compiler_params=pltpu.CompilerParams(vmem_limit_bytes=40 * 2**20),
        name="final_vectors",
    )(start, terms, dense)


def device_spins():
    wide_log = lax.axis_size("wide").bit_length() - 1
    narrow_log = lax.axis_size("narrow").bit_length() - 1
    of_bond = [("wide", wide_log - 1), ("wide", 0), ("narrow", narrow_log - 1), ("narrow", 0)]
    spins = []
    for bond in (0, 2, 3, 1):
        if of_bond[bond] not in spins:
            spins.append(of_bond[bond])
    return spins, [spins.index(spin) for spin in of_bond]


def gather(rounded, spins, width):
    states = rounded.shape[1]
    late = [
        {1: partner(rounded[:, start : start + width], *spins[0])} for start in range(0, states, width)
    ]
    early = {0: rounded}
    for at, spin in enumerate(spins[1:], 1):
        for owner in sorted(early):
            early[owner | 1 << at] = partner(early[owner], *spin)
    for chunk in late:
        for at, spin in enumerate(spins[1:], 1):
            for owner in sorted(chunk):
                chunk[owner | 1 << at] = partner(chunk[owner], *spin)
    return early, late


def shards(
    initial,
    block_values,
    block_index,
    bond_sites,
    bond_coupling,
    pin_sites,
    pin_partner,
    pinned_spins,
    pin_coupling,
    cross_sites,
    cross_coupling,
):
    state = initial[0, 0]
    columns, states = state.shape
    width = states // CHUNKS
    spins, spin_of_bond = device_spins()
    own_bits = jnp.stack([bit_of(lax.axis_index(axis), position) for axis, position in spins]).astype(jnp.int32)
    rounded = state.astype(BF16)
    early, late = gather(rounded, spins, width)
    dense, product = low_operator(block_values, block_index, rounded)
    high, low = polynomial_rows(
        columns,
        spin_of_bond,
        4,
        bond_sites,
        bond_coupling,
        pin_sites,
        pin_partner,
        pinned_spins,
        pin_coupling,
        cross_sites,
        cross_coupling,
        own_bits,
    )
    held = None
    for at in range(CHUNKS):
        pieces = [
            late[at][owner] if owner & 1 else early[owner] for owner in range(1, 1 << len(spins))
        ]
        held = chunk_terms(at, width, state, product, high, low, pieces, held)
    third, fourth = final_vectors(*held, dense)
    return third[None, None], fourth[None, None]


def solution(mesh):
    vector = P("wide", "narrow", None, None)
    return jax.shard_map(
        shards,
        mesh=mesh,
        in_specs=(vector,) + (P(),) * 10,
        out_specs=(vector, vector),
        check_vma=False,
    )
```

```python
import functools
import math

import jax
import jax.numpy as jnp
from jax import lax
from jax.experimental import pallas as pl
from jax.experimental.pallas import tpu as pltpu
from jax.sharding import PartitionSpec as P

TILE = 256
FINAL_TILE = 512
F32 = jnp.float32
BF16 = jnp.bfloat16


def partner(block, axis, position):
    count = lax.axis_size(axis)
    return lax.ppermute(block, axis, [(at, at ^ (1 << position)) for at in range(count)])


def split(value):
    high = value.astype(BF16)
    return high, (value - high.astype(F32)).astype(BF16)


def cost(microseconds):
    return pl.CostEstimate(flops=microseconds * 10**9, bytes_accessed=0, transcendentals=0)


def dot(left, right):
    return jnp.dot(left, right, preferred_element_type=F32)


def prepare_kernel(widths, state_ref, turned_ref, whole_ref, *part_refs):
    turned = state_ref[...].T
    turned_ref[...] = turned
    rounded = turned.astype(BF16)
    whole_ref[...] = rounded
    start = 0
    for width, part_ref in zip(widths, part_refs):
        part_ref[...] = rounded[start : start + width]
        start += width


def prepare(state, widths):
    columns, states = state.shape
    whole = pl.BlockSpec(memory_space=pltpu.VMEM)
    return pl.pallas_call(
        functools.partial(prepare_kernel, widths),
        in_specs=[whole],
        out_specs=[whole] * (2 + len(widths)),
        out_shape=[jax.ShapeDtypeStruct((states, columns), F32)]
        + [jax.ShapeDtypeStruct((rows, columns), BF16) for rows in (states, *widths)],
        compiler_params=pltpu.CompilerParams(vmem_limit_bytes=16 * 2**20),
        cost_estimate=cost(3),
        name="prepare",
    )(state)


def low_kernel(index_ref, values_ref, state_ref, dense_ref, product_ref, token_ref):
    token_ref[...] = jnp.zeros(token_ref.shape, token_ref.dtype)
    tile = pl.program_id(0)
    rows, kept, size, _ = values_ref.shape
    dense_ref[...] = jnp.zeros(dense_ref.shape, BF16)
    for row in range(rows):
        for slot in range(kept):
            start = pl.multiple_of(index_ref[tile * rows + row, slot] * size, size)
            dense_ref[0, row * size : (row + 1) * size, pl.ds(start, size)] = values_ref[row, slot].T
    product_ref[...] = dot(dense_ref[0], state_ref[...])


def low_operator(block_values, block_index, rounded):
    brows, kept, size, _ = block_values.shape
    width = brows * size
    rows = TILE // size
    columns = rounded.shape[1]
    return pl.pallas_call(
        low_kernel,
        grid=(brows // rows,),
        in_specs=[
            pl.BlockSpec(memory_space=pltpu.SMEM),
            pl.BlockSpec((rows, kept, size, size), lambda t: (t, 0, 0, 0)),
            pl.BlockSpec((width, columns), lambda t: (0, 0)),
        ],
        out_specs=[
            pl.BlockSpec((1, TILE, width), lambda t: (t, 0, 0)),
            pl.BlockSpec((TILE, columns), lambda t: (t, 0)),
            pl.BlockSpec((8, columns), lambda t: (0, 0)),
        ],
        out_shape=[
            jax.ShapeDtypeStruct((width // TILE, TILE, width), BF16),
            jax.ShapeDtypeStruct((width, columns), F32),
            jax.ShapeDtypeStruct((8, columns), jnp.int32),
        ],
        compiler_params=pltpu.CompilerParams(vmem_limit_bytes=24 * 2**20),
        cost_estimate=cost(3),
        name="low_operator",
    )(block_index, block_values, rounded)


def bit_of(values, position):
    return jnp.bitwise_and(jnp.right_shift(values, position), 1)


def polynomial_kernel(
    spin_of_bond,
    sites_ref,
    coupling_ref,
    pin_sites_ref,
    pin_partner_ref,
    pinned_ref,
    pin_coupling_ref,
    cross_sites_ref,
    cross_coupling_ref,
    own_ref,
    high_ref,
    low_ref,
    token_ref,
    op_high,
    op_low,
    poly_ref,
):
    token_ref[...] = jnp.zeros(token_ref.shape, token_ref.dtype)
    whole, size = poly_ref.shape[1:]
    blocks = whole // size
    row = lax.broadcasted_iota(jnp.int32, (size, size), 0)
    col = lax.broadcasted_iota(jnp.int32, (size, size), 1)
    same = row == col
    zero = jnp.zeros((size, size), F32)
    matrix = zero
    field = zero
    for bond in range(sites_ref.shape[0]):
        one, two = sites_ref[bond, 0], sites_ref[bond, 1]
        strength = coupling_ref[bond]
        differ = jnp.bitwise_xor(bit_of(row, one), bit_of(row, two)).astype(F32)
        flips = jnp.bitwise_xor(
            jnp.left_shift(jnp.int32(1), one), jnp.left_shift(jnp.int32(1), two)
        )
        matrix += jnp.where(col == jnp.bitwise_xor(row, flips), strength * 0.5 * differ, 0.0)
        field += strength * (1.0 - 2.0 * differ) * 0.25
    for pin in range(pin_sites_ref.shape[0]):
        pinned = pinned_ref[pin_partner_ref[pin]]
        aligned = jnp.bitwise_xor(bit_of(row, pin_sites_ref[pin]), pinned).astype(F32)
        field += pin_coupling_ref[pin] * (1.0 - 2.0 * aligned) * 0.25
    spins = max(spin_of_bond) + 1
    fields = [[zero, zero] for _ in range(spins)]
    hops = [[zero, zero] for _ in range(spins)]
    for bond, spin in enumerate(spin_of_bond):
        site = cross_sites_ref[bond]
        strength = cross_coupling_ref[bond]
        target = jnp.bitwise_xor(row, jnp.left_shift(jnp.int32(1), site))
        for turned in range(2):
            own = jnp.bitwise_xor(own_ref[spin], turned)
            parity = jnp.bitwise_xor(bit_of(row, site), own).astype(F32)
            fields[spin][turned] += strength * (1.0 - 2.0 * parity) * 0.25
            hops[spin][turned] += jnp.where(col == target, strength * 0.5 * parity, 0.0)
    hop_parts = [[split(hops[spin][turned]) for turned in range(2)] for spin in range(spins)]
    op_high[...] = jnp.zeros(op_high.shape, BF16)
    op_low[...] = jnp.zeros(op_low.shape, BF16)
    poly_ref[0] = jnp.zeros((whole, size), F32)
    poly_ref[1] = jnp.zeros((whole, size), F32)
    poly_ref[0, :size, :] = jnp.where(same, 1.0, 0.0)
    for block in range(blocks):
        at = slice(block * size, (block + 1) * size)
        own_field = field
        for spin in range(spins):
            turned = block >> spin & 1
            own_field = own_field + fields[spin][turned]
            other = block ^ 1 << spin
            high, low = hop_parts[spin][turned]
            op_high[at, other * size : (other + 1) * size] = high
            op_low[at, other * size : (other + 1) * size] = low
            if other == 0:
                poly_ref[1, at, :] = hops[spin][turned]
        diagonal = matrix + jnp.where(same, own_field, 0.0)
        high, low = split(diagonal)
        op_high[at, at] = high
        op_low[at, at] = low
        if block == 0:
            poly_ref[1, at, :] = diagonal
    orders = high_ref.shape[1] // size
    tile = min(2 * TILE, whole)
    for order in range(1, orders + 1):
        high, low = split(poly_ref[order])
        high_ref[:, (order - 1) * size : order * size] = high
        low_ref[:, (order - 1) * size : order * size] = low
        if order == orders:
            break
        both = jnp.concatenate([high, low], axis=1)
        for start in range(0, whole, tile):
            at = slice(start, start + tile)
            product = dot(op_high[at, :], both)
            product = product[:, :size] + product[:, size:] + dot(op_low[at, :], high)
            poly_ref[order + 1, at, :] = 2.0 * product - poly_ref[order - 1, at, :]


def polynomial_columns(
    columns, spin_of_bond, orders, sites, coupling, pin_sites, pin_partner, pinned, pin_coupling, cross_sites, cross_coupling, own_bits
):
    whole = columns << (max(spin_of_bond) + 1)
    operands = (sites, coupling, pin_sites, pin_partner, pinned, pin_coupling, cross_sites, cross_coupling, own_bits)
    out = jax.ShapeDtypeStruct((whole, orders * columns), BF16)
    return pl.pallas_call(
        functools.partial(polynomial_kernel, spin_of_bond),
        in_specs=[pl.BlockSpec(memory_space=pltpu.SMEM)] * len(operands),
        out_specs=[pl.BlockSpec(memory_space=pltpu.VMEM)] * 3,
        out_shape=[out, out, jax.ShapeDtypeStruct((16, columns), BF16)],
        scratch_shapes=[
            pltpu.VMEM((whole, whole), BF16),
            pltpu.VMEM((whole, whole), BF16),
            pltpu.VMEM((orders + 1, whole, columns), F32),
        ],
        compiler_params=pltpu.CompilerParams(vmem_limit_bytes=40 * 2**20),
        cost_estimate=cost(3),
        name="polynomial_columns",
    )(*operands)


def chunk_kernel(places, arrays, *refs):
    state_ref, product_ref, high_ref, low_ref = refs[:4]
    piece_refs = refs[4 : 4 + arrays]
    start_ref, terms_ref, token_ref = refs[-3:]
    token_ref[...] = jnp.zeros(token_ref.shape, token_ref.dtype)
    size = state_ref.shape[1]
    state = state_ref[...]
    own, rest = split(state)
    pieces = [own]
    for owner in sorted(places):
        number, place = places[owner]
        pieces.append(piece_refs[number][:, place * size : (place + 1) * size])
    gathered = jnp.concatenate(pieces, axis=1)
    powers = dot(gathered, high_ref[...]) + dot(gathered, low_ref[...]) + dot(rest, high_ref[:size, :])
    one, two, three, four = (powers[:, k * size : (k + 1) * size] for k in range(4))
    product = product_ref[...]
    start_ref[:, :size] = (8.0 * product + 32.0 * one).astype(BF16)
    start_ref[:, size:] = (4.0 * product + 12.0 * one).astype(BF16)
    terms_ref[:, :size] = 24.0 * two + 16.0 * state
    terms_ref[:, size : 2 * size] = 6.0 * two + 3.0 * state
    terms_ref[:, 2 * size : 3 * size] = 8.0 * (three + one)
    terms_ref[:, 3 * size : 4 * size] = three
    terms_ref[:, 4 * size :] = four


def chunk_terms(start, width, state, product, high, low, arrays, places, ahead, held):
    states, columns = state.shape
    step = math.gcd(start, width)
    at, steps = start // step, width // step
    block = pl.BlockSpec((step, columns), lambda t: (at + t, 0))
    full = pl.BlockSpec(memory_space=pltpu.VMEM)
    operands = [state, product, high, low, *arrays, ahead]
    pieces = [pl.BlockSpec((step, array.shape[1]), lambda t: (t, 0)) for array in arrays]
    specs = [block, block, full, full, *pieces, pl.BlockSpec(memory_space=pl.ANY)]
    aliases = {}
    if held is not None:
        aliases = {len(operands): 0, len(operands) + 1: 1}
        operands += held
        specs += [pl.BlockSpec(memory_space=pl.ANY)] * 2
    return pl.pallas_call(
        functools.partial(chunk_kernel, places, len(arrays)),
        grid=(steps,),
        in_specs=specs,
        out_specs=[
            pl.BlockSpec((step, 2 * columns), lambda t: (at + t, 0)),
            pl.BlockSpec((step, 5 * columns), lambda t: (at + t, 0)),
            full,
        ],
        out_shape=[
            jax.ShapeDtypeStruct((states, 2 * columns), BF16),
            jax.ShapeDtypeStruct((states, 5 * columns), F32),
            jax.ShapeDtypeStruct((16, columns), BF16),
        ],
        input_output_aliases=aliases,
        compiler_params=pltpu.CompilerParams(vmem_limit_bytes=24 * 2**20),
        cost_estimate=cost(3),
        name="chunk_terms",
    )(*operands)


def final_kernel(start_hbm, terms_hbm, dense_hbm, third_ref, fourth_ref, left, second, last, dense, terms, sems):
    tiles, tile, states = dense.shape
    size = third_ref.shape[0]

    def dense_copy(t):
        return pltpu.make_async_copy(dense_hbm.at[t], dense.at[t], sems.at[t])

    def terms_copy():
        return pltpu.make_async_copy(terms_hbm, terms, sems.at[tiles])

    start_copy = pltpu.make_async_copy(start_hbm, left, sems.at[tiles + 1])
    start_copy.start()
    dense_copy(0).start()
    terms_copy().start()
    for t in range(1, tiles):
        dense_copy(t).start()
    start_copy.wait()
    terms_copy().wait()

    def rows(t):
        return pl.ds(pl.multiple_of(t * tile, tile), tile)

    @pl.loop(0, tiles)
    def _(t):
        dense_copy(t).wait()
        at = rows(t)
        second[at, :] = (dot(dense[t], left[...]) + terms[at, : 2 * size]).astype(BF16)

    @pl.loop(0, tiles)
    def _(t):
        at = rows(t)
        product = dot(dense[t], second[...])
        high, low = split(product[:, :size] + terms[at, 2 * size : 3 * size])
        last[at, :size] = high
        last[at, size:] = low
        third_ref[:, at] = (product[:, size:] + terms[at, 3 * size : 4 * size]).T

    @pl.loop(0, tiles)
    def _(t):
        at = rows(t)
        product = dot(dense[t], last[...])
        fourth_ref[:, at] = (product[:, :size] + product[:, size:] + terms[at, 4 * size :]).T


def final_vectors(start, terms, dense):
    states, two = start.shape
    columns = two // 2
    tiles = states // FINAL_TILE
    dense = dense.reshape(tiles, FINAL_TILE, states)
    out = jax.ShapeDtypeStruct((columns, states), F32)
    return pl.pallas_call(
        final_kernel,
        in_specs=[pl.BlockSpec(memory_space=pl.ANY)] * 3,
        out_specs=[pl.BlockSpec(memory_space=pltpu.VMEM)] * 2,
        out_shape=[out, out],
        scratch_shapes=[
            pltpu.VMEM(start.shape, BF16),
            pltpu.VMEM(start.shape, BF16),
            pltpu.VMEM(start.shape, BF16),
            pltpu.VMEM(dense.shape, BF16),
            pltpu.VMEM(terms.shape, F32),
            pltpu.SemaphoreType.DMA((tiles + 2,)),
        ],
        compiler_params=pltpu.CompilerParams(vmem_limit_bytes=32 * 2**20),
        cost_estimate=cost(3),
        name="final_vectors",
    )(start, terms, dense)


def device_spins():
    wide_log = lax.axis_size("wide").bit_length() - 1
    narrow_log = lax.axis_size("narrow").bit_length() - 1
    of_bond = [("wide", wide_log - 1), ("wide", 0), ("narrow", narrow_log - 1), ("narrow", 0)]
    spins = []
    for bond in (0, 2, 3, 1):
        if of_bond[bond] not in spins:
            spins.append(of_bond[bond])
    return spins, [spins.index(spin) for spin in of_bond]


def after(value, token):
    return value + token[0, : value.shape[-1]]


def gathered(early, first, middle, last):
    late = {1: first}
    for at, spin in enumerate(middle, 1):
        for owner in sorted(late):
            late[owner | 1 << at] = partner(late[owner], *spin)
    arrays = [late[owner] for owner in late] + [early[owner] for owner in early if owner]
    owners = [owner for owner in late] + [owner for owner in early if owner]
    places = {owner: (number, 0) for number, owner in enumerate(owners)}
    for group in ([*early, 1], [owner for owner in late if owner != 1]):
        if group:
            sent = jnp.concatenate([{**early, **late}[owner] for owner in group], axis=1)
            for place, owner in enumerate(group):
                places[owner | 1 << len(middle) + 1] = (len(arrays), place)
            arrays.append(partner(sent, *last))
    return arrays, places


def shards(initial, block_values, block_index, *column_operands):
    state = initial[0, 0]
    columns, states = state.shape
    eighth = states // 8
    splits = [[3 * eighth, 2 * eighth], [2 * eighth, eighth]]
    spins, spin_of_bond = device_spins()
    own_bits = jnp.stack([bit_of(lax.axis_index(axis), position) for axis, position in spins]).astype(jnp.int32)
    turned, rounded, *parts = prepare(state, [sum(widths) for widths in splits])
    firsts = [partner(part, *spins[0]) for part in parts]
    early = {0: rounded}
    for at, spin in enumerate(spins[1:-1], 1):
        for owner in sorted(early):
            early[owner | 1 << at] = partner(early[owner], *spin)
    dense, product, token = low_operator(block_values, block_index, rounded)
    high, low, token = polynomial_columns(columns, spin_of_bond, 4, *column_operands, after(own_bits, token))
    held = None
    start = 0
    first = after(firsts[0], token)
    for part, widths in enumerate(splits):
        pieces = []
        for chunk, width in enumerate(widths):
            inside = sum(widths[:chunk])
            own_parts = {owner: piece[start + inside : start + inside + width] for owner, piece in early.items()}
            pieces.append(gathered(own_parts, first[inside : inside + width], spins[1:-1], spins[-1]))
        for chunk, width in enumerate(widths):
            if chunk == len(widths) - 1 and part + 1 < len(splits):
                first = after(firsts[part + 1], token)
            *held, token = chunk_terms(start, width, turned, product, high, low, *pieces[chunk], first, held)
            start += width
    third, fourth = final_vectors(*held, dense)
    return third[None, None], fourth[None, None]


def solution(mesh):
    vector = P("wide", "narrow", None, None)
    return jax.shard_map(
        shards,
        mesh=mesh,
        in_specs=(vector,) + (P(),) * 10,
        out_specs=(vector, vector),
        check_vma=False,
    )
```

```python
import functools

import jax
import jax.numpy as jnp
from jax import lax
from jax.experimental import pallas as pl
from jax.experimental.pallas import tpu as pltpu
from jax.sharding import PartitionSpec as P

TILE = 256
FINAL_TILE = 512
F32 = jnp.float32
BF16 = jnp.bfloat16


def partner(block, axis, position):
    count = lax.axis_size(axis)
    return lax.ppermute(block, axis, [(at, at ^ (1 << position)) for at in range(count)])


def split(value):
    high = value.astype(BF16)
    return high, (value - high.astype(F32)).astype(BF16)


def cost(microseconds):
    return pl.CostEstimate(flops=microseconds * 10**9, bytes_accessed=0, transcendentals=0)


def dot(left, right):
    return jnp.dot(left, right, preferred_element_type=F32)


def prepare_kernel(state_ref, turned_ref, whole_ref, first_ref):
    turned = state_ref[...].T
    turned_ref[...] = turned
    rounded = turned.astype(BF16)
    whole_ref[...] = rounded
    first_ref[...] = rounded[: first_ref.shape[0]]


def prepare(state, first):
    columns, states = state.shape
    full = pl.BlockSpec(memory_space=pltpu.VMEM)
    return pl.pallas_call(
        prepare_kernel,
        in_specs=[full],
        out_specs=[full] * 3,
        out_shape=[
            jax.ShapeDtypeStruct((states, columns), F32),
            jax.ShapeDtypeStruct((states, columns), BF16),
            jax.ShapeDtypeStruct((first, columns), BF16),
        ],
        compiler_params=pltpu.CompilerParams(vmem_limit_bytes=16 * 2**20),
        cost_estimate=cost(2),
        name="prepare",
    )(state)


def low_kernel(index_ref, values_ref, state_ref, dense_ref, product_ref, token_ref):
    token_ref[...] = jnp.zeros(token_ref.shape, token_ref.dtype)
    tile = pl.program_id(0)
    rows, kept, size, _ = values_ref.shape
    dense_ref[...] = jnp.zeros(dense_ref.shape, BF16)
    for row in range(rows):
        for slot in range(kept):
            start = pl.multiple_of(index_ref[tile * rows + row, slot] * size, size)
            dense_ref[0, row * size : (row + 1) * size, pl.ds(start, size)] = values_ref[row, slot].T
    product_ref[...] = dot(dense_ref[0], state_ref[...])


def low_operator(block_values, block_index, rounded):
    brows, kept, size, _ = block_values.shape
    width = brows * size
    rows = TILE // size
    columns = rounded.shape[1]
    return pl.pallas_call(
        low_kernel,
        grid=(brows // rows,),
        in_specs=[
            pl.BlockSpec(memory_space=pltpu.SMEM),
            pl.BlockSpec((rows, kept, size, size), lambda t: (t, 0, 0, 0)),
            pl.BlockSpec((width, columns), lambda t: (0, 0)),
        ],
        out_specs=[
            pl.BlockSpec((1, TILE, width), lambda t: (t, 0, 0)),
            pl.BlockSpec((TILE, columns), lambda t: (t, 0)),
            pl.BlockSpec((8, columns), lambda t: (0, 0)),
        ],
        out_shape=[
            jax.ShapeDtypeStruct((width // TILE, TILE, width), BF16),
            jax.ShapeDtypeStruct((width, columns), F32),
            jax.ShapeDtypeStruct((8, columns), jnp.int32),
        ],
        compiler_params=pltpu.CompilerParams(vmem_limit_bytes=24 * 2**20),
        cost_estimate=cost(2),
        name="low_operator",
    )(block_index, block_values, rounded)


def bit_of(values, position):
    return jnp.bitwise_and(jnp.right_shift(values, position), 1)


def polynomial_kernel(
    spin_of_bond,
    sites_ref,
    coupling_ref,
    pin_sites_ref,
    pin_partner_ref,
    pinned_ref,
    pin_coupling_ref,
    cross_sites_ref,
    cross_coupling_ref,
    own_ref,
    high_ref,
    low_ref,
    token_ref,
    op_high,
    op_low,
    poly_ref,
):
    token_ref[...] = jnp.zeros(token_ref.shape, token_ref.dtype)
    whole, size = poly_ref.shape[1:]
    blocks = whole // size
    row = lax.broadcasted_iota(jnp.int32, (size, size), 0)
    col = lax.broadcasted_iota(jnp.int32, (size, size), 1)
    same = row == col
    zero = jnp.zeros((size, size), F32)
    matrix = zero
    field = zero
    for bond in range(sites_ref.shape[0]):
        one, two = sites_ref[bond, 0], sites_ref[bond, 1]
        strength = coupling_ref[bond]
        differ = jnp.bitwise_xor(bit_of(row, one), bit_of(row, two)).astype(F32)
        flips = jnp.bitwise_xor(
            jnp.left_shift(jnp.int32(1), one), jnp.left_shift(jnp.int32(1), two)
        )
        matrix += jnp.where(col == jnp.bitwise_xor(row, flips), strength * 0.5 * differ, 0.0)
        field += strength * (1.0 - 2.0 * differ) * 0.25
    for pin in range(pin_sites_ref.shape[0]):
        pinned = pinned_ref[pin_partner_ref[pin]]
        aligned = jnp.bitwise_xor(bit_of(row, pin_sites_ref[pin]), pinned).astype(F32)
        field += pin_coupling_ref[pin] * (1.0 - 2.0 * aligned) * 0.25
    spins = max(spin_of_bond) + 1
    fields = [[zero, zero] for _ in range(spins)]
    hops = [[zero, zero] for _ in range(spins)]
    for bond, spin in enumerate(spin_of_bond):
        site = cross_sites_ref[bond]
        strength = cross_coupling_ref[bond]
        target = jnp.bitwise_xor(row, jnp.left_shift(jnp.int32(1), site))
        for turned in range(2):
            own = jnp.bitwise_xor(own_ref[spin], turned)
            parity = jnp.bitwise_xor(bit_of(row, site), own).astype(F32)
            fields[spin][turned] += strength * (1.0 - 2.0 * parity) * 0.25
            hops[spin][turned] += jnp.where(col == target, strength * 0.5 * parity, 0.0)
    hop_parts = [[split(hops[spin][turned]) for turned in range(2)] for spin in range(spins)]
    op_high[...] = jnp.zeros(op_high.shape, BF16)
    op_low[...] = jnp.zeros(op_low.shape, BF16)
    poly_ref[0] = jnp.zeros((whole, size), F32)
    poly_ref[1] = jnp.zeros((whole, size), F32)
    poly_ref[0, :size, :] = jnp.where(same, 1.0, 0.0)
    for block in range(blocks):
        at = slice(block * size, (block + 1) * size)
        own_field = field
        for spin in range(spins):
            turned = block >> spin & 1
            own_field = own_field + fields[spin][turned]
            other = block ^ 1 << spin
            high, low = hop_parts[spin][turned]
            op_high[at, other * size : (other + 1) * size] = high
            op_low[at, other * size : (other + 1) * size] = low
            if other == 0:
                poly_ref[1, at, :] = hops[spin][turned]
        diagonal = matrix + jnp.where(same, own_field, 0.0)
        high, low = split(diagonal)
        op_high[at, at] = high
        op_low[at, at] = low
        if block == 0:
            poly_ref[1, at, :] = diagonal
    orders = high_ref.shape[1] // size
    tile = min(2 * TILE, whole)
    for order in range(1, orders + 1):
        high, low = split(poly_ref[order])
        high_ref[:, (order - 1) * size : order * size] = high
        low_ref[:, (order - 1) * size : order * size] = low
        if order == orders:
            break
        both = jnp.concatenate([high, low], axis=1)
        for start in range(0, whole, tile):
            at = slice(start, start + tile)
            product = dot(op_high[at, :], both)
            product = product[:, :size] + product[:, size:] + dot(op_low[at, :], high)
            poly_ref[order + 1, at, :] = 2.0 * product - poly_ref[order - 1, at, :]


def polynomial_columns(
    columns, spin_of_bond, orders, sites, coupling, pin_sites, pin_partner, pinned, pin_coupling, cross_sites, cross_coupling, own_bits
):
    whole = columns << (max(spin_of_bond) + 1)
    operands = (sites, coupling, pin_sites, pin_partner, pinned, pin_coupling, cross_sites, cross_coupling, own_bits)
    out = jax.ShapeDtypeStruct((whole, orders * columns), BF16)
    return pl.pallas_call(
        functools.partial(polynomial_kernel, spin_of_bond),
        in_specs=[pl.BlockSpec(memory_space=pltpu.SMEM)] * len(operands),
        out_specs=[pl.BlockSpec(memory_space=pltpu.VMEM)] * 3,
        out_shape=[out, out, jax.ShapeDtypeStruct((16, columns), BF16)],
        scratch_shapes=[
            pltpu.VMEM((whole, whole), BF16),
            pltpu.VMEM((whole, whole), BF16),
            pltpu.VMEM((orders + 1, whole, columns), F32),
        ],
        compiler_params=pltpu.CompilerParams(vmem_limit_bytes=4 * whole * whole + 48 * whole * columns + 6 * 2**20),
        cost_estimate=cost(2),
        name="polynomial_columns",
    )(*operands)


def chunk_kernel(start, places, arrays, *refs):
    state_ref, product_ref, high_ref, low_ref = refs[:4]
    piece_refs = refs[4 : 4 + arrays]
    start_ref, terms_ref, token_ref = refs[-3:]
    token_ref[...] = jnp.zeros(token_ref.shape, token_ref.dtype)
    width = start_ref.shape[0]
    size = state_ref.shape[1]
    state = state_ref[start : start + width, :]
    product = product_ref[start : start + width, :]
    own, rest = split(state)
    pieces = [own]
    for owner in sorted(places):
        number, place = places[owner]
        pieces.append(piece_refs[number][:, place * size : (place + 1) * size])
    gathered = jnp.concatenate(pieces, axis=1)
    powers = dot(gathered, high_ref[...]) + dot(gathered, low_ref[...]) + dot(rest, high_ref[:size, :])
    one, two, three, four = (powers[:, k * size : (k + 1) * size] for k in range(4))
    start_ref[:, :size] = (8.0 * product + 32.0 * one).astype(BF16)
    start_ref[:, size:] = (4.0 * product + 12.0 * one).astype(BF16)
    terms_ref[:, :size] = 24.0 * two + 16.0 * state
    terms_ref[:, size : 2 * size] = 6.0 * two + 3.0 * state
    terms_ref[:, 2 * size : 3 * size] = 8.0 * (three + one)
    terms_ref[:, 3 * size : 4 * size] = three
    terms_ref[:, 4 * size :] = four


def chunk_terms(start, width, state, product, high, low, arrays, places, ahead):
    columns = state.shape[1]
    full = pl.BlockSpec(memory_space=pltpu.VMEM)
    operands = [state, product, high, low, *arrays]
    return pl.pallas_call(
        functools.partial(chunk_kernel, start, places, len(arrays)),
        in_specs=[full] * len(operands) + [pl.BlockSpec(memory_space=pl.ANY)] * len(ahead),
        out_specs=[full] * 3,
        out_shape=[
            jax.ShapeDtypeStruct((width, 2 * columns), BF16),
            jax.ShapeDtypeStruct((width, 5 * columns), F32),
            jax.ShapeDtypeStruct((16, columns), BF16),
        ],
        compiler_params=pltpu.CompilerParams(vmem_limit_bytes=20 * 2**20),
        cost_estimate=cost(2),
        name="chunk_terms",
    )(*operands, *ahead)


def final_kernel(chunks, *refs):
    start_refs, term_refs = refs[:chunks], refs[chunks : 2 * chunks]
    dense, third_ref, fourth_ref, left, second, last = refs[2 * chunks :]
    size = third_ref.shape[0]
    tiles = []
    row = 0
    for start_ref, terms in zip(start_refs, term_refs):
        for inside in range(0, terms.shape[0], FINAL_TILE):
            width = min(FINAL_TILE, terms.shape[0] - inside)
            left[row : row + width, :] = start_ref[inside : inside + width, :]
            tiles.append((slice(row, row + width), terms, slice(inside, inside + width)))
            row += width
    for at, terms, inside in tiles:
        second[at, :] = (dot(dense[at, :], left[...]) + terms[inside, : 2 * size]).astype(BF16)
    for at, terms, inside in tiles:
        product = dot(dense[at, :], second[...])
        high, low = split(product[:, :size] + terms[inside, 2 * size : 3 * size])
        last[at, :size] = high
        last[at, size:] = low
        third_ref[:, at] = (product[:, size:] + terms[inside, 3 * size : 4 * size]).T
    for at, terms, inside in tiles:
        product = dot(dense[at, :], last[...])
        fourth_ref[:, at] = (product[:, :size] + product[:, size:] + terms[inside, 4 * size :]).T


def final_vectors(starts, terms, dense):
    states = dense.shape[2]
    columns = starts[0].shape[1] // 2
    full = pl.BlockSpec(memory_space=pltpu.VMEM)
    operands = [*starts, *terms, dense.reshape(states, states)]
    return pl.pallas_call(
        functools.partial(final_kernel, len(starts)),
        in_specs=[full] * len(operands),
        out_specs=[full] * 2,
        out_shape=[jax.ShapeDtypeStruct((columns, states), F32)] * 2,
        scratch_shapes=[pltpu.VMEM((states, 2 * columns), BF16)] * 3,
        compiler_params=pltpu.CompilerParams(vmem_limit_bytes=28 * 2**20),
        cost_estimate=cost(2),
        name="final_vectors",
    )(*operands)


def device_spins():
    wide_log = lax.axis_size("wide").bit_length() - 1
    narrow_log = lax.axis_size("narrow").bit_length() - 1
    of_bond = [("wide", wide_log - 1), ("wide", 0), ("narrow", narrow_log - 1), ("narrow", 0)]
    spins = []
    for bond in (0, 2, 3, 1):
        if of_bond[bond] not in spins:
            spins.append(of_bond[bond])
    return spins, [spins.index(spin) for spin in of_bond]


def after(value, token):
    return value + token[0, : value.shape[-1]].astype(value.dtype)


def gathered(early, first, middle, last):
    late = {1: first}
    for at, spin in enumerate(middle, 1):
        for owner in sorted(late):
            late[owner | 1 << at] = partner(late[owner], *spin)
    arrays = [late[owner] for owner in late] + [early[owner] for owner in early if owner]
    owners = [owner for owner in late] + [owner for owner in early if owner]
    places = {owner: (number, 0) for number, owner in enumerate(owners)}
    for group in ([*early, 1], [owner for owner in late if owner != 1]):
        if group:
            sent = jnp.concatenate([{**early, **late}[owner] for owner in group], axis=1)
            for place, owner in enumerate(group):
                places[owner | 1 << len(middle) + 1] = (len(arrays), place)
            arrays.append(partner(sent, *last))
    return arrays, places


def shards(initial, block_values, block_index, *column_operands):
    state = initial[0, 0]
    columns, states = state.shape
    part = states // 16
    splits = [[6 * part, 4 * part], [3 * part, 3 * part]]
    spins, spin_of_bond = device_spins()
    own_bits = jnp.stack([bit_of(lax.axis_index(axis), position) for axis, position in spins]).astype(jnp.int32)
    turned, rounded, first = prepare(state, sum(splits[0]))
    firsts = [partner(first, *spins[0])]
    early = {0: rounded}
    for at, spin in enumerate(spins[1:-1], 1):
        for owner in sorted(early):
            early[owner | 1 << at] = partner(early[owner], *spin)
    dense, product, token = low_operator(block_values, block_index, rounded)
    start = sum(splits[0])
    firsts.append(partner(after(rounded[start : start + sum(splits[1])], token), *spins[0]))
    high, low, token = polynomial_columns(columns, spin_of_bond, 4, *column_operands, after(own_bits, token))
    starts, terms = [], []
    start = 0
    first = after(firsts[0], token)
    for number, widths in enumerate(splits):
        pieces = []
        for chunk, width in enumerate(widths):
            inside = sum(widths[:chunk])
            own_parts = {owner: piece[start + inside : start + inside + width] for owner, piece in early.items()}
            pieces.append(gathered(own_parts, first[inside : inside + width], spins[1:-1], spins[-1]))
        for chunk, width in enumerate(widths):
            ahead = []
            if chunk == len(widths) - 1 and number + 1 < len(splits):
                first = after(firsts[number + 1], token)
                ahead = [first]
            *given, token = chunk_terms(start, width, turned, product, high, low, *pieces[chunk], ahead)
            starts.append(given[0])
            terms.append(given[1])
            start += width
    third, fourth = final_vectors(starts, terms, dense)
    return third[None, None], fourth[None, None]


def solution(mesh):
    vector = P("wide", "narrow", None, None)
    return jax.shard_map(
        shards,
        mesh=mesh,
        in_specs=(vector,) + (P(),) * 10,
        out_specs=(vector, vector),
        check_vma=False,
    )
```

```python
import functools

import jax
import jax.numpy as jnp
from jax import lax
from jax.experimental import pallas as pl
from jax.experimental.pallas import tpu as pltpu
from jax.sharding import PartitionSpec as P

TILE = 256
ROWS = 512
F32 = jnp.float32
BF16 = jnp.bfloat16


def partner(block, axis, position):
    count = lax.axis_size(axis)
    return lax.ppermute(block, axis, [(at, at ^ (1 << position)) for at in range(count)])


def split(value):
    high = value.astype(BF16)
    return high, (value - high.astype(F32)).astype(BF16)


def dot(left, right):
    return jnp.dot(left, right, preferred_element_type=F32)


def prepare_kernel(state_ref, turned_ref, whole_ref, first_ref):
    turned = state_ref[...].T
    turned_ref[...] = turned
    rounded = turned.astype(BF16)
    whole_ref[...] = rounded
    first_ref[...] = rounded[: first_ref.shape[0]]


def prepare(state, first):
    columns, states = state.shape
    full = pl.BlockSpec(memory_space=pltpu.VMEM)
    return pl.pallas_call(
        prepare_kernel,
        in_specs=[full],
        out_specs=[full] * 3,
        out_shape=[
            jax.ShapeDtypeStruct((states, columns), F32),
            jax.ShapeDtypeStruct((states, columns), BF16),
            jax.ShapeDtypeStruct((first, columns), BF16),
        ],
        compiler_params=pltpu.CompilerParams(vmem_limit_bytes=16 * 2**20),
        name="prepare",
    )(state)


def low_kernel(index_ref, values_hbm, state_ref, dense_ref, product_ref, token_ref, values, sems):
    tile = pl.program_id(0)
    slots, rows, kept, size, _ = values.shape
    token_ref[...] = jnp.zeros(token_ref.shape, token_ref.dtype)

    def copy(t):
        slot = lax.rem(t, slots)
        return pltpu.make_async_copy(values_hbm.at[pl.ds(t * rows, rows)], values.at[slot], sems.at[slot])

    @pl.when(tile == 0)
    def _():
        copy(tile).start()

    @pl.when(tile + 1 < pl.num_programs(0))
    def _():
        copy(tile + 1).start()

    copy(tile).wait()
    slot = lax.rem(tile, slots)
    dense_ref[...] = jnp.zeros(dense_ref.shape, BF16)
    for row in range(rows):
        for at in range(kept):
            start = pl.multiple_of(index_ref[tile * rows + row, at] * size, size)
            dense_ref[row * size : (row + 1) * size, pl.ds(start, size)] = values[slot, row, at].T
    product_ref[...] = dot(dense_ref[...], state_ref[...])


def low_operator(block_values, block_index, rounded):
    brows, kept, size, _ = block_values.shape
    width = brows * size
    rows = TILE // size
    columns = rounded.shape[1]
    return pl.pallas_call(
        low_kernel,
        grid=(brows // rows,),
        in_specs=[
            pl.BlockSpec(memory_space=pltpu.SMEM),
            pl.BlockSpec(memory_space=pltpu.HBM),
            pl.BlockSpec(memory_space=pltpu.VMEM),
        ],
        out_specs=[
            pl.BlockSpec((TILE, width), lambda t: (t, 0)),
            pl.BlockSpec((TILE, columns), lambda t: (t, 0)),
            pl.BlockSpec((8, columns), lambda t: (0, 0)),
        ],
        out_shape=[
            jax.ShapeDtypeStruct((width, width), BF16),
            jax.ShapeDtypeStruct((width, columns), F32),
            jax.ShapeDtypeStruct((8, columns), jnp.int32),
        ],
        scratch_shapes=[
            pltpu.VMEM((2, rows, kept, size, size), BF16),
            pltpu.SemaphoreType.DMA((2,)),
        ],
        compiler_params=pltpu.CompilerParams(vmem_limit_bytes=16 * 2**20),
        name="low_operator",
    )(block_index, pltpu.with_memory_space_constraint(block_values, pltpu.HBM), rounded)


def bit_of(values, position):
    return jnp.bitwise_and(jnp.right_shift(values, position), 1)


def polynomial_kernel(
    spin_of_bond,
    sites_ref,
    coupling_ref,
    pin_sites_ref,
    pin_partner_ref,
    pinned_ref,
    pin_coupling_ref,
    cross_sites_ref,
    cross_coupling_ref,
    own_ref,
    high_ref,
    low_ref,
    token_ref,
    op_high,
    op_low,
    poly_ref,
):
    token_ref[...] = jnp.zeros(token_ref.shape, token_ref.dtype)
    whole, size = poly_ref.shape[1:]
    blocks = whole // size
    row = lax.broadcasted_iota(jnp.int32, (size, size), 0)
    col = lax.broadcasted_iota(jnp.int32, (size, size), 1)
    same = row == col
    zero = jnp.zeros((size, size), F32)
    matrix = zero
    field = zero
    for bond in range(sites_ref.shape[0]):
        one, two = sites_ref[bond, 0], sites_ref[bond, 1]
        strength = coupling_ref[bond]
        differ = jnp.bitwise_xor(bit_of(row, one), bit_of(row, two)).astype(F32)
        flips = jnp.bitwise_xor(
            jnp.left_shift(jnp.int32(1), one), jnp.left_shift(jnp.int32(1), two)
        )
        matrix += jnp.where(col == jnp.bitwise_xor(row, flips), strength * 0.5 * differ, 0.0)
        field += strength * (1.0 - 2.0 * differ) * 0.25
    for pin in range(pin_sites_ref.shape[0]):
        pinned = pinned_ref[pin_partner_ref[pin]]
        aligned = jnp.bitwise_xor(bit_of(row, pin_sites_ref[pin]), pinned).astype(F32)
        field += pin_coupling_ref[pin] * (1.0 - 2.0 * aligned) * 0.25
    spins = max(spin_of_bond) + 1
    fields = [[zero, zero] for _ in range(spins)]
    hops = [[zero, zero] for _ in range(spins)]
    for bond, spin in enumerate(spin_of_bond):
        site = cross_sites_ref[bond]
        strength = cross_coupling_ref[bond]
        target = jnp.bitwise_xor(row, jnp.left_shift(jnp.int32(1), site))
        for turned in range(2):
            own = jnp.bitwise_xor(own_ref[spin], turned)
            parity = jnp.bitwise_xor(bit_of(row, site), own).astype(F32)
            fields[spin][turned] += strength * (1.0 - 2.0 * parity) * 0.25
            hops[spin][turned] += jnp.where(col == target, strength * 0.5 * parity, 0.0)
    hop_parts = [[split(hops[spin][turned]) for turned in range(2)] for spin in range(spins)]
    op_high[...] = jnp.zeros(op_high.shape, BF16)
    op_low[...] = jnp.zeros(op_low.shape, BF16)
    poly_ref[0] = jnp.zeros((whole, size), F32)
    poly_ref[1] = jnp.zeros((whole, size), F32)
    poly_ref[0, :size, :] = jnp.where(same, 1.0, 0.0)
    for block in range(blocks):
        at = slice(block * size, (block + 1) * size)
        own_field = field
        for spin in range(spins):
            turned = block >> spin & 1
            own_field = own_field + fields[spin][turned]
            other = block ^ 1 << spin
            high, low = hop_parts[spin][turned]
            op_high[at, other * size : (other + 1) * size] = high
            op_low[at, other * size : (other + 1) * size] = low
            if other == 0:
                poly_ref[1, at, :] = hops[spin][turned]
        diagonal = matrix + jnp.where(same, own_field, 0.0)
        high, low = split(diagonal)
        op_high[at, at] = high
        op_low[at, at] = low
        if block == 0:
            poly_ref[1, at, :] = diagonal
    orders = high_ref.shape[1] // size
    tile = min(2 * TILE, whole)
    for order in range(1, orders + 1):
        high, low = split(poly_ref[order])
        high_ref[:, (order - 1) * size : order * size] = high
        low_ref[:, (order - 1) * size : order * size] = low
        if order == orders:
            break
        both = jnp.concatenate([high, low], axis=1)
        for start in range(0, whole, tile):
            at = slice(start, start + tile)
            product = dot(op_high[at, :], both)
            product = product[:, :size] + product[:, size:] + dot(op_low[at, :], high)
            poly_ref[order + 1, at, :] = 2.0 * product - poly_ref[order - 1, at, :]


def polynomial_columns(
    columns, spin_of_bond, orders, sites, coupling, pin_sites, pin_partner, pinned, pin_coupling, cross_sites, cross_coupling, own_bits
):
    whole = columns << (max(spin_of_bond) + 1)
    operands = (sites, coupling, pin_sites, pin_partner, pinned, pin_coupling, cross_sites, cross_coupling, own_bits)
    out = jax.ShapeDtypeStruct((whole, orders * columns), BF16)
    return pl.pallas_call(
        functools.partial(polynomial_kernel, spin_of_bond),
        in_specs=[pl.BlockSpec(memory_space=pltpu.SMEM)] * len(operands),
        out_specs=[pl.BlockSpec(memory_space=pltpu.VMEM)] * 3,
        out_shape=[out, out, jax.ShapeDtypeStruct((16, columns), BF16)],
        scratch_shapes=[
            pltpu.VMEM((whole, whole), BF16),
            pltpu.VMEM((whole, whole), BF16),
            pltpu.VMEM((orders + 1, whole, columns), F32),
        ],
        compiler_params=pltpu.CompilerParams(vmem_limit_bytes=4 * whole * whole + 48 * whole * columns + 6 * 2**20),
        name="polynomial_columns",
    )(*operands)


def chunk_kernel(start, places, arrays, summed, *refs):
    state_ref, product_ref, high_ref, low_ref, dense_ref = refs[:5]
    piece_refs = refs[5 : 5 + arrays]
    sum_ref, terms_ref = refs[-2:]
    width = terms_ref.shape[0]
    size = state_ref.shape[1]
    state = state_ref[start : start + width, :]
    product = product_ref[start : start + width, :]
    own, rest = split(state)
    pieces = [own]
    for owner in sorted(places):
        number, place = places[owner]
        pieces.append(piece_refs[number][:, place * size : (place + 1) * size])
    gathered = jnp.concatenate(pieces, axis=1)
    powers = dot(gathered, high_ref[...]) + dot(gathered, low_ref[...]) + dot(rest, high_ref[:size, :])
    one, two, three, four = (powers[:, k * size : (k + 1) * size] for k in range(4))
    both = jnp.concatenate([8.0 * product + 32.0 * one, 4.0 * product + 12.0 * one], axis=1).astype(BF16)
    terms_ref[:, :size] = 24.0 * two + 16.0 * state
    terms_ref[:, size : 2 * size] = 6.0 * two + 3.0 * state
    terms_ref[:, 2 * size : 3 * size] = 8.0 * (three + one)
    terms_ref[:, 3 * size : 4 * size] = three
    terms_ref[:, 4 * size :] = four
    for at in range(0, sum_ref.shape[0], ROWS):
        share = dot(dense_ref[at : at + ROWS, start : start + width], both)
        sum_ref[at : at + ROWS, :] = refs[5 + arrays][at : at + ROWS, :] + share if summed else share


def chunk_terms(start, width, state, product, high, low, dense, arrays, places, summed, ahead):
    states, columns = state.shape
    full = pl.BlockSpec(memory_space=pltpu.VMEM)
    operands = [state, product, high, low, dense, *arrays, *summed]
    return pl.pallas_call(
        functools.partial(chunk_kernel, start, places, len(arrays), len(summed)),
        in_specs=[full] * len(operands) + [pl.BlockSpec(memory_space=pl.ANY)] * len(ahead),
        out_specs=[full] * 2,
        out_shape=[
            jax.ShapeDtypeStruct((states, 2 * columns), F32),
            jax.ShapeDtypeStruct((width, 5 * columns), F32),
        ],
        compiler_params=pltpu.CompilerParams(vmem_limit_bytes=28 * 2**20),
        cost_estimate=pl.CostEstimate(flops=4 * 10**9, bytes_accessed=0, transcendentals=0),
        name="chunk_terms",
    )(*operands, *ahead)


def final_kernel(chunks, sum_ref, dense, *refs):
    term_refs = refs[:chunks]
    third_hbm, fourth_hbm, third, fourth, second, last, sems = refs[chunks:]
    size = third.shape[0]
    tiles = []
    row = 0
    for terms in term_refs:
        width = terms.shape[0]
        at = slice(row, row + width)
        second[at, :] = (sum_ref[at, :] + terms[:, : 2 * size]).astype(BF16)
        tiles.append((at, terms))
        row += width
    copies = []

    def give(source, target, at):
        copies.append(pltpu.make_async_copy(source.at[:, at], target.at[:, at], sems.at[len(copies)]))
        copies[-1].start()

    for at, terms in tiles:
        product = dot(dense[at, :], second[...])
        high, low = split(product[:, :size] + terms[:, 2 * size : 3 * size])
        last[at, :size] = high
        last[at, size:] = low
        third[:, at] = (product[:, size:] + terms[:, 3 * size : 4 * size]).T
        give(third, third_hbm, at)
    for at, terms in tiles:
        product = dot(dense[at, :], last[...])
        fourth[:, at] = (product[:, :size] + product[:, size:] + terms[:, 4 * size :]).T
        give(fourth, fourth_hbm, at)
    for copy in copies:
        copy.wait()


def final_vectors(summed, dense, terms):
    states, two = summed.shape
    columns = two // 2
    full = pl.BlockSpec(memory_space=pltpu.VMEM)
    operands = [summed, dense, *terms]
    out = jax.ShapeDtypeStruct((columns, states), F32)
    return pl.pallas_call(
        functools.partial(final_kernel, len(terms)),
        in_specs=[full] * len(operands),
        out_specs=[pl.BlockSpec(memory_space=pltpu.HBM)] * 2,
        out_shape=[out, out],
        scratch_shapes=[
            pltpu.VMEM((columns, states), F32),
            pltpu.VMEM((columns, states), F32),
            pltpu.VMEM((states, two), BF16),
            pltpu.VMEM((states, two), BF16),
            pltpu.SemaphoreType.DMA((2 * len(terms),)),
        ],
        compiler_params=pltpu.CompilerParams(vmem_limit_bytes=28 * 2**20),
        name="final_vectors",
    )(*operands)


def device_spins():
    wide_log = lax.axis_size("wide").bit_length() - 1
    narrow_log = lax.axis_size("narrow").bit_length() - 1
    of_bond = [("wide", wide_log - 1), ("wide", 0), ("narrow", narrow_log - 1), ("narrow", 0)]
    spins = []
    for bond in (0, 2, 3, 1):
        if of_bond[bond] not in spins:
            spins.append(of_bond[bond])
    return spins, [spins.index(spin) for spin in of_bond]


def after(value, token):
    return value + token[0, : value.shape[-1]].astype(value.dtype)


def gathered(early, first, middle, last):
    late = {1: first}
    for at, spin in enumerate(middle, 1):
        for owner in sorted(late):
            late[owner | 1 << at] = partner(late[owner], *spin)
    arrays = [late[owner] for owner in late] + [early[owner] for owner in early if owner]
    owners = [owner for owner in late] + [owner for owner in early if owner]
    places = {owner: (number, 0) for number, owner in enumerate(owners)}
    for group in ([*early, 1], [owner for owner in late if owner != 1]):
        if group:
            sent = jnp.concatenate([{**early, **late}[owner] for owner in group], axis=1)
            for place, owner in enumerate(group):
                places[owner | 1 << len(middle) + 1] = (len(arrays), place)
            arrays.append(partner(sent, *last))
    return arrays, places


def shards(initial, block_values, block_index, *column_operands):
    state = initial[0, 0]
    columns, states = state.shape
    part = states // 16
    splits = [[6 * part, 4 * part], [3 * part, 3 * part]]
    spins, spin_of_bond = device_spins()
    own_bits = jnp.stack([bit_of(lax.axis_index(axis), position) for axis, position in spins]).astype(jnp.int32)
    turned, rounded, first = prepare(state, sum(splits[0]))
    firsts = [partner(first, *spins[0])]
    early = {0: rounded}
    for at, spin in enumerate(spins[1:-1], 1):
        for owner in sorted(early):
            early[owner | 1 << at] = partner(early[owner], *spin)
    dense, product, token = low_operator(block_values, block_index, rounded)
    start = sum(splits[0])
    firsts.append(partner(after(rounded[start : start + sum(splits[1])], token), *spins[0]))
    high, low, token = polynomial_columns(columns, spin_of_bond, 4, *column_operands, after(own_bits, token))
    pieces, afters = [], []
    start = 0
    for first, widths in zip(firsts, splits):
        first = after(first, token)
        for chunk, width in enumerate(widths):
            inside = sum(widths[:chunk])
            own_parts = {owner: piece[start + inside : start + inside + width] for owner, piece in early.items()}
            pieces.append(gathered(own_parts, first[inside : inside + width], spins[1:-1], spins[-1]))
        afters.append(first)
        token = pieces[-len(widths)][0][1][:1] * 0
        start += sum(widths)
    terms, summed = [], []
    start = 0
    for number, widths in enumerate(splits):
        for width in widths:
            total, term = chunk_terms(
                start, width, turned, product, high, low, dense, *pieces[len(terms)], summed, afters[number + 1 : number + 2]
            )
            summed = [total]
            terms.append(term)
            start += width
    third, fourth = final_vectors(total, dense, terms)
    return third[None, None], fourth[None, None]


def solution(mesh):
    vector = P("wide", "narrow", None, None)
    return jax.shard_map(
        shards,
        mesh=mesh,
        in_specs=(vector,) + (P(),) * 10,
        out_specs=(vector, vector),
        check_vma=False,
    )
```

```python
import functools

import jax
import jax.numpy as jnp
from jax import lax
from jax.experimental import pallas as pl
from jax.experimental.pallas import tpu as pltpu
from jax.sharding import PartitionSpec as P

TILE = 256
ROWS = 512
F32 = jnp.float32
BF16 = jnp.bfloat16


def partner(block, axis, position):
    count = lax.axis_size(axis)
    return lax.ppermute(block, axis, [(at, at ^ (1 << position)) for at in range(count)])


def split(value):
    high = value.astype(BF16)
    return high, (value - high.astype(F32)).astype(BF16)


def dot(left, right):
    return jnp.dot(left, right, preferred_element_type=F32)


def prepare_kernel(state_ref, turned_ref, whole_ref, first_ref):
    turned = state_ref[...].T
    turned_ref[...] = turned
    rounded = turned.astype(BF16)
    whole_ref[...] = rounded
    first_ref[...] = rounded[: first_ref.shape[0]]


def prepare(state, first):
    columns, states = state.shape
    full = pl.BlockSpec(memory_space=pltpu.VMEM)
    return pl.pallas_call(
        prepare_kernel,
        in_specs=[full],
        out_specs=[full] * 3,
        out_shape=[
            jax.ShapeDtypeStruct((states, columns), F32),
            jax.ShapeDtypeStruct((states, columns), BF16),
            jax.ShapeDtypeStruct((first, columns), BF16),
        ],
        compiler_params=pltpu.CompilerParams(vmem_limit_bytes=8 * 2**20),
        name="prepare",
    )(state)


def low_kernel(index_ref, values_hbm, state_ref, dense_ref, product_ref, token_ref, values, sems):
    brows, kept, size, _ = values.shape
    token_ref[...] = jnp.zeros(token_ref.shape, token_ref.dtype)
    rows = TILE // size

    def copy(first):
        at = pl.ds(first, rows)
        return pltpu.make_async_copy(values_hbm.at[at], values.at[at], sems.at[first // rows])

    for first in range(0, brows, rows):
        copy(first).start()
    for first in range(0, brows, rows):
        copy(first).wait()
        tile = slice(first * size, (first + rows) * size)
        dense_ref[tile, :] = jnp.zeros((rows * size, dense_ref.shape[1]), BF16)
        for row in range(first, first + rows):
            for at in range(kept):
                start = pl.multiple_of(index_ref[row, at] * size, size)
                dense_ref[row * size : (row + 1) * size, pl.ds(start, size)] = values[row, at].T
        product_ref[tile, :] = dot(dense_ref[tile, :], state_ref[...])


def low_operator(block_values, block_index, rounded):
    brows, kept, size, _ = block_values.shape
    width = brows * size
    columns = rounded.shape[1]
    full = pl.BlockSpec(memory_space=pltpu.VMEM)
    return pl.pallas_call(
        low_kernel,
        in_specs=[pl.BlockSpec(memory_space=pltpu.SMEM), pl.BlockSpec(memory_space=pltpu.HBM), full],
        out_specs=[full] * 3,
        out_shape=[
            jax.ShapeDtypeStruct((width, width), BF16),
            jax.ShapeDtypeStruct((width, columns), F32),
            jax.ShapeDtypeStruct((8, columns), jnp.int32),
        ],
        scratch_shapes=[
            pltpu.VMEM(block_values.shape, BF16),
            pltpu.SemaphoreType.DMA((brows * size // TILE,)),
        ],
        compiler_params=pltpu.CompilerParams(vmem_limit_bytes=2 * block_values.size + 4 * 2**20),
        name="low_operator",
    )(block_index, pltpu.with_memory_space_constraint(block_values, pltpu.HBM), rounded)


def bit_of(values, position):
    return jnp.bitwise_and(jnp.right_shift(values, position), 1)


def polynomial_kernel(
    spin_of_bond,
    sites_ref,
    coupling_ref,
    pin_sites_ref,
    pin_partner_ref,
    pinned_ref,
    pin_coupling_ref,
    cross_sites_ref,
    cross_coupling_ref,
    own_ref,
    high_ref,
    low_ref,
    token_ref,
    op_high,
    op_low,
    poly_ref,
):
    token_ref[...] = jnp.zeros(token_ref.shape, token_ref.dtype)
    whole, size = poly_ref.shape[1:]
    blocks = whole // size
    row = lax.broadcasted_iota(jnp.int32, (size, size), 0)
    col = lax.broadcasted_iota(jnp.int32, (size, size), 1)
    same = row == col
    zero = jnp.zeros((size, size), F32)
    matrix = zero
    field = zero
    for bond in range(sites_ref.shape[0]):
        one, two = sites_ref[bond, 0], sites_ref[bond, 1]
        strength = coupling_ref[bond]
        differ = jnp.bitwise_xor(bit_of(row, one), bit_of(row, two)).astype(F32)
        flips = jnp.bitwise_xor(
            jnp.left_shift(jnp.int32(1), one), jnp.left_shift(jnp.int32(1), two)
        )
        matrix += jnp.where(col == jnp.bitwise_xor(row, flips), strength * 0.5 * differ, 0.0)
        field += strength * (1.0 - 2.0 * differ) * 0.25
    for pin in range(pin_sites_ref.shape[0]):
        pinned = pinned_ref[pin_partner_ref[pin]]
        aligned = jnp.bitwise_xor(bit_of(row, pin_sites_ref[pin]), pinned).astype(F32)
        field += pin_coupling_ref[pin] * (1.0 - 2.0 * aligned) * 0.25
    spins = max(spin_of_bond) + 1
    fields = [[zero, zero] for _ in range(spins)]
    hops = [[zero, zero] for _ in range(spins)]
    for bond, spin in enumerate(spin_of_bond):
        site = cross_sites_ref[bond]
        strength = cross_coupling_ref[bond]
        target = jnp.bitwise_xor(row, jnp.left_shift(jnp.int32(1), site))
        for turned in range(2):
            own = jnp.bitwise_xor(own_ref[spin], turned)
            parity = jnp.bitwise_xor(bit_of(row, site), own).astype(F32)
            fields[spin][turned] += strength * (1.0 - 2.0 * parity) * 0.25
            hops[spin][turned] += jnp.where(col == target, strength * 0.5 * parity, 0.0)
    hop_parts = [[split(hops[spin][turned]) for turned in range(2)] for spin in range(spins)]
    op_high[...] = jnp.zeros(op_high.shape, BF16)
    op_low[...] = jnp.zeros(op_low.shape, BF16)
    poly_ref[0] = jnp.zeros((whole, size), F32)
    poly_ref[1] = jnp.zeros((whole, size), F32)
    poly_ref[0, :size, :] = jnp.where(same, 1.0, 0.0)
    for block in range(blocks):
        at = slice(block * size, (block + 1) * size)
        own_field = field
        for spin in range(spins):
            turned = block >> spin & 1
            own_field = own_field + fields[spin][turned]
            other = block ^ 1 << spin
            high, low = hop_parts[spin][turned]
            op_high[at, other * size : (other + 1) * size] = high
            op_low[at, other * size : (other + 1) * size] = low
            if other == 0:
                poly_ref[1, at, :] = hops[spin][turned]
        diagonal = matrix + jnp.where(same, own_field, 0.0)
        high, low = split(diagonal)
        op_high[at, at] = high
        op_low[at, at] = low
        if block == 0:
            poly_ref[1, at, :] = diagonal
    orders = high_ref.shape[1] // size
    tile = min(2 * TILE, whole)
    for order in range(1, orders + 1):
        high, low = split(poly_ref[order])
        high_ref[:, (order - 1) * size : order * size] = high
        low_ref[:, (order - 1) * size : order * size] = low
        if order == orders:
            break
        both = jnp.concatenate([high, low], axis=1)
        for start in range(0, whole, tile):
            at = slice(start, start + tile)
            product = dot(op_high[at, :], both)
            product = product[:, :size] + product[:, size:] + dot(op_low[at, :], high)
            poly_ref[order + 1, at, :] = 2.0 * product - poly_ref[order - 1, at, :]


def polynomial_columns(
    columns, spin_of_bond, orders, sites, coupling, pin_sites, pin_partner, pinned, pin_coupling, cross_sites, cross_coupling, own_bits
):
    whole = columns << (max(spin_of_bond) + 1)
    operands = (sites, coupling, pin_sites, pin_partner, pinned, pin_coupling, cross_sites, cross_coupling, own_bits)
    out = jax.ShapeDtypeStruct((whole, orders * columns), BF16)
    return pl.pallas_call(
        functools.partial(polynomial_kernel, spin_of_bond),
        in_specs=[pl.BlockSpec(memory_space=pltpu.SMEM)] * len(operands),
        out_specs=[pl.BlockSpec(memory_space=pltpu.VMEM)] * 3,
        out_shape=[out, out, jax.ShapeDtypeStruct((16, columns), BF16)],
        scratch_shapes=[
            pltpu.VMEM((whole, whole), BF16),
            pltpu.VMEM((whole, whole), BF16),
            pltpu.VMEM((orders + 1, whole, columns), F32),
        ],
        compiler_params=pltpu.CompilerParams(vmem_limit_bytes=4 * whole * whole + 24 * whole * columns + 4 * 2**20),
        name="polynomial_columns",
    )(*operands)


def chunk_kernel(start, places, arrays, summed, *refs):
    state_ref, product_ref, high_ref, low_ref, dense_ref = refs[:5]
    piece_refs = refs[5 : 5 + arrays]
    sum_ref, terms_ref = refs[-2:]
    width = terms_ref.shape[0]
    size = state_ref.shape[1]
    state = state_ref[start : start + width, :]
    product = product_ref[start : start + width, :]
    own, rest = split(state)
    pieces = [own]
    for owner in sorted(places):
        number, place = places[owner]
        pieces.append(piece_refs[number][:, place * size : (place + 1) * size])
    gathered = jnp.concatenate(pieces, axis=1)
    powers = dot(gathered, high_ref[...]) + dot(gathered, low_ref[...]) + dot(rest, high_ref[:size, :])
    one, two, three, four = (powers[:, k * size : (k + 1) * size] for k in range(4))
    both = jnp.concatenate([8.0 * product + 32.0 * one, 4.0 * product + 12.0 * one], axis=1).astype(BF16)
    terms_ref[:, :size] = 24.0 * two + 16.0 * state
    terms_ref[:, size : 2 * size] = 6.0 * two + 3.0 * state
    terms_ref[:, 2 * size : 3 * size] = 8.0 * (three + one)
    terms_ref[:, 3 * size : 4 * size] = three
    terms_ref[:, 4 * size :] = four
    for at in range(0, sum_ref.shape[0], ROWS):
        share = dot(dense_ref[at : at + ROWS, start : start + width], both)
        sum_ref[at : at + ROWS, :] = refs[5 + arrays][at : at + ROWS, :] + share if summed else share


def chunk_terms(start, width, state, product, high, low, dense, arrays, places, summed, ahead):
    states, columns = state.shape
    full = pl.BlockSpec(memory_space=pltpu.VMEM)
    operands = [state, product, high, low, dense, *arrays, *summed]
    return pl.pallas_call(
        functools.partial(chunk_kernel, start, places, len(arrays), len(summed)),
        in_specs=[full] * len(operands) + [pl.BlockSpec(memory_space=pl.ANY)] * len(ahead),
        out_specs=[full] * 2,
        out_shape=[
            jax.ShapeDtypeStruct((states, 2 * columns), F32),
            jax.ShapeDtypeStruct((width, 5 * columns), F32),
        ],
        compiler_params=pltpu.CompilerParams(vmem_limit_bytes=12 * 2**20),
        cost_estimate=pl.CostEstimate(flops=4 * 10**9, bytes_accessed=0, transcendentals=0),
        name="chunk_terms",
    )(*operands, *ahead)


def final_kernel(chunks, sum_ref, dense, *refs):
    term_refs = refs[:chunks]
    third_hbm, fourth_hbm, third, fourth, second, last, sems = refs[chunks:]
    size = third.shape[0]
    tiles = []
    row = 0
    for terms in term_refs:
        width = terms.shape[0]
        at = slice(row, row + width)
        second[at, :] = (sum_ref[at, :] + terms[:, : 2 * size]).astype(BF16)
        tiles.append((at, terms))
        row += width
    copies = []

    def give(source, target, at):
        copies.append(pltpu.make_async_copy(source.at[:, at], target.at[:, at], sems.at[len(copies)]))
        copies[-1].start()

    for at, terms in tiles:
        product = dot(dense[at, :], second[...])
        high, low = split(product[:, :size] + terms[:, 2 * size : 3 * size])
        last[at, :size] = high
        last[at, size:] = low
        third[:, at] = (product[:, size:] + terms[:, 3 * size : 4 * size]).T
        give(third, third_hbm, at)
    for at, terms in tiles:
        product = dot(dense[at, :], last[...])
        fourth[:, at] = (product[:, :size] + product[:, size:] + terms[:, 4 * size :]).T
        give(fourth, fourth_hbm, at)
    for copy in copies:
        copy.wait()


def final_vectors(summed, dense, terms):
    states, two = summed.shape
    columns = two // 2
    full = pl.BlockSpec(memory_space=pltpu.VMEM)
    operands = [summed, dense, *terms]
    out = jax.ShapeDtypeStruct((columns, states), F32)
    return pl.pallas_call(
        functools.partial(final_kernel, len(terms)),
        in_specs=[full] * len(operands),
        out_specs=[pl.BlockSpec(memory_space=pltpu.HBM)] * 2,
        out_shape=[out, out],
        scratch_shapes=[
            pltpu.VMEM((columns, states), F32),
            pltpu.VMEM((columns, states), F32),
            pltpu.VMEM((states, two), BF16),
            pltpu.VMEM((states, two), BF16),
            pltpu.SemaphoreType.DMA((2 * len(terms),)),
        ],
        compiler_params=pltpu.CompilerParams(vmem_limit_bytes=12 * 2**20),
        name="final_vectors",
    )(*operands)


def device_spins():
    wide_log = lax.axis_size("wide").bit_length() - 1
    narrow_log = lax.axis_size("narrow").bit_length() - 1
    of_bond = [("wide", wide_log - 1), ("wide", 0), ("narrow", narrow_log - 1), ("narrow", 0)]
    spins = []
    for bond in (0, 2, 3, 1):
        if of_bond[bond] not in spins:
            spins.append(of_bond[bond])
    return spins, [spins.index(spin) for spin in of_bond]


def after(value, token):
    return value + token[0, : value.shape[-1]].astype(value.dtype)


def gathered(early, first, middle, last):
    late = {1: first}
    for at, spin in enumerate(middle, 1):
        for owner in sorted(late):
            late[owner | 1 << at] = partner(late[owner], *spin)
    arrays = [late[owner] for owner in late] + [early[owner] for owner in early if owner]
    owners = [owner for owner in late] + [owner for owner in early if owner]
    places = {owner: (number, 0) for number, owner in enumerate(owners)}
    for group in ([*early, 1], [owner for owner in late if owner != 1]):
        if group:
            sent = jnp.concatenate([{**early, **late}[owner] for owner in group], axis=1)
            for place, owner in enumerate(group):
                places[owner | 1 << len(middle) + 1] = (len(arrays), place)
            arrays.append(partner(sent, *last))
    return arrays, places


def shards(initial, block_values, block_index, *column_operands):
    state = initial[0, 0]
    columns, states = state.shape
    part = states // 16
    splits = [[6 * part, 4 * part], [3 * part, 3 * part]]
    spins, spin_of_bond = device_spins()
    own_bits = jnp.stack([bit_of(lax.axis_index(axis), position) for axis, position in spins]).astype(jnp.int32)
    turned, rounded, first = prepare(state, sum(splits[0]))
    firsts = [partner(first, *spins[0])]
    early = {0: rounded}
    for at, spin in enumerate(spins[1:-1], 1):
        for owner in sorted(early):
            early[owner | 1 << at] = partner(early[owner], *spin)
    dense, product, token = low_operator(block_values, block_index, rounded)
    start = sum(splits[0])
    firsts.append(partner(after(rounded[start : start + sum(splits[1])], token), *spins[0]))
    high, low, token = polynomial_columns(columns, spin_of_bond, 4, *column_operands, after(own_bits, token))
    pieces, afters = [], []
    start = 0
    for first, widths in zip(firsts, splits):
        first = after(first, token)
        for chunk, width in enumerate(widths):
            inside = sum(widths[:chunk])
            own_parts = {owner: piece[start + inside : start + inside + width] for owner, piece in early.items()}
            pieces.append(gathered(own_parts, first[inside : inside + width], spins[1:-1], spins[-1]))
        afters.append(first)
        token = pieces[-len(widths)][0][1][:1] * 0
        start += sum(widths)
    terms, summed = [], []
    start = 0
    for number, widths in enumerate(splits):
        for width in widths:
            total, term = chunk_terms(
                start, width, turned, product, high, low, dense, *pieces[len(terms)], summed, afters[number + 1 : number + 2]
            )
            summed = [total]
            terms.append(term)
            start += width
    third, fourth = final_vectors(total, dense, terms)
    return third[None, None], fourth[None, None]


def solution(mesh):
    vector = P("wide", "narrow", None, None)
    return jax.shard_map(
        shards,
        mesh=mesh,
        in_specs=(vector,) + (P(),) * 10,
        out_specs=(vector, vector),
        check_vma=False,
    )
```

```python
import functools

import jax
import jax.numpy as jnp
from jax import lax
from jax.experimental import pallas as pl
from jax.experimental.pallas import tpu as pltpu
from jax.sharding import PartitionSpec as P

TILE = 256
ROWS = 512
F32 = jnp.float32
BF16 = jnp.bfloat16


def partner(block, axis, position):
    count = lax.axis_size(axis)
    return lax.ppermute(block, axis, [(at, at ^ (1 << position)) for at in range(count)])


def split(value):
    high = value.astype(BF16)
    return high, (value - high.astype(F32)).astype(BF16)


def dot(left, right):
    return jnp.dot(left, right, preferred_element_type=F32)


def prepare_kernel(state_ref, turned_ref, whole_ref, first_ref):
    turned = state_ref[...].T
    turned_ref[...] = turned
    rounded = turned.astype(BF16)
    whole_ref[...] = rounded
    first_ref[...] = rounded[: first_ref.shape[0]]


def prepare(state, first):
    columns, states = state.shape
    full = pl.BlockSpec(memory_space=pltpu.VMEM)
    return pl.pallas_call(
        prepare_kernel,
        in_specs=[full],
        out_specs=[full] * 3,
        out_shape=[
            jax.ShapeDtypeStruct((states, columns), F32),
            jax.ShapeDtypeStruct((states, columns), BF16),
            jax.ShapeDtypeStruct((first, columns), BF16),
        ],
        compiler_params=pltpu.CompilerParams(vmem_limit_bytes=8 * 2**20),
        name="prepare",
    )(state)


def low_kernel(index_ref, values_hbm, state_ref, dense_ref, product_ref, part_ref, values, sems):
    brows, kept, size, _ = values.shape
    part_ref[...] = state_ref[state_ref.shape[0] - part_ref.shape[0] :, :]
    rows = TILE // size

    def copy(first):
        at = pl.ds(first, rows)
        return pltpu.make_async_copy(values_hbm.at[at], values.at[at], sems.at[first // rows])

    for first in range(0, brows, rows):
        copy(first).start()
    for first in range(0, brows, rows):
        copy(first).wait()
        tile = slice(first * size, (first + rows) * size)
        dense_ref[tile, :] = jnp.zeros((rows * size, dense_ref.shape[1]), BF16)
        for row in range(first, first + rows):
            for at in range(kept):
                start = pl.multiple_of(index_ref[row, at] * size, size)
                dense_ref[row * size : (row + 1) * size, pl.ds(start, size)] = values[row, at].T
        product_ref[tile, :] = dot(dense_ref[tile, :], state_ref[...])


def low_operator(block_values, block_index, rounded, part):
    brows, kept, size, _ = block_values.shape
    width = brows * size
    columns = rounded.shape[1]
    full = pl.BlockSpec(memory_space=pltpu.VMEM)
    return pl.pallas_call(
        low_kernel,
        in_specs=[pl.BlockSpec(memory_space=pltpu.SMEM), pl.BlockSpec(memory_space=pltpu.HBM), full],
        out_specs=[full] * 3,
        out_shape=[
            jax.ShapeDtypeStruct((width, width), BF16),
            jax.ShapeDtypeStruct((width, columns), F32),
            jax.ShapeDtypeStruct((part, columns), BF16),
        ],
        scratch_shapes=[
            pltpu.VMEM(block_values.shape, BF16),
            pltpu.SemaphoreType.DMA((brows * size // TILE,)),
        ],
        compiler_params=pltpu.CompilerParams(vmem_limit_bytes=2 * block_values.size + 4 * 2**20),
        name="low_operator",
    )(block_index, pltpu.with_memory_space_constraint(block_values, pltpu.HBM), rounded)


def bit_of(values, position):
    return jnp.bitwise_and(jnp.right_shift(values, position), 1)


def polynomial_kernel(
    spins,
    spin_of_bond,
    sites_ref,
    coupling_ref,
    pin_sites_ref,
    pin_partner_ref,
    pinned_ref,
    pin_coupling_ref,
    cross_sites_ref,
    cross_coupling_ref,
    before_ref,
    high_ref,
    low_ref,
    token_ref,
    op_high,
    op_low,
    poly_ref,
):
    token_ref[...] = jnp.zeros(token_ref.shape, token_ref.dtype)
    whole, size = poly_ref.shape[1:]
    blocks = whole // size
    row = lax.broadcasted_iota(jnp.int32, (size, size), 0)
    col = lax.broadcasted_iota(jnp.int32, (size, size), 1)
    same = row == col
    zero = jnp.zeros((size, size), F32)
    matrix = zero
    field = zero
    for bond in range(sites_ref.shape[0]):
        one, two = sites_ref[bond, 0], sites_ref[bond, 1]
        strength = coupling_ref[bond]
        differ = jnp.bitwise_xor(bit_of(row, one), bit_of(row, two)).astype(F32)
        flips = jnp.bitwise_xor(
            jnp.left_shift(jnp.int32(1), one), jnp.left_shift(jnp.int32(1), two)
        )
        matrix += jnp.where(col == jnp.bitwise_xor(row, flips), strength * 0.5 * differ, 0.0)
        field += strength * (1.0 - 2.0 * differ) * 0.25
    for pin in range(pin_sites_ref.shape[0]):
        pinned = pinned_ref[pin_partner_ref[pin]]
        aligned = jnp.bitwise_xor(bit_of(row, pin_sites_ref[pin]), pinned).astype(F32)
        field += pin_coupling_ref[pin] * (1.0 - 2.0 * aligned) * 0.25
    own_bits = [bit_of(lax.axis_index(axis), position) for axis, position in spins]
    fields = [[zero, zero] for _ in spins]
    hops = [[zero, zero] for _ in spins]
    for bond, spin in enumerate(spin_of_bond):
        site = cross_sites_ref[bond]
        strength = cross_coupling_ref[bond]
        target = jnp.bitwise_xor(row, jnp.left_shift(jnp.int32(1), site))
        for turned in range(2):
            own = jnp.bitwise_xor(own_bits[spin], turned)
            parity = jnp.bitwise_xor(bit_of(row, site), own).astype(F32)
            fields[spin][turned] += strength * (1.0 - 2.0 * parity) * 0.25
            hops[spin][turned] += jnp.where(col == target, strength * 0.5 * parity, 0.0)
    hop_parts = [[split(hops[spin][turned]) for turned in range(2)] for spin in range(len(spins))]
    op_high[...] = jnp.zeros(op_high.shape, BF16)
    op_low[...] = jnp.zeros(op_low.shape, BF16)
    poly_ref[0] = jnp.zeros((whole, size), F32)
    poly_ref[1] = jnp.zeros((whole, size), F32)
    poly_ref[0, :size, :] = jnp.where(same, 1.0, 0.0)
    for block in range(blocks):
        at = slice(block * size, (block + 1) * size)
        own_field = field
        for spin in range(len(spins)):
            turned = block >> spin & 1
            own_field = own_field + fields[spin][turned]
            other = block ^ 1 << spin
            high, low = hop_parts[spin][turned]
            op_high[at, other * size : (other + 1) * size] = high
            op_low[at, other * size : (other + 1) * size] = low
            if other == 0:
                poly_ref[1, at, :] = hops[spin][turned]
        diagonal = matrix + jnp.where(same, own_field, 0.0)
        high, low = split(diagonal)
        op_high[at, at] = high
        op_low[at, at] = low
        if block == 0:
            poly_ref[1, at, :] = diagonal
    orders = high_ref.shape[1] // size
    tile = min(2 * TILE, whole)
    for order in range(1, orders + 1):
        high, low = split(poly_ref[order])
        high_ref[:, (order - 1) * size : order * size] = high
        low_ref[:, (order - 1) * size : order * size] = low
        if order == orders:
            break
        both = jnp.concatenate([high, low], axis=1)
        for start in range(0, whole, tile):
            at = slice(start, start + tile)
            product = dot(op_high[at, :], both)
            product = product[:, :size] + product[:, size:] + dot(op_low[at, :], high)
            poly_ref[order + 1, at, :] = 2.0 * product - poly_ref[order - 1, at, :]


def polynomial_columns(columns, spins, spin_of_bond, orders, operands, before):
    whole = columns << len(spins)
    out = jax.ShapeDtypeStruct((whole, orders * columns), BF16)
    return pl.pallas_call(
        functools.partial(polynomial_kernel, spins, spin_of_bond),
        in_specs=[pl.BlockSpec(memory_space=pltpu.SMEM)] * len(operands) + [pl.BlockSpec(memory_space=pl.ANY)],
        out_specs=[pl.BlockSpec(memory_space=pltpu.VMEM)] * 3,
        out_shape=[out, out, jax.ShapeDtypeStruct((16, columns), BF16)],
        scratch_shapes=[
            pltpu.VMEM((whole, whole), BF16),
            pltpu.VMEM((whole, whole), BF16),
            pltpu.VMEM((orders + 1, whole, columns), F32),
        ],
        compiler_params=pltpu.CompilerParams(vmem_limit_bytes=4 * whole * whole + 24 * whole * columns + 4 * 2**20),
        name="polynomial_columns",
    )(*operands, before)


def chunk_kernel(start, places, arrays, summed, *refs):
    state_ref, product_ref, high_ref, low_ref, dense_ref = refs[:5]
    piece_refs = refs[5 : 5 + arrays]
    sum_ref, terms_ref = refs[-2:]
    width = terms_ref.shape[0]
    size = state_ref.shape[1]
    state = state_ref[start : start + width, :]
    product = product_ref[start : start + width, :]
    own, rest = split(state)
    pieces = [own]
    for owner in sorted(places):
        number, place = places[owner]
        pieces.append(piece_refs[number][:, place * size : (place + 1) * size])
    gathered = jnp.concatenate(pieces, axis=1)
    powers = dot(gathered, high_ref[...]) + dot(gathered, low_ref[...]) + dot(rest, high_ref[:size, :])
    one, two, three, four = (powers[:, k * size : (k + 1) * size] for k in range(4))
    both = jnp.concatenate([8.0 * product + 32.0 * one, 4.0 * product + 12.0 * one], axis=1).astype(BF16)
    terms_ref[:, :size] = 24.0 * two + 16.0 * state
    terms_ref[:, size : 2 * size] = 6.0 * two + 3.0 * state
    terms_ref[:, 2 * size : 3 * size] = 8.0 * (three + one)
    terms_ref[:, 3 * size : 4 * size] = three
    terms_ref[:, 4 * size :] = four
    for at in range(0, sum_ref.shape[0], ROWS):
        share = dot(dense_ref[at : at + ROWS, start : start + width], both)
        sum_ref[at : at + ROWS, :] = refs[5 + arrays][at : at + ROWS, :] + share if summed else share


def chunk_terms(start, width, state, product, high, low, dense, arrays, places, summed, ahead):
    states, columns = state.shape
    full = pl.BlockSpec(memory_space=pltpu.VMEM)
    operands = [state, product, high, low, dense, *arrays, *summed]
    return pl.pallas_call(
        functools.partial(chunk_kernel, start, places, len(arrays), len(summed)),
        in_specs=[full] * len(operands) + [pl.BlockSpec(memory_space=pl.ANY)] * len(ahead),
        out_specs=[full] * 2,
        out_shape=[
            jax.ShapeDtypeStruct((states, 2 * columns), F32),
            jax.ShapeDtypeStruct((width, 5 * columns), F32),
        ],
        compiler_params=pltpu.CompilerParams(vmem_limit_bytes=12 * 2**20),
        cost_estimate=pl.CostEstimate(flops=4 * 10**9, bytes_accessed=0, transcendentals=0),
        name="chunk_terms",
    )(*operands, *ahead)


def final_kernel(chunks, sum_ref, dense, *refs):
    term_refs = refs[:chunks]
    third_hbm, fourth_hbm, third, fourth, second, last, sems = refs[chunks:]
    size = third.shape[0]
    tiles = []
    row = 0
    for terms in term_refs:
        width = terms.shape[0]
        at = slice(row, row + width)
        second[at, :] = (sum_ref[at, :] + terms[:, : 2 * size]).astype(BF16)
        tiles.append((at, terms))
        row += width
    copies = []

    def give(source, target, at):
        copies.append(pltpu.make_async_copy(source.at[:, at], target.at[:, at], sems.at[len(copies)]))
        copies[-1].start()

    for at, terms in tiles:
        product = dot(dense[at, :], second[...])
        high, low = split(product[:, :size] + terms[:, 2 * size : 3 * size])
        last[at, :size] = high
        last[at, size:] = low
        third[:, at] = (product[:, size:] + terms[:, 3 * size : 4 * size]).T
        give(third, third_hbm, at)
    for at, terms in tiles:
        product = dot(dense[at, :], last[...])
        fourth[:, at] = (product[:, :size] + product[:, size:] + terms[:, 4 * size :]).T
        give(fourth, fourth_hbm, at)
    for copy in copies:
        copy.wait()


def final_vectors(summed, dense, terms):
    states, two = summed.shape
    columns = two // 2
    full = pl.BlockSpec(memory_space=pltpu.VMEM)
    operands = [summed, dense, *terms]
    out = jax.ShapeDtypeStruct((columns, states), F32)
    return pl.pallas_call(
        functools.partial(final_kernel, len(terms)),
        in_specs=[full] * len(operands),
        out_specs=[pl.BlockSpec(memory_space=pltpu.HBM)] * 2,
        out_shape=[out, out],
        scratch_shapes=[
            pltpu.VMEM((columns, states), F32),
            pltpu.VMEM((columns, states), F32),
            pltpu.VMEM((states, two), BF16),
            pltpu.VMEM((states, two), BF16),
            pltpu.SemaphoreType.DMA((2 * len(terms),)),
        ],
        compiler_params=pltpu.CompilerParams(vmem_limit_bytes=12 * 2**20),
        name="final_vectors",
    )(*operands)


def device_spins():
    wide_log = lax.axis_size("wide").bit_length() - 1
    narrow_log = lax.axis_size("narrow").bit_length() - 1
    of_bond = [("wide", wide_log - 1), ("wide", 0), ("narrow", narrow_log - 1), ("narrow", 0)]
    spins = []
    for bond in (0, 2, 3, 1):
        if of_bond[bond] not in spins:
            spins.append(of_bond[bond])
    return spins, [spins.index(spin) for spin in of_bond]


def after(value, token):
    return value + token[0, : value.shape[-1]].astype(value.dtype)


def gathered(early, first, middle, last):
    late = {1: first}
    for at, spin in enumerate(middle, 1):
        for owner in sorted(late):
            late[owner | 1 << at] = partner(late[owner], *spin)
    arrays = [late[owner] for owner in late] + [early[owner] for owner in early if owner]
    owners = [owner for owner in late] + [owner for owner in early if owner]
    places = {owner: (number, 0) for number, owner in enumerate(owners)}
    for group in ([*early, 1], [owner for owner in late if owner != 1]):
        if group:
            sent = jnp.concatenate([{**early, **late}[owner] for owner in group], axis=1)
            for place, owner in enumerate(group):
                places[owner | 1 << len(middle) + 1] = (len(arrays), place)
            arrays.append(partner(sent, *last))
    return arrays, places


def shards(initial, block_values, block_index, *column_operands):
    state = initial[0, 0]
    columns, states = state.shape
    part = states // 16
    splits = [[6 * part, 4 * part], [3 * part, 3 * part]]
    spins, spin_of_bond = device_spins()
    turned, rounded, first = prepare(state, sum(splits[0]))
    firsts = [partner(first, *spins[0])]
    early = {0: rounded}
    for at, spin in enumerate(spins[1:-1], 1):
        for owner in sorted(early):
            early[owner | 1 << at] = partner(early[owner], *spin)
    dense, product, second = low_operator(block_values, block_index, rounded, sum(splits[1]))
    firsts.append(partner(second, *spins[0]))
    high, low, token = polynomial_columns(columns, spins, spin_of_bond, 4, column_operands, product)
    pieces, afters = [], []
    start = 0
    for first, widths in zip(firsts, splits):
        first = after(first, token)
        for chunk, width in enumerate(widths):
            inside = sum(widths[:chunk])
            own_parts = {owner: piece[start + inside : start + inside + width] for owner, piece in early.items()}
            pieces.append(gathered(own_parts, first[inside : inside + width], spins[1:-1], spins[-1]))
        afters.append(first)
        token = pieces[-len(widths)][0][1][:1] * 0
        start += sum(widths)
    terms, summed = [], []
    start = 0
    for number, widths in enumerate(splits):
        for width in widths:
            total, term = chunk_terms(
                start, width, turned, product, high, low, dense, *pieces[len(terms)], summed, afters[number + 1 : number + 2]
            )
            summed = [total]
            terms.append(term)
            start += width
    third, fourth = final_vectors(total, dense, terms)
    return third[None, None], fourth[None, None]


def solution(mesh):
    vector = P("wide", "narrow", None, None)
    return jax.shard_map(
        shards,
        mesh=mesh,
        in_specs=(vector,) + (P(),) * 10,
        out_specs=(vector, vector),
        check_vma=False,
    )
```

```python
import functools

import jax
import jax.numpy as jnp
from jax import lax
from jax.experimental import pallas as pl
from jax.experimental.pallas import tpu as pltpu
from jax.sharding import PartitionSpec as P

TILE = 256
ROWS = 512
F32 = jnp.float32
BF16 = jnp.bfloat16


def partner(block, axis, position):
    count = lax.axis_size(axis)
    return lax.ppermute(block, axis, [(at, at ^ (1 << position)) for at in range(count)])


def split(value):
    high = value.astype(BF16)
    return high, (value - high.astype(F32)).astype(BF16)


def dot(left, right):
    return jnp.dot(left, right, preferred_element_type=F32)


def prepare_kernel(state_ref, turned_ref, whole_ref, first_ref):
    turned = state_ref[...].T
    turned_ref[...] = turned
    rounded = turned.astype(BF16)
    whole_ref[...] = rounded
    first_ref[...] = rounded[: first_ref.shape[0]]


def prepare(state, first):
    columns, states = state.shape
    full = pl.BlockSpec(memory_space=pltpu.VMEM)
    return pl.pallas_call(
        prepare_kernel,
        in_specs=[full],
        out_specs=[full] * 3,
        out_shape=[
            jax.ShapeDtypeStruct((states, columns), F32),
            jax.ShapeDtypeStruct((states, columns), BF16),
            jax.ShapeDtypeStruct((first, columns), BF16),
        ],
        compiler_params=pltpu.CompilerParams(vmem_limit_bytes=8 * 2**20),
        name="prepare",
    )(state)


def low_kernel(index_ref, values_hbm, state_ref, dense_ref, product_ref, part_ref, values, sems):
    brows, kept, size, _ = values.shape
    part_ref[...] = state_ref[state_ref.shape[0] - part_ref.shape[0] :, :]
    rows = TILE // size

    def copy(first):
        at = pl.ds(first, rows)
        return pltpu.make_async_copy(values_hbm.at[at], values.at[at], sems.at[first // rows])

    for first in range(0, brows, rows):
        copy(first).start()
    for first in range(0, brows, rows):
        copy(first).wait()
        tile = slice(first * size, (first + rows) * size)
        dense_ref[tile, :] = jnp.zeros((rows * size, dense_ref.shape[1]), BF16)
        for row in range(first, first + rows):
            for at in range(kept):
                start = pl.multiple_of(index_ref[row, at] * size, size)
                dense_ref[row * size : (row + 1) * size, pl.ds(start, size)] = values[row, at].T
        product_ref[tile, :] = dot(dense_ref[tile, :], state_ref[...])


def low_operator(block_values, block_index, rounded, part):
    brows, kept, size, _ = block_values.shape
    width = brows * size
    columns = rounded.shape[1]
    full = pl.BlockSpec(memory_space=pltpu.VMEM)
    return pl.pallas_call(
        low_kernel,
        in_specs=[pl.BlockSpec(memory_space=pltpu.SMEM), pl.BlockSpec(memory_space=pltpu.HBM), full],
        out_specs=[full] * 3,
        out_shape=[
            jax.ShapeDtypeStruct((width, width), BF16),
            jax.ShapeDtypeStruct((width, columns), F32),
            jax.ShapeDtypeStruct((part, columns), BF16),
        ],
        scratch_shapes=[
            pltpu.VMEM(block_values.shape, BF16),
            pltpu.SemaphoreType.DMA((brows * size // TILE,)),
        ],
        compiler_params=pltpu.CompilerParams(vmem_limit_bytes=2 * block_values.size + 4 * 2**20),
        name="low_operator",
    )(block_index, pltpu.with_memory_space_constraint(block_values, pltpu.HBM), rounded)


def bit_of(values, position):
    return jnp.bitwise_and(jnp.right_shift(values, position), 1)


def polynomial_kernel(
    spins,
    spin_of_bond,
    sites_ref,
    coupling_ref,
    pin_sites_ref,
    pin_partner_ref,
    pinned_ref,
    pin_coupling_ref,
    cross_sites_ref,
    cross_coupling_ref,
    before_ref,
    high_ref,
    low_ref,
    token_ref,
    op_high,
    op_low,
    poly_ref,
):
    token_ref[...] = jnp.zeros(token_ref.shape, token_ref.dtype)
    whole, size = poly_ref.shape[1:]
    blocks = whole // size
    row = lax.broadcasted_iota(jnp.int32, (size, size), 0)
    col = lax.broadcasted_iota(jnp.int32, (size, size), 1)
    same = row == col
    zero = jnp.zeros((size, size), F32)
    matrix = zero
    field = zero
    for bond in range(sites_ref.shape[1]):
        one, two = sites_ref[0, bond], sites_ref[1, bond]
        strength = coupling_ref[bond]
        differ = jnp.bitwise_xor(bit_of(row, one), bit_of(row, two)).astype(F32)
        flips = jnp.bitwise_xor(
            jnp.left_shift(jnp.int32(1), one), jnp.left_shift(jnp.int32(1), two)
        )
        matrix += jnp.where(col == jnp.bitwise_xor(row, flips), strength * 0.5 * differ, 0.0)
        field += strength * (1.0 - 2.0 * differ) * 0.25
    for pin in range(pin_sites_ref.shape[0]):
        pinned = pinned_ref[pin_partner_ref[pin]]
        aligned = jnp.bitwise_xor(bit_of(row, pin_sites_ref[pin]), pinned).astype(F32)
        field += pin_coupling_ref[pin] * (1.0 - 2.0 * aligned) * 0.25
    own_bits = [bit_of(lax.axis_index(axis), position) for axis, position in spins]
    fields = [[zero, zero] for _ in spins]
    hops = [[zero, zero] for _ in spins]
    for bond, spin in enumerate(spin_of_bond):
        site = cross_sites_ref[bond]
        strength = cross_coupling_ref[bond]
        target = jnp.bitwise_xor(row, jnp.left_shift(jnp.int32(1), site))
        for turned in range(2):
            own = jnp.bitwise_xor(own_bits[spin], turned)
            parity = jnp.bitwise_xor(bit_of(row, site), own).astype(F32)
            fields[spin][turned] += strength * (1.0 - 2.0 * parity) * 0.25
            hops[spin][turned] += jnp.where(col == target, strength * 0.5 * parity, 0.0)
    hop_parts = [[split(hops[spin][turned]) for turned in range(2)] for spin in range(len(spins))]
    op_high[...] = jnp.zeros(op_high.shape, BF16)
    op_low[...] = jnp.zeros(op_low.shape, BF16)
    poly_ref[0] = jnp.zeros((whole, size), F32)
    poly_ref[1] = jnp.zeros((whole, size), F32)
    poly_ref[0, :size, :] = jnp.where(same, 1.0, 0.0)
    for block in range(blocks):
        at = slice(block * size, (block + 1) * size)
        own_field = field
        for spin in range(len(spins)):
            turned = block >> spin & 1
            own_field = own_field + fields[spin][turned]
            other = block ^ 1 << spin
            high, low = hop_parts[spin][turned]
            op_high[at, other * size : (other + 1) * size] = high
            op_low[at, other * size : (other + 1) * size] = low
            if other == 0:
                poly_ref[1, at, :] = hops[spin][turned]
        diagonal = matrix + jnp.where(same, own_field, 0.0)
        high, low = split(diagonal)
        op_high[at, at] = high
        op_low[at, at] = low
        if block == 0:
            poly_ref[1, at, :] = diagonal
    orders = high_ref.shape[1] // size
    tile = min(2 * TILE, whole)
    for order in range(1, orders + 1):
        high, low = split(poly_ref[order])
        high_ref[:, (order - 1) * size : order * size] = high
        low_ref[:, (order - 1) * size : order * size] = low
        if order == orders:
            break
        both = jnp.concatenate([high, low], axis=1)
        for start in range(0, whole, tile):
            at = slice(start, start + tile)
            product = dot(op_high[at, :], both)
            product = product[:, :size] + product[:, size:] + dot(op_low[at, :], high)
            poly_ref[order + 1, at, :] = 2.0 * product - poly_ref[order - 1, at, :]


def polynomial_columns(columns, spins, spin_of_bond, orders, operands, before):
    whole = columns << len(spins)
    out = jax.ShapeDtypeStruct((whole, orders * columns), BF16)
    return pl.pallas_call(
        functools.partial(polynomial_kernel, spins, spin_of_bond),
        in_specs=[pl.BlockSpec(memory_space=pltpu.SMEM)] * len(operands) + [pl.BlockSpec(memory_space=pl.ANY)],
        out_specs=[pl.BlockSpec(memory_space=pltpu.VMEM)] * 3,
        out_shape=[out, out, jax.ShapeDtypeStruct((16, columns), BF16)],
        scratch_shapes=[
            pltpu.VMEM((whole, whole), BF16),
            pltpu.VMEM((whole, whole), BF16),
            pltpu.VMEM((orders + 1, whole, columns), F32),
        ],
        compiler_params=pltpu.CompilerParams(vmem_limit_bytes=4 * whole * whole + 24 * whole * columns + 4 * 2**20),
        name="polynomial_columns",
    )(*operands, before)


def chunk_kernel(start, places, arrays, summed, *refs):
    state_ref, product_ref, high_ref, low_ref, dense_ref = refs[:5]
    piece_refs = refs[5 : 5 + arrays]
    sum_ref, terms_ref, token_ref = refs[-3:]
    token_ref[...] = jnp.zeros(token_ref.shape, token_ref.dtype)
    width = terms_ref.shape[0]
    size = state_ref.shape[1]
    state = state_ref[start : start + width, :]
    product = product_ref[start : start + width, :]
    own, rest = split(state)
    pieces = [own]
    for owner in sorted(places):
        number, place = places[owner]
        pieces.append(piece_refs[number][:, place * size : (place + 1) * size])
    gathered = jnp.concatenate(pieces, axis=1)
    powers = dot(gathered, high_ref[...]) + dot(gathered, low_ref[...]) + dot(rest, high_ref[:size, :])
    one, two, three, four = (powers[:, k * size : (k + 1) * size] for k in range(4))
    both = jnp.concatenate([8.0 * product + 32.0 * one, 4.0 * product + 12.0 * one], axis=1).astype(BF16)
    terms_ref[:, :size] = 24.0 * two + 16.0 * state
    terms_ref[:, size : 2 * size] = 6.0 * two + 3.0 * state
    terms_ref[:, 2 * size : 3 * size] = 8.0 * (three + one)
    terms_ref[:, 3 * size : 4 * size] = three
    terms_ref[:, 4 * size :] = four
    for at in range(0, sum_ref.shape[0], ROWS):
        share = dot(dense_ref[at : at + ROWS, start : start + width], both)
        sum_ref[at : at + ROWS, :] = refs[5 + arrays][at : at + ROWS, :] + share if summed else share


def chunk_terms(start, width, state, product, high, low, dense, arrays, places, summed, ahead):
    states, columns = state.shape
    full = pl.BlockSpec(memory_space=pltpu.VMEM)
    operands = [state, product, high, low, dense, *arrays, *summed]
    return pl.pallas_call(
        functools.partial(chunk_kernel, start, places, len(arrays), len(summed)),
        in_specs=[full] * len(operands) + [pl.BlockSpec(memory_space=pl.ANY)] * len(ahead),
        out_specs=[full] * 3,
        out_shape=[
            jax.ShapeDtypeStruct((states, 2 * columns), F32),
            jax.ShapeDtypeStruct((width, 5 * columns), F32),
            jax.ShapeDtypeStruct((16, columns), BF16),
        ],
        compiler_params=pltpu.CompilerParams(vmem_limit_bytes=12 * 2**20),
        cost_estimate=pl.CostEstimate(flops=4 * 10**9, bytes_accessed=0, transcendentals=0),
        name="chunk_terms",
    )(*operands, *ahead)


def final_kernel(chunks, sum_ref, dense, *refs):
    term_refs = refs[:chunks]
    third_hbm, fourth_hbm, third, fourth, second, last, sems = refs[chunks:]
    size = third.shape[0]
    tiles = []
    row = 0
    for terms in term_refs:
        width = terms.shape[0]
        at = slice(row, row + width)
        second[at, :] = (sum_ref[at, :] + terms[:, : 2 * size]).astype(BF16)
        tiles.append((at, terms))
        row += width
    copies = []

    def give(source, target, at):
        copies.append(pltpu.make_async_copy(source.at[:, at], target.at[:, at], sems.at[len(copies)]))
        copies[-1].start()

    for at, terms in tiles:
        product = dot(dense[at, :], second[...])
        high, low = split(product[:, :size] + terms[:, 2 * size : 3 * size])
        last[at, :size] = high
        last[at, size:] = low
        third[:, at] = (product[:, size:] + terms[:, 3 * size : 4 * size]).T
        give(third, third_hbm, at)
    for at, terms in tiles:
        product = dot(dense[at, :], last[...])
        fourth[:, at] = (product[:, :size] + product[:, size:] + terms[:, 4 * size :]).T
        give(fourth, fourth_hbm, at)
    for copy in copies:
        copy.wait()


def final_vectors(summed, dense, terms):
    states, two = summed.shape
    columns = two // 2
    full = pl.BlockSpec(memory_space=pltpu.VMEM)
    operands = [summed, dense, *terms]
    out = jax.ShapeDtypeStruct((columns, states), F32)
    return pl.pallas_call(
        functools.partial(final_kernel, len(terms)),
        in_specs=[full] * len(operands),
        out_specs=[pl.BlockSpec(memory_space=pltpu.HBM)] * 2,
        out_shape=[out, out],
        scratch_shapes=[
            pltpu.VMEM((columns, states), F32),
            pltpu.VMEM((columns, states), F32),
            pltpu.VMEM((states, two), BF16),
            pltpu.VMEM((states, two), BF16),
            pltpu.SemaphoreType.DMA((2 * len(terms),)),
        ],
        compiler_params=pltpu.CompilerParams(vmem_limit_bytes=12 * 2**20),
        name="final_vectors",
    )(*operands)


def device_spins():
    wide_log = lax.axis_size("wide").bit_length() - 1
    narrow_log = lax.axis_size("narrow").bit_length() - 1
    of_bond = [("wide", wide_log - 1), ("wide", 0), ("narrow", narrow_log - 1), ("narrow", 0)]
    spins = []
    for bond in (0, 2, 3, 1):
        if of_bond[bond] not in spins:
            spins.append(of_bond[bond])
    return spins, [spins.index(spin) for spin in of_bond]


def after(value, token):
    return value + token[0, : value.shape[-1]].astype(value.dtype)


def gathered(early, first, middle, last, hold):
    late = {1: first}
    for at, spin in enumerate(middle, 1):
        for owner in sorted(late):
            late[owner | 1 << at] = partner(late[owner], *spin)
    arrays = [late[owner] for owner in late] + [early[owner] for owner in early if owner]
    owners = [owner for owner in late] + [owner for owner in early if owner]
    places = {owner: (number, 0) for number, owner in enumerate(owners)}
    for group in ([*early, 1], [owner for owner in late if owner != 1]):
        if group:
            sent = jnp.concatenate([{**early, **late}[owner] for owner in group], axis=1)
            if hold is not None and 1 not in group:
                sent = after(sent, jnp.tile(hold, (1, len(group))))
            for place, owner in enumerate(group):
                places[owner | 1 << len(middle) + 1] = (len(arrays), place)
            arrays.append(partner(sent, *last))
    return arrays, places


def shards(initial, block_values, block_index, bond_sites, *column_operands):
    state = initial[0, 0]
    columns, states = state.shape
    part = states // 16
    splits = [[6 * part, 4 * part], [3 * part, 3 * part]]
    spins, spin_of_bond = device_spins()
    turned, rounded, first = prepare(state, sum(splits[0]))
    firsts = [partner(first, *spins[0])]
    early = {0: rounded}
    for at, spin in enumerate(spins[1:-1], 1):
        for owner in sorted(early):
            early[owner | 1 << at] = partner(early[owner], *spin)
    dense, product, second = low_operator(block_values, block_index, rounded, sum(splits[1]))
    firsts.append(partner(second, *spins[0]))
    high, low, token = polynomial_columns(columns, spins, spin_of_bond, 4, (bond_sites.T, *column_operands), product)
    terms, summed = [], []

    def run(pieces, widths, ahead):
        tokens = []
        for (arrays, places), width in zip(pieces, widths):
            start = sum(term.shape[0] for term in terms)
            total, term, token = chunk_terms(
                start, width, turned, product, high, low, dense, arrays, places, summed, ahead
            )
            summed[:] = [total]
            terms.append(term)
            tokens.append(token)
        return tokens

    start = 0
    pieces, tokens = [], []
    for number, (first, widths) in enumerate(zip(firsts, splits)):
        first = after(first, token)
        if number:
            tokens = run(pieces, splits[number - 1], [first])
        pieces = []
        for chunk, width in enumerate(widths):
            inside = sum(widths[:chunk])
            own_parts = {owner: piece[start + inside : start + inside + width] for owner, piece in early.items()}
            hold = tokens[min(chunk, len(tokens) - 1)] if tokens else None
            pieces.append(gathered(own_parts, first[inside : inside + width], spins[1:-1], spins[-1], hold))
        token = pieces[-1][0][-1][:1, :columns] * 0
        start += sum(widths)
    run(pieces, splits[-1], [])
    third, fourth = final_vectors(*summed, dense, terms)
    return third[None, None], fourth[None, None]


def solution(mesh):
    vector = P("wide", "narrow", None, None)
    return jax.shard_map(
        shards,
        mesh=mesh,
        in_specs=(vector,) + (P(),) * 10,
        out_specs=(vector, vector),
        check_vma=False,
    )
```

```python
import functools

import jax
import jax.numpy as jnp
from jax import lax
from jax.experimental import pallas as pl
from jax.experimental.pallas import tpu as pltpu
from jax.sharding import PartitionSpec as P

TILE = 256
ROWS = 512
F32 = jnp.float32
BF16 = jnp.bfloat16


def partner(block, axis, position):
    count = lax.axis_size(axis)
    return lax.ppermute(block, axis, [(at, at ^ (1 << position)) for at in range(count)])


def split(value):
    high = value.astype(BF16)
    return high, (value - high.astype(F32)).astype(BF16)


def dot(left, right):
    return jnp.dot(left, right, preferred_element_type=F32)


def prepare_kernel(state_ref, turned_ref, whole_ref, first_ref):
    turned = state_ref[...].T
    turned_ref[...] = turned
    rounded = turned.astype(BF16)
    whole_ref[...] = rounded
    first_ref[...] = rounded[: first_ref.shape[0]]


def prepare(state, first):
    columns, states = state.shape
    full = pl.BlockSpec(memory_space=pltpu.VMEM)
    return pl.pallas_call(
        prepare_kernel,
        in_specs=[full],
        out_specs=[full] * 3,
        out_shape=[
            jax.ShapeDtypeStruct((states, columns), F32),
            jax.ShapeDtypeStruct((states, columns), BF16),
            jax.ShapeDtypeStruct((first, columns), BF16),
        ],
        compiler_params=pltpu.CompilerParams(vmem_limit_bytes=8 * 2**20),
        name="prepare",
    )(state)


def low_kernel(part, index_ref, values_hbm, state_ref, dense_ref, product_ref, part_ref, token_ref, values, sems):
    brows, kept, size, _ = values.shape
    part_ref[...] = state_ref[part[0] : part[1], :]
    token_ref[...] = jnp.zeros(token_ref.shape, token_ref.dtype)
    rows = TILE // size

    def copy(first):
        at = pl.ds(first, rows)
        return pltpu.make_async_copy(values_hbm.at[at], values.at[at], sems.at[first // rows])

    for first in range(0, brows, rows):
        copy(first).start()
    for first in range(0, brows, rows):
        copy(first).wait()
        tile = slice(first * size, (first + rows) * size)
        dense_ref[tile, :] = jnp.zeros((rows * size, dense_ref.shape[1]), BF16)
        for row in range(first, first + rows):
            for at in range(kept):
                start = pl.multiple_of(index_ref[row, at] * size, size)
                dense_ref[row * size : (row + 1) * size, pl.ds(start, size)] = values[row, at].T
        product_ref[tile, :] = dot(dense_ref[tile, :], state_ref[...])


def low_operator(block_values, block_index, rounded, part):
    brows, kept, size, _ = block_values.shape
    width = brows * size
    columns = rounded.shape[1]
    full = pl.BlockSpec(memory_space=pltpu.VMEM)
    return pl.pallas_call(
        functools.partial(low_kernel, part),
        in_specs=[pl.BlockSpec(memory_space=pltpu.SMEM), pl.BlockSpec(memory_space=pltpu.HBM), full],
        out_specs=[full] * 4,
        out_shape=[
            jax.ShapeDtypeStruct((width, width), BF16),
            jax.ShapeDtypeStruct((width, columns), F32),
            jax.ShapeDtypeStruct((part[1] - part[0], columns), BF16),
            jax.ShapeDtypeStruct((16, columns), BF16),
        ],
        scratch_shapes=[
            pltpu.VMEM(block_values.shape, BF16),
            pltpu.SemaphoreType.DMA((brows * size // TILE,)),
        ],
        compiler_params=pltpu.CompilerParams(vmem_limit_bytes=2 * block_values.size + 4 * 2**20),
        name="low_operator",
    )(block_index, pltpu.with_memory_space_constraint(block_values, pltpu.HBM), rounded)


def bit_of(values, position):
    return jnp.bitwise_and(jnp.right_shift(values, position), 1)


def polynomial_kernel(
    spins,
    spin_of_bond,
    part,
    sites_ref,
    coupling_ref,
    pin_sites_ref,
    pin_partner_ref,
    pinned_ref,
    pin_coupling_ref,
    cross_sites_ref,
    cross_coupling_ref,
    state_ref,
    before_ref,
    high_ref,
    low_ref,
    part_ref,
    token_ref,
    op_high,
    op_low,
    poly_ref,
):
    part_ref[...] = state_ref[part[0] : part[1], :]
    token_ref[...] = jnp.zeros(token_ref.shape, token_ref.dtype)
    whole, size = poly_ref.shape[1:]
    blocks = whole // size
    row = lax.broadcasted_iota(jnp.int32, (size, size), 0)
    col = lax.broadcasted_iota(jnp.int32, (size, size), 1)
    same = row == col
    zero = jnp.zeros((size, size), F32)
    matrix = zero
    field = zero
    for bond in range(sites_ref.shape[1]):
        one, two = sites_ref[0, bond], sites_ref[1, bond]
        strength = coupling_ref[bond]
        differ = jnp.bitwise_xor(bit_of(row, one), bit_of(row, two)).astype(F32)
        flips = jnp.bitwise_xor(
            jnp.left_shift(jnp.int32(1), one), jnp.left_shift(jnp.int32(1), two)
        )
        matrix += jnp.where(col == jnp.bitwise_xor(row, flips), strength * 0.5 * differ, 0.0)
        field += strength * (1.0 - 2.0 * differ) * 0.25
    for pin in range(pin_sites_ref.shape[0]):
        pinned = pinned_ref[pin_partner_ref[pin]]
        aligned = jnp.bitwise_xor(bit_of(row, pin_sites_ref[pin]), pinned).astype(F32)
        field += pin_coupling_ref[pin] * (1.0 - 2.0 * aligned) * 0.25
    own_bits = [bit_of(lax.axis_index(axis), position) for axis, position in spins]
    fields = [[zero, zero] for _ in spins]
    hops = [[zero, zero] for _ in spins]
    for bond, spin in enumerate(spin_of_bond):
        site = cross_sites_ref[bond]
        strength = cross_coupling_ref[bond]
        target = jnp.bitwise_xor(row, jnp.left_shift(jnp.int32(1), site))
        for turned in range(2):
            own = jnp.bitwise_xor(own_bits[spin], turned)
            parity = jnp.bitwise_xor(bit_of(row, site), own).astype(F32)
            fields[spin][turned] += strength * (1.0 - 2.0 * parity) * 0.25
            hops[spin][turned] += jnp.where(col == target, strength * 0.5 * parity, 0.0)
    hop_parts = [[split(hops[spin][turned]) for turned in range(2)] for spin in range(len(spins))]
    op_high[...] = jnp.zeros(op_high.shape, BF16)
    op_low[...] = jnp.zeros(op_low.shape, BF16)
    poly_ref[0] = jnp.zeros((whole, size), F32)
    poly_ref[1] = jnp.zeros((whole, size), F32)
    poly_ref[0, :size, :] = jnp.where(same, 1.0, 0.0)
    for block in range(blocks):
        at = slice(block * size, (block + 1) * size)
        own_field = field
        for spin in range(len(spins)):
            turned = block >> spin & 1
            own_field = own_field + fields[spin][turned]
            other = block ^ 1 << spin
            high, low = hop_parts[spin][turned]
            op_high[at, other * size : (other + 1) * size] = high
            op_low[at, other * size : (other + 1) * size] = low
            if other == 0:
                poly_ref[1, at, :] = hops[spin][turned]
        diagonal = matrix + jnp.where(same, own_field, 0.0)
        high, low = split(diagonal)
        op_high[at, at] = high
        op_low[at, at] = low
        if block == 0:
            poly_ref[1, at, :] = diagonal
    orders = high_ref.shape[1] // size
    tile = min(2 * TILE, whole)
    for order in range(1, orders + 1):
        high, low = split(poly_ref[order])
        high_ref[:, (order - 1) * size : order * size] = high
        low_ref[:, (order - 1) * size : order * size] = low
        if order == orders:
            break
        both = jnp.concatenate([high, low], axis=1)
        for start in range(0, whole, tile):
            at = slice(start, start + tile)
            product = dot(op_high[at, :], both)
            product = product[:, :size] + product[:, size:] + dot(op_low[at, :], high)
            poly_ref[order + 1, at, :] = 2.0 * product - poly_ref[order - 1, at, :]


def polynomial_columns(spins, spin_of_bond, orders, operands, state, part, before):
    columns = state.shape[1]
    whole = columns << len(spins)
    out = jax.ShapeDtypeStruct((whole, orders * columns), BF16)
    return pl.pallas_call(
        functools.partial(polynomial_kernel, spins, spin_of_bond, part),
        in_specs=[pl.BlockSpec(memory_space=pltpu.SMEM)] * len(operands)
        + [pl.BlockSpec(memory_space=pltpu.VMEM), pl.BlockSpec(memory_space=pl.ANY)],
        out_specs=[pl.BlockSpec(memory_space=pltpu.VMEM)] * 4,
        out_shape=[out, out, jax.ShapeDtypeStruct((part[1] - part[0], columns), BF16), jax.ShapeDtypeStruct((16, columns), BF16)],
        scratch_shapes=[
            pltpu.VMEM((whole, whole), BF16),
            pltpu.VMEM((whole, whole), BF16),
            pltpu.VMEM((orders + 1, whole, columns), F32),
        ],
        compiler_params=pltpu.CompilerParams(vmem_limit_bytes=4 * whole * whole + 24 * whole * columns + 4 * 2**20),
        name="polynomial_columns",
    )(*operands, state, before)


def chunk_kernel(start, places, arrays, summed, *refs):
    state_ref, product_ref, high_ref, low_ref, dense_ref = refs[:5]
    piece_refs = refs[5 : 5 + arrays]
    sum_ref, terms_ref, token_ref = refs[-3:]
    token_ref[...] = jnp.zeros(token_ref.shape, token_ref.dtype)
    width = terms_ref.shape[0]
    size = state_ref.shape[1]
    state = state_ref[start : start + width, :]
    product = product_ref[start : start + width, :]
    own, rest = split(state)
    pieces = [own]
    for owner in sorted(places):
        number, place = places[owner]
        pieces.append(piece_refs[number][:, place * size : (place + 1) * size])
    gathered = jnp.concatenate(pieces, axis=1)
    powers = dot(gathered, high_ref[...]) + dot(gathered, low_ref[...]) + dot(rest, high_ref[:size, :])
    one, two, three, four = (powers[:, k * size : (k + 1) * size] for k in range(4))
    both = jnp.concatenate([8.0 * product + 32.0 * one, 4.0 * product + 12.0 * one], axis=1).astype(BF16)
    terms_ref[:, :size] = 24.0 * two + 16.0 * state
    terms_ref[:, size : 2 * size] = 6.0 * two + 3.0 * state
    terms_ref[:, 2 * size : 3 * size] = 8.0 * (three + one)
    terms_ref[:, 3 * size : 4 * size] = three
    terms_ref[:, 4 * size :] = four
    for at in range(0, sum_ref.shape[0], ROWS):
        share = dot(dense_ref[at : at + ROWS, start : start + width], both)
        sum_ref[at : at + ROWS, :] = refs[5 + arrays][at : at + ROWS, :] + share if summed else share


def chunk_terms(start, width, state, product, high, low, dense, arrays, places, summed, ahead):
    states, columns = state.shape
    full = pl.BlockSpec(memory_space=pltpu.VMEM)
    operands = [state, product, high, low, dense, *arrays, *summed]
    return pl.pallas_call(
        functools.partial(chunk_kernel, start, places, len(arrays), len(summed)),
        in_specs=[full] * len(operands) + [pl.BlockSpec(memory_space=pl.ANY)] * len(ahead),
        out_specs=[full] * 3,
        out_shape=[
            jax.ShapeDtypeStruct((states, 2 * columns), F32),
            jax.ShapeDtypeStruct((width, 5 * columns), F32),
            jax.ShapeDtypeStruct((16, columns), BF16),
        ],
        compiler_params=pltpu.CompilerParams(vmem_limit_bytes=12 * 2**20),
        cost_estimate=pl.CostEstimate(flops=4 * 10**9, bytes_accessed=0, transcendentals=0),
        name="chunk_terms",
    )(*operands, *ahead)


def final_kernel(chunks, sum_ref, dense, *refs):
    term_refs = refs[:chunks]
    third_hbm, fourth_hbm, third, fourth, second, last, sems = refs[chunks:]
    size = third.shape[0]
    tiles = []
    row = 0
    for terms in term_refs:
        width = terms.shape[0]
        at = slice(row, row + width)
        second[at, :] = (sum_ref[at, :] + terms[:, : 2 * size]).astype(BF16)
        tiles.append((at, terms))
        row += width
    copies = []

    def give(source, target, at):
        copies.append(pltpu.make_async_copy(source.at[:, at], target.at[:, at], sems.at[len(copies)]))
        copies[-1].start()

    for at, terms in tiles:
        product = dot(dense[at, :], second[...])
        high, low = split(product[:, :size] + terms[:, 2 * size : 3 * size])
        last[at, :size] = high
        last[at, size:] = low
        third[:, at] = (product[:, size:] + terms[:, 3 * size : 4 * size]).T
        give(third, third_hbm, at)
    for at, terms in tiles:
        product = dot(dense[at, :], last[...])
        fourth[:, at] = (product[:, :size] + product[:, size:] + terms[:, 4 * size :]).T
        give(fourth, fourth_hbm, at)
    for copy in copies:
        copy.wait()


def final_vectors(summed, dense, terms):
    states, two = summed.shape
    columns = two // 2
    full = pl.BlockSpec(memory_space=pltpu.VMEM)
    operands = [summed, dense, *terms]
    out = jax.ShapeDtypeStruct((columns, states), F32)
    return pl.pallas_call(
        functools.partial(final_kernel, len(terms)),
        in_specs=[full] * len(operands),
        out_specs=[pl.BlockSpec(memory_space=pltpu.HBM)] * 2,
        out_shape=[out, out],
        scratch_shapes=[
            pltpu.VMEM((columns, states), F32),
            pltpu.VMEM((columns, states), F32),
            pltpu.VMEM((states, two), BF16),
            pltpu.VMEM((states, two), BF16),
            pltpu.SemaphoreType.DMA((2 * len(terms),)),
        ],
        compiler_params=pltpu.CompilerParams(vmem_limit_bytes=12 * 2**20),
        name="final_vectors",
    )(*operands)


def device_spins():
    wide_log = lax.axis_size("wide").bit_length() - 1
    narrow_log = lax.axis_size("narrow").bit_length() - 1
    of_bond = [("wide", wide_log - 1), ("wide", 0), ("narrow", narrow_log - 1), ("narrow", 0)]
    spins = []
    for bond in (0, 2, 3, 1):
        if of_bond[bond] not in spins:
            spins.append(of_bond[bond])
    return spins, [spins.index(spin) for spin in of_bond]


def after(value, token):
    return value + token[0, : value.shape[-1]].astype(value.dtype)


def gathered(early, first, middle, last, holds):
    late = {1: first}
    for at, spin in enumerate(middle, 1):
        for owner in sorted(late):
            late[owner | 1 << at] = partner(late[owner], *spin)
    arrays = [late[owner] for owner in late] + [early[owner] for owner in early if owner]
    owners = [owner for owner in late] + [owner for owner in early if owner]
    places = {owner: (number, 0) for number, owner in enumerate(owners)}
    for group, hold in zip(([*early, 1], [owner for owner in late if owner != 1]), holds):
        if group:
            sent = jnp.concatenate([{**early, **late}[owner] for owner in group], axis=1)
            if hold is not None:
                sent = after(sent, jnp.tile(hold[:1], (1, len(group))))
            for place, owner in enumerate(group):
                places[owner | 1 << len(middle) + 1] = (len(arrays), place)
            arrays.append(partner(sent, *last))
    return arrays, places


def shards(initial, block_values, block_index, bond_sites, *column_operands):
    state = initial[0, 0]
    columns, states = state.shape
    sixteenth = states // 16
    splits = [[6 * sixteenth], [2 * sixteenth, 3 * sixteenth], [2 * sixteenth, 3 * sixteenth]]
    ends = [sum(sum(widths) for widths in splits[: number + 1]) for number in range(3)]
    spins, spin_of_bond = device_spins()
    terms, summed = [], []

    def pieces_of(number, first, holds):
        start = ends[number] - sum(splits[number])
        found = []
        inside = 0
        for width in splits[number]:
            own_parts = {owner: piece[start + inside : start + inside + width] for owner, piece in early.items()}
            found.append(gathered(own_parts, first[inside : inside + width], spins[1:-1], spins[-1], holds))
            inside += width
        return found

    def run(number, pieces, ahead):
        for (arrays, places), width in zip(pieces, splits[number]):
            start = sum(term.shape[0] for term in terms)
            total, term, token = chunk_terms(
                start, width, turned, product, high, low, dense, arrays, places, summed, ahead
            )
            summed[:] = [total]
            terms.append(term)
        return token

    turned, rounded, part = prepare(state, ends[0])
    first = partner(part, *spins[0])
    early = {0: rounded}
    for at, spin in enumerate(spins[1:-1], 1):
        for owner in sorted(early):
            early[owner | 1 << at] = partner(early[owner], *spin)
    dense, product, part, token = low_operator(block_values, block_index, rounded, (ends[0], ends[1]))
    second = partner(part, *spins[0])
    first = after(first, token)
    high, low, part, token = polynomial_columns(
        spins, spin_of_bond, 4, (bond_sites.T, *column_operands), rounded, (ends[1], ends[2]), first
    )
    third = partner(part, *spins[0])
    first_pieces = pieces_of(0, first, (token, None))
    second = after(after(second, token), first_pieces[0][0][1][:1, :columns] * 0)
    second_pieces = pieces_of(1, second, (None, None))
    token = run(0, first_pieces, [])
    third = after(after(third, token), second_pieces[0][0][1][:1, :columns] * 0)
    token = run(1, second_pieces, [third])
    run(2, pieces_of(2, third, (None, token)), [])
    previous, current = final_vectors(*summed, dense, terms)
    return previous[None, None], current[None, None]


def solution(mesh):
    vector = P("wide", "narrow", None, None)
    return jax.shard_map(
        shards,
        mesh=mesh,
        in_specs=(vector,) + (P(),) * 10,
        out_specs=(vector, vector),
        check_vma=False,
    )
```

```python
import functools

import jax
import jax.numpy as jnp
from jax import lax
from jax.experimental import pallas as pl
from jax.experimental.pallas import tpu as pltpu
from jax.sharding import PartitionSpec as P

TILE = 256
ROWS = 512
F32 = jnp.float32
BF16 = jnp.bfloat16


def partner(block, axis, position):
    count = lax.axis_size(axis)
    return lax.ppermute(block, axis, [(at, at ^ (1 << position)) for at in range(count)])


def split(value):
    high = value.astype(BF16)
    return high, (value - high.astype(F32)).astype(BF16)


def dot(left, right):
    return jnp.dot(left, right, preferred_element_type=F32)


def prepare_kernel(state_ref, turned_ref, whole_ref, first_ref):
    turned = state_ref[...].T
    turned_ref[...] = turned
    rounded = turned.astype(BF16)
    whole_ref[...] = rounded
    first_ref[...] = rounded[: first_ref.shape[0]]


def prepare(state, first):
    columns, states = state.shape
    full = pl.BlockSpec(memory_space=pltpu.VMEM)
    return pl.pallas_call(
        prepare_kernel,
        in_specs=[full],
        out_specs=[full] * 3,
        out_shape=[
            jax.ShapeDtypeStruct((states, columns), F32),
            jax.ShapeDtypeStruct((states, columns), BF16),
            jax.ShapeDtypeStruct((first, columns), BF16),
        ],
        compiler_params=pltpu.CompilerParams(vmem_limit_bytes=8 * 2**20),
        name="prepare",
    )(state)


def low_kernel(part, index_ref, values_hbm, state_ref, dense_ref, product_ref, part_ref, token_ref, values, sems):
    brows, kept, size, _ = values.shape
    part_ref[...] = state_ref[part[0] : part[1], :]
    token_ref[...] = jnp.zeros(token_ref.shape, token_ref.dtype)
    rows = TILE // size

    def copy(first):
        at = pl.ds(first, rows)
        return pltpu.make_async_copy(values_hbm.at[at], values.at[at], sems.at[first // rows])

    for first in range(0, brows, rows):
        copy(first).start()
    for first in range(0, brows, rows):
        copy(first).wait()
        tile = slice(first * size, (first + rows) * size)
        dense_ref[tile, :] = jnp.zeros((rows * size, dense_ref.shape[1]), BF16)
        for row in range(first, first + rows):
            for at in range(kept):
                start = pl.multiple_of(index_ref[row, at] * size, size)
                dense_ref[row * size : (row + 1) * size, pl.ds(start, size)] = values[row, at].T
        product_ref[tile, :] = dot(dense_ref[tile, :], state_ref[...])


def low_operator(block_values, block_index, rounded, part):
    brows, kept, size, _ = block_values.shape
    width = brows * size
    columns = rounded.shape[1]
    full = pl.BlockSpec(memory_space=pltpu.VMEM)
    return pl.pallas_call(
        functools.partial(low_kernel, part),
        in_specs=[pl.BlockSpec(memory_space=pltpu.SMEM), pl.BlockSpec(memory_space=pltpu.HBM), full],
        out_specs=[full] * 4,
        out_shape=[
            jax.ShapeDtypeStruct((width, width), BF16),
            jax.ShapeDtypeStruct((width, columns), F32),
            jax.ShapeDtypeStruct((part[1] - part[0], columns), BF16),
            jax.ShapeDtypeStruct((16, columns), BF16),
        ],
        scratch_shapes=[
            pltpu.VMEM(block_values.shape, BF16),
            pltpu.SemaphoreType.DMA((brows * size // TILE,)),
        ],
        compiler_params=pltpu.CompilerParams(vmem_limit_bytes=2 * block_values.size + 4 * 2**20),
        name="low_operator",
    )(block_index, pltpu.with_memory_space_constraint(block_values, pltpu.HBM), rounded)


def bit_of(values, position):
    return jnp.bitwise_and(jnp.right_shift(values, position), 1)


def polynomial_kernel(
    spins,
    spin_of_bond,
    part,
    sites_ref,
    coupling_ref,
    pin_sites_ref,
    pin_partner_ref,
    pinned_ref,
    pin_coupling_ref,
    cross_sites_ref,
    cross_coupling_ref,
    state_ref,
    before_ref,
    high_ref,
    low_ref,
    part_ref,
    token_ref,
    op_high,
    op_low,
    poly_ref,
):
    part_ref[...] = state_ref[part[0] : part[1], :]
    token_ref[...] = jnp.zeros(token_ref.shape, token_ref.dtype)
    whole, size = poly_ref.shape[1:]
    blocks = whole // size
    row = lax.broadcasted_iota(jnp.int32, (size, size), 0)
    col = lax.broadcasted_iota(jnp.int32, (size, size), 1)
    same = row == col
    zero = jnp.zeros((size, size), F32)
    matrix = zero
    field = zero
    for bond in range(sites_ref.shape[1]):
        one, two = sites_ref[0, bond], sites_ref[1, bond]
        strength = coupling_ref[bond]
        differ = jnp.bitwise_xor(bit_of(row, one), bit_of(row, two)).astype(F32)
        flips = jnp.bitwise_xor(
            jnp.left_shift(jnp.int32(1), one), jnp.left_shift(jnp.int32(1), two)
        )
        matrix += jnp.where(col == jnp.bitwise_xor(row, flips), strength * 0.5 * differ, 0.0)
        field += strength * (1.0 - 2.0 * differ) * 0.25
    for pin in range(pin_sites_ref.shape[0]):
        pinned = pinned_ref[pin_partner_ref[pin]]
        aligned = jnp.bitwise_xor(bit_of(row, pin_sites_ref[pin]), pinned).astype(F32)
        field += pin_coupling_ref[pin] * (1.0 - 2.0 * aligned) * 0.25
    own_bits = [bit_of(lax.axis_index(axis), position) for axis, position in spins]
    fields = [[zero, zero] for _ in spins]
    hops = [[zero, zero] for _ in spins]
    for bond, spin in enumerate(spin_of_bond):
        site = cross_sites_ref[bond]
        strength = cross_coupling_ref[bond]
        target = jnp.bitwise_xor(row, jnp.left_shift(jnp.int32(1), site))
        for turned in range(2):
            own = jnp.bitwise_xor(own_bits[spin], turned)
            parity = jnp.bitwise_xor(bit_of(row, site), own).astype(F32)
            fields[spin][turned] += strength * (1.0 - 2.0 * parity) * 0.25
            hops[spin][turned] += jnp.where(col == target, strength * 0.5 * parity, 0.0)
    hop_parts = [[split(hops[spin][turned]) for turned in range(2)] for spin in range(len(spins))]
    op_high[...] = jnp.zeros(op_high.shape, BF16)
    op_low[...] = jnp.zeros(op_low.shape, BF16)
    poly_ref[0] = jnp.zeros((whole, size), F32)
    poly_ref[1] = jnp.zeros((whole, size), F32)
    poly_ref[0, :size, :] = jnp.where(same, 1.0, 0.0)
    for block in range(blocks):
        at = slice(block * size, (block + 1) * size)
        own_field = field
        for spin in range(len(spins)):
            turned = block >> spin & 1
            own_field = own_field + fields[spin][turned]
            other = block ^ 1 << spin
            high, low = hop_parts[spin][turned]
            op_high[at, other * size : (other + 1) * size] = high
            op_low[at, other * size : (other + 1) * size] = low
            if other == 0:
                poly_ref[1, at, :] = hops[spin][turned]
        diagonal = matrix + jnp.where(same, own_field, 0.0)
        high, low = split(diagonal)
        op_high[at, at] = high
        op_low[at, at] = low
        if block == 0:
            poly_ref[1, at, :] = diagonal
    orders = high_ref.shape[1] // size
    tile = min(2 * TILE, whole)
    for order in range(1, orders + 1):
        high, low = split(poly_ref[order])
        high_ref[:, (order - 1) * size : order * size] = high
        low_ref[:, (order - 1) * size : order * size] = low
        if order == orders:
            break
        both = jnp.concatenate([high, low], axis=1)
        for start in range(0, whole, tile):
            at = slice(start, start + tile)
            product = dot(op_high[at, :], both)
            product = product[:, :size] + product[:, size:] + dot(op_low[at, :], high)
            poly_ref[order + 1, at, :] = 2.0 * product - poly_ref[order - 1, at, :]


def polynomial_columns(spins, spin_of_bond, orders, operands, state, part, before):
    columns = state.shape[1]
    whole = columns << len(spins)
    out = jax.ShapeDtypeStruct((whole, orders * columns), BF16)
    return pl.pallas_call(
        functools.partial(polynomial_kernel, spins, spin_of_bond, part),
        in_specs=[pl.BlockSpec(memory_space=pltpu.SMEM)] * len(operands)
        + [pl.BlockSpec(memory_space=pltpu.VMEM), pl.BlockSpec(memory_space=pl.ANY)],
        out_specs=[pl.BlockSpec(memory_space=pltpu.VMEM)] * 4,
        out_shape=[out, out, jax.ShapeDtypeStruct((part[1] - part[0], columns), BF16), jax.ShapeDtypeStruct((16, columns), BF16)],
        scratch_shapes=[
            pltpu.VMEM((whole, whole), BF16),
            pltpu.VMEM((whole, whole), BF16),
            pltpu.VMEM((orders + 1, whole, columns), F32),
        ],
        compiler_params=pltpu.CompilerParams(vmem_limit_bytes=4 * whole * whole + 24 * whole * columns + 4 * 2**20),
        name="polynomial_columns",
    )(*operands, state, before)


def chunk_kernel(start, places, arrays, summed, *refs):
    state_ref, product_ref, high_ref, low_ref, dense_ref = refs[:5]
    piece_refs = refs[5 : 5 + arrays]
    sum_ref, terms_ref, token_ref = refs[-3:]
    token_ref[...] = jnp.zeros(token_ref.shape, token_ref.dtype)
    width = terms_ref.shape[0]
    size = state_ref.shape[1]
    state = state_ref[start : start + width, :]
    product = product_ref[start : start + width, :]
    own, rest = split(state)
    pieces = [own]
    for owner in sorted(places):
        number, place = places[owner]
        pieces.append(piece_refs[number][:, place * size : (place + 1) * size])
    gathered = jnp.concatenate(pieces, axis=1)
    powers = dot(gathered, high_ref[...]) + dot(gathered, low_ref[...]) + dot(rest, high_ref[:size, :])
    one, two, three, four = (powers[:, k * size : (k + 1) * size] for k in range(4))
    both = jnp.concatenate([8.0 * product + 32.0 * one, 4.0 * product + 12.0 * one], axis=1).astype(BF16)
    terms_ref[:, :size] = 24.0 * two + 16.0 * state
    terms_ref[:, size : 2 * size] = 6.0 * two + 3.0 * state
    terms_ref[:, 2 * size : 3 * size] = 8.0 * (three + one)
    terms_ref[:, 3 * size : 4 * size] = three
    terms_ref[:, 4 * size :] = four
    for at in range(0, sum_ref.shape[0], ROWS):
        share = dot(dense_ref[at : at + ROWS, start : start + width], both)
        sum_ref[at : at + ROWS, :] = refs[5 + arrays][at : at + ROWS, :] + share if summed else share


def chunk_terms(start, width, state, product, high, low, dense, arrays, places, summed, ahead):
    states, columns = state.shape
    full = pl.BlockSpec(memory_space=pltpu.VMEM)
    operands = [state, product, high, low, dense, *arrays, *summed]
    return pl.pallas_call(
        functools.partial(chunk_kernel, start, places, len(arrays), len(summed)),
        in_specs=[full] * len(operands) + [pl.BlockSpec(memory_space=pl.ANY)] * len(ahead),
        out_specs=[full] * 3,
        out_shape=[
            jax.ShapeDtypeStruct((states, 2 * columns), F32),
            jax.ShapeDtypeStruct((width, 5 * columns), F32),
            jax.ShapeDtypeStruct((16, columns), BF16),
        ],
        compiler_params=pltpu.CompilerParams(vmem_limit_bytes=12 * 2**20),
        cost_estimate=pl.CostEstimate(flops=4 * 10**9, bytes_accessed=0, transcendentals=0),
        name="chunk_terms",
    )(*operands, *ahead)


def final_kernel(chunks, sum_ref, dense, *refs):
    term_refs = refs[:chunks]
    third_hbm, fourth_hbm, third, fourth, second, last, sems = refs[chunks:]
    size = third.shape[0]
    tiles = []
    row = 0
    for terms in term_refs:
        width = terms.shape[0]
        at = slice(row, row + width)
        second[at, :] = (sum_ref[at, :] + terms[:, : 2 * size]).astype(BF16)
        tiles.append((at, terms))
        row += width
    copies = []

    def give(source, target, at):
        copies.append(pltpu.make_async_copy(source.at[:, at], target.at[:, at], sems.at[len(copies)]))
        copies[-1].start()

    for at, terms in tiles:
        product = dot(dense[at, :], second[...])
        high, low = split(product[:, :size] + terms[:, 2 * size : 3 * size])
        last[at, :size] = high
        last[at, size:] = low
        third[:, at] = (product[:, size:] + terms[:, 3 * size : 4 * size]).T
        give(third, third_hbm, at)
    for at, terms in tiles:
        product = dot(dense[at, :], last[...])
        fourth[:, at] = (product[:, :size] + product[:, size:] + terms[:, 4 * size :]).T
        give(fourth, fourth_hbm, at)
    for copy in copies:
        copy.wait()


def final_vectors(summed, dense, terms):
    states, two = summed.shape
    columns = two // 2
    full = pl.BlockSpec(memory_space=pltpu.VMEM)
    operands = [summed, dense, *terms]
    out = jax.ShapeDtypeStruct((columns, states), F32)
    return pl.pallas_call(
        functools.partial(final_kernel, len(terms)),
        in_specs=[full] * len(operands),
        out_specs=[pl.BlockSpec(memory_space=pltpu.HBM)] * 2,
        out_shape=[out, out],
        scratch_shapes=[
            pltpu.VMEM((columns, states), F32),
            pltpu.VMEM((columns, states), F32),
            pltpu.VMEM((states, two), BF16),
            pltpu.VMEM((states, two), BF16),
            pltpu.SemaphoreType.DMA((2 * len(terms),)),
        ],
        compiler_params=pltpu.CompilerParams(vmem_limit_bytes=12 * 2**20),
        name="final_vectors",
    )(*operands)


def device_spins():
    wide_log = lax.axis_size("wide").bit_length() - 1
    narrow_log = lax.axis_size("narrow").bit_length() - 1
    of_bond = [("wide", wide_log - 1), ("wide", 0), ("narrow", narrow_log - 1), ("narrow", 0)]
    spins = []
    for bond in (0, 2, 3, 1):
        if of_bond[bond] not in spins:
            spins.append(of_bond[bond])
    return spins, [spins.index(spin) for spin in of_bond]


def after(value, token):
    return value + token[0, : value.shape[-1]].astype(value.dtype)


def gathered(early, first, middle, last, hold):
    late = {1: first}
    for at, spin in enumerate(middle, 1):
        for owner in sorted(late):
            late[owner | 1 << at] = partner(late[owner], *spin)
    arrays = [late[owner] for owner in late] + [early[owner] for owner in early if owner]
    owners = [owner for owner in late] + [owner for owner in early if owner]
    places = {owner: (number, 0) for number, owner in enumerate(owners)}
    group = [*early, *late]
    sent = jnp.concatenate([{**early, **late}[owner] for owner in group], axis=1)
    if hold is not None:
        sent = after(sent, jnp.tile(hold[:1], (1, len(group))))
    for place, owner in enumerate(group):
        places[owner | 1 << len(middle) + 1] = (len(arrays), place)
    arrays.append(partner(sent, *last))
    return arrays, places


def shards(initial, block_values, block_index, bond_sites, *column_operands):
    state = initial[0, 0]
    columns, states = state.shape
    sixteenth = states // 16
    splits = [[6 * sixteenth], [2 * sixteenth, 5 * sixteenth], [3 * sixteenth]]
    ends = [sum(sum(widths) for widths in splits[: number + 1]) for number in range(3)]
    spins, spin_of_bond = device_spins()
    terms, summed = [], []

    def pieces_of(number, first, holds):
        start = ends[number] - sum(splits[number])
        found = []
        inside = 0
        for width, hold in zip(splits[number], holds):
            own_parts = {owner: piece[start + inside : start + inside + width] for owner, piece in early.items()}
            found.append(gathered(own_parts, first[inside : inside + width], spins[1:-1], spins[-1], hold))
            inside += width
        return found

    def run(number, pieces, ahead):
        tokens = []
        for (arrays, places), width in zip(pieces, splits[number]):
            start = sum(term.shape[0] for term in terms)
            total, term, token = chunk_terms(
                start, width, turned, product, high, low, dense, arrays, places, summed, ahead
            )
            summed[:] = [total]
            terms.append(term)
            tokens.append(token)
        return tokens

    turned, rounded, part = prepare(state, ends[0])
    first = partner(part, *spins[0])
    early = {0: rounded}
    for at, spin in enumerate(spins[1:-1], 1):
        for owner in sorted(early):
            early[owner | 1 << at] = partner(early[owner], *spin)
    dense, product, part, token = low_operator(block_values, block_index, rounded, (ends[0], ends[1]))
    second = partner(part, *spins[0])
    first = after(first, token)
    high, low, part, token = polynomial_columns(
        spins, spin_of_bond, 4, (bond_sites.T, *column_operands), rounded, (ends[1], ends[2]), first
    )
    third = partner(part, *spins[0])
    first_pieces = pieces_of(0, first, [token])
    second = after(after(second, token), first_pieces[0][0][1][:1, :columns] * 0)
    (token,) = run(0, first_pieces, [])
    second_pieces = pieces_of(1, second, [None, token])
    third = after(after(third, token), second_pieces[0][0][1][:1, :columns] * 0)
    tokens = run(1, second_pieces, [third])
    run(2, pieces_of(2, third, tokens[:1]), [])
    previous, current = final_vectors(*summed, dense, terms)
    return previous[None, None], current[None, None]


def solution(mesh):
    vector = P("wide", "narrow", None, None)
    return jax.shard_map(
        shards,
        mesh=mesh,
        in_specs=(vector,) + (P(),) * 10,
        out_specs=(vector, vector),
        check_vma=False,
    )
```

```python
import functools

import jax
import jax.numpy as jnp
from jax import lax
from jax.experimental import pallas as pl
from jax.experimental.pallas import tpu as pltpu
from jax.sharding import PartitionSpec as P

TILE = 256
ROWS = 512
F32 = jnp.float32
BF16 = jnp.bfloat16


def partner(block, axis, position):
    count = lax.axis_size(axis)
    return lax.ppermute(block, axis, [(at, at ^ (1 << position)) for at in range(count)])


def split(value):
    high = value.astype(BF16)
    return high, (value - high.astype(F32)).astype(BF16)


def dot(left, right):
    return jnp.dot(left, right, preferred_element_type=F32)


def prepare_kernel(state_hbm, turned_ref, whole_ref, first_ref, state, sems):
    states = state.shape[1]
    width = states // sems.shape[0]
    copies = []
    for start in range(0, states, width):
        at = pl.ds(start, width)
        copies.append(pltpu.make_async_copy(state_hbm.at[:, at], state.at[:, at], sems.at[len(copies)]))
        copies[-1].start()
    for start, copy in zip(range(0, states, width), copies):
        copy.wait()
        turned = state[:, start : start + width].T
        turned_ref[start : start + width, :] = turned
        rounded = turned.astype(BF16)
        whole_ref[start : start + width, :] = rounded
        inside = min(max(first_ref.shape[0] - start, 0), width)
        if inside:
            first_ref[start : start + inside, :] = rounded[:inside]


def prepare(state, first):
    columns, states = state.shape
    full = pl.BlockSpec(memory_space=pltpu.VMEM)
    return pl.pallas_call(
        prepare_kernel,
        in_specs=[pl.BlockSpec(memory_space=pltpu.HBM)],
        out_specs=[full] * 3,
        out_shape=[
            jax.ShapeDtypeStruct((states, columns), F32),
            jax.ShapeDtypeStruct((states, columns), BF16),
            jax.ShapeDtypeStruct((first, columns), BF16),
        ],
        scratch_shapes=[pltpu.VMEM((columns, states), F32), pltpu.SemaphoreType.DMA((4,))],
        compiler_params=pltpu.CompilerParams(vmem_limit_bytes=8 * 2**20),
        name="prepare",
    )(pltpu.with_memory_space_constraint(state, pltpu.HBM))


def low_kernel(part, index_ref, values_hbm, state_ref, dense_ref, product_ref, part_ref, token_ref, values, sems):
    brows, kept, size, _ = values.shape
    part_ref[...] = state_ref[part[0] : part[1], :]
    token_ref[...] = jnp.zeros(token_ref.shape, token_ref.dtype)
    rows = TILE // size

    def copy(first):
        at = pl.ds(first, rows)
        return pltpu.make_async_copy(values_hbm.at[at], values.at[at], sems.at[first // rows])

    for first in range(0, brows, rows):
        copy(first).start()
    for first in range(0, brows, rows):
        copy(first).wait()
        tile = slice(first * size, (first + rows) * size)
        dense_ref[tile, :] = jnp.zeros((rows * size, dense_ref.shape[1]), BF16)
        for row in range(first, first + rows):
            for at in range(kept):
                start = pl.multiple_of(index_ref[row, at] * size, size)
                dense_ref[row * size : (row + 1) * size, pl.ds(start, size)] = values[row, at].T
        product_ref[tile, :] = dot(dense_ref[tile, :], state_ref[...])


def low_operator(block_values, block_index, rounded, part):
    brows, kept, size, _ = block_values.shape
    width = brows * size
    columns = rounded.shape[1]
    full = pl.BlockSpec(memory_space=pltpu.VMEM)
    return pl.pallas_call(
        functools.partial(low_kernel, part),
        in_specs=[pl.BlockSpec(memory_space=pltpu.SMEM), pl.BlockSpec(memory_space=pltpu.HBM), full],
        out_specs=[full] * 4,
        out_shape=[
            jax.ShapeDtypeStruct((width, width), BF16),
            jax.ShapeDtypeStruct((width, columns), F32),
            jax.ShapeDtypeStruct((part[1] - part[0], columns), BF16),
            jax.ShapeDtypeStruct((16, columns), BF16),
        ],
        scratch_shapes=[
            pltpu.VMEM(block_values.shape, BF16),
            pltpu.SemaphoreType.DMA((brows * size // TILE,)),
        ],
        compiler_params=pltpu.CompilerParams(vmem_limit_bytes=2 * block_values.size + 4 * 2**20),
        name="low_operator",
    )(block_index, pltpu.with_memory_space_constraint(block_values, pltpu.HBM), rounded)


def bit_of(values, position):
    return jnp.bitwise_and(jnp.right_shift(values, position), 1)


def polynomial_kernel(
    spins,
    spin_of_bond,
    part,
    sites_ref,
    coupling_ref,
    pin_sites_ref,
    pin_partner_ref,
    pinned_ref,
    pin_coupling_ref,
    cross_sites_ref,
    cross_coupling_ref,
    state_ref,
    before_ref,
    high_ref,
    low_ref,
    part_ref,
    token_ref,
    op_high,
    op_low,
    poly_ref,
):
    part_ref[...] = state_ref[part[0] : part[1], :]
    token_ref[...] = jnp.zeros(token_ref.shape, token_ref.dtype)
    whole, size = poly_ref.shape[1:]
    blocks = whole // size
    row = lax.broadcasted_iota(jnp.int32, (size, size), 0)
    col = lax.broadcasted_iota(jnp.int32, (size, size), 1)
    same = row == col
    zero = jnp.zeros((size, size), F32)
    matrix = zero
    field = zero
    for bond in range(sites_ref.shape[1]):
        one, two = sites_ref[0, bond], sites_ref[1, bond]
        strength = coupling_ref[bond]
        differ = jnp.bitwise_xor(bit_of(row, one), bit_of(row, two)).astype(F32)
        flips = jnp.bitwise_xor(
            jnp.left_shift(jnp.int32(1), one), jnp.left_shift(jnp.int32(1), two)
        )
        matrix += jnp.where(col == jnp.bitwise_xor(row, flips), strength * 0.5 * differ, 0.0)
        field += strength * (1.0 - 2.0 * differ) * 0.25
    for pin in range(pin_sites_ref.shape[0]):
        pinned = pinned_ref[pin_partner_ref[pin]]
        aligned = jnp.bitwise_xor(bit_of(row, pin_sites_ref[pin]), pinned).astype(F32)
        field += pin_coupling_ref[pin] * (1.0 - 2.0 * aligned) * 0.25
    own_bits = [bit_of(lax.axis_index(axis), position) for axis, position in spins]
    fields = [[zero, zero] for _ in spins]
    hops = [[zero, zero] for _ in spins]
    for bond, spin in enumerate(spin_of_bond):
        site = cross_sites_ref[bond]
        strength = cross_coupling_ref[bond]
        target = jnp.bitwise_xor(row, jnp.left_shift(jnp.int32(1), site))
        for turned in range(2):
            own = jnp.bitwise_xor(own_bits[spin], turned)
            parity = jnp.bitwise_xor(bit_of(row, site), own).astype(F32)
            fields[spin][turned] += strength * (1.0 - 2.0 * parity) * 0.25
            hops[spin][turned] += jnp.where(col == target, strength * 0.5 * parity, 0.0)
    hop_parts = [[split(hops[spin][turned]) for turned in range(2)] for spin in range(len(spins))]
    op_high[...] = jnp.zeros(op_high.shape, BF16)
    op_low[...] = jnp.zeros(op_low.shape, BF16)
    poly_ref[0] = jnp.zeros((whole, size), F32)
    poly_ref[1] = jnp.zeros((whole, size), F32)
    poly_ref[0, :size, :] = jnp.where(same, 1.0, 0.0)
    for block in range(blocks):
        at = slice(block * size, (block + 1) * size)
        own_field = field
        for spin in range(len(spins)):
            turned = block >> spin & 1
            own_field = own_field + fields[spin][turned]
            other = block ^ 1 << spin
            high, low = hop_parts[spin][turned]
            op_high[at, other * size : (other + 1) * size] = high
            op_low[at, other * size : (other + 1) * size] = low
            if other == 0:
                poly_ref[1, at, :] = hops[spin][turned]
        diagonal = matrix + jnp.where(same, own_field, 0.0)
        high, low = split(diagonal)
        op_high[at, at] = high
        op_low[at, at] = low
        if block == 0:
            poly_ref[1, at, :] = diagonal
    orders = high_ref.shape[1] // size
    tile = min(2 * TILE, whole)
    for order in range(1, orders + 1):
        high, low = split(poly_ref[order])
        high_ref[:, (order - 1) * size : order * size] = high
        low_ref[:, (order - 1) * size : order * size] = low
        if order == orders:
            break
        both = jnp.concatenate([high, low], axis=1)
        for start in range(0, whole, tile):
            at = slice(start, start + tile)
            product = dot(op_high[at, :], both)
            product = product[:, :size] + product[:, size:] + dot(op_low[at, :], high)
            poly_ref[order + 1, at, :] = 2.0 * product - poly_ref[order - 1, at, :]


def polynomial_columns(spins, spin_of_bond, orders, operands, state, part, before):
    columns = state.shape[1]
    whole = columns << len(spins)
    out = jax.ShapeDtypeStruct((whole, orders * columns), BF16)
    return pl.pallas_call(
        functools.partial(polynomial_kernel, spins, spin_of_bond, part),
        in_specs=[pl.BlockSpec(memory_space=pltpu.SMEM)] * len(operands)
        + [pl.BlockSpec(memory_space=pltpu.VMEM), pl.BlockSpec(memory_space=pl.ANY)],
        out_specs=[pl.BlockSpec(memory_space=pltpu.VMEM)] * 4,
        out_shape=[out, out, jax.ShapeDtypeStruct((part[1] - part[0], columns), BF16), jax.ShapeDtypeStruct((16, columns), BF16)],
        scratch_shapes=[
            pltpu.VMEM((whole, whole), BF16),
            pltpu.VMEM((whole, whole), BF16),
            pltpu.VMEM((orders + 1, whole, columns), F32),
        ],
        compiler_params=pltpu.CompilerParams(vmem_limit_bytes=4 * whole * whole + 24 * whole * columns + 4 * 2**20),
        name="polynomial_columns",
    )(*operands, state, before)


def chunk_kernel(start, places, arrays, summed, *refs):
    state_ref, product_ref, high_ref, low_ref, dense_ref = refs[:5]
    piece_refs = refs[5 : 5 + arrays]
    sum_ref, terms_ref, token_ref = refs[-3:]
    token_ref[...] = jnp.zeros(token_ref.shape, token_ref.dtype)
    width = terms_ref.shape[0]
    size = state_ref.shape[1]
    state = state_ref[start : start + width, :]
    product = product_ref[start : start + width, :]
    own, rest = split(state)
    pieces = [own]
    for owner in sorted(places):
        number, place = places[owner]
        pieces.append(piece_refs[number][:, place * size : (place + 1) * size])
    gathered = jnp.concatenate(pieces, axis=1)
    powers = dot(gathered, high_ref[...]) + dot(gathered, low_ref[...]) + dot(rest, high_ref[:size, :])
    one, two, three, four = (powers[:, k * size : (k + 1) * size] for k in range(4))
    both = jnp.concatenate([8.0 * product + 32.0 * one, 4.0 * product + 12.0 * one], axis=1).astype(BF16)
    terms_ref[:, :size] = 24.0 * two + 16.0 * state
    terms_ref[:, size : 2 * size] = 6.0 * two + 3.0 * state
    terms_ref[:, 2 * size : 3 * size] = 8.0 * (three + one)
    terms_ref[:, 3 * size : 4 * size] = three
    terms_ref[:, 4 * size :] = four
    for at in range(0, sum_ref.shape[0], ROWS):
        share = dot(dense_ref[at : at + ROWS, start : start + width], both)
        sum_ref[at : at + ROWS, :] = refs[5 + arrays][at : at + ROWS, :] + share if summed else share


def chunk_terms(start, width, state, product, high, low, dense, arrays, places, summed, ahead):
    states, columns = state.shape
    full = pl.BlockSpec(memory_space=pltpu.VMEM)
    operands = [state, product, high, low, dense, *arrays, *summed]
    return pl.pallas_call(
        functools.partial(chunk_kernel, start, places, len(arrays), len(summed)),
        in_specs=[full] * len(operands) + [pl.BlockSpec(memory_space=pl.ANY)] * len(ahead),
        out_specs=[full] * 3,
        out_shape=[
            jax.ShapeDtypeStruct((states, 2 * columns), F32),
            jax.ShapeDtypeStruct((width, 5 * columns), F32),
            jax.ShapeDtypeStruct((16, columns), BF16),
        ],
        compiler_params=pltpu.CompilerParams(vmem_limit_bytes=12 * 2**20),
        cost_estimate=pl.CostEstimate(flops=4 * 10**9, bytes_accessed=0, transcendentals=0),
        name="chunk_terms",
    )(*operands, *ahead)


def final_kernel(chunks, sum_ref, dense, *refs):
    term_refs = refs[:chunks]
    third_hbm, fourth_hbm, third, fourth, second, last, sems = refs[chunks:]
    size = third.shape[0]
    tiles = []
    row = 0
    for terms in term_refs:
        width = terms.shape[0]
        at = slice(row, row + width)
        second[at, :] = (sum_ref[at, :] + terms[:, : 2 * size]).astype(BF16)
        tiles.append((at, terms))
        row += width
    copies = []

    def give(source, target, at):
        copies.append(pltpu.make_async_copy(source.at[:, at], target.at[:, at], sems.at[len(copies)]))
        copies[-1].start()

    for at, terms in tiles:
        product = dot(dense[at, :], second[...])
        high, low = split(product[:, :size] + terms[:, 2 * size : 3 * size])
        last[at, :size] = high
        last[at, size:] = low
        third[:, at] = (product[:, size:] + terms[:, 3 * size : 4 * size]).T
        give(third, third_hbm, at)
    for at, terms in tiles:
        product = dot(dense[at, :], last[...])
        fourth[:, at] = (product[:, :size] + product[:, size:] + terms[:, 4 * size :]).T
        give(fourth, fourth_hbm, at)
    for copy in copies:
        copy.wait()


def final_vectors(summed, dense, terms):
    states, two = summed.shape
    columns = two // 2
    full = pl.BlockSpec(memory_space=pltpu.VMEM)
    operands = [summed, dense, *terms]
    out = jax.ShapeDtypeStruct((columns, states), F32)
    return pl.pallas_call(
        functools.partial(final_kernel, len(terms)),
        in_specs=[full] * len(operands),
        out_specs=[pl.BlockSpec(memory_space=pltpu.HBM)] * 2,
        out_shape=[out, out],
        scratch_shapes=[
            pltpu.VMEM((columns, states), F32),
            pltpu.VMEM((columns, states), F32),
            pltpu.VMEM((states, two), BF16),
            pltpu.VMEM((states, two), BF16),
            pltpu.SemaphoreType.DMA((2 * len(terms),)),
        ],
        compiler_params=pltpu.CompilerParams(vmem_limit_bytes=12 * 2**20),
        name="final_vectors",
    )(*operands)


def device_spins():
    wide_log = lax.axis_size("wide").bit_length() - 1
    narrow_log = lax.axis_size("narrow").bit_length() - 1
    of_bond = [("wide", wide_log - 1), ("wide", 0), ("narrow", narrow_log - 1), ("narrow", 0)]
    spins = []
    for bond in (0, 2, 3, 1):
        if of_bond[bond] not in spins:
            spins.append(of_bond[bond])
    return spins, [spins.index(spin) for spin in of_bond]


def after(value, token):
    return value + token[0, : value.shape[-1]].astype(value.dtype)


def gathered(early, first, middle, last, hold):
    late = {1: first}
    for at, spin in enumerate(middle, 1):
        for owner in sorted(late):
            late[owner | 1 << at] = partner(late[owner], *spin)
    arrays = [late[owner] for owner in late] + [early[owner] for owner in early if owner]
    owners = [owner for owner in late] + [owner for owner in early if owner]
    places = {owner: (number, 0) for number, owner in enumerate(owners)}
    group = [*early, *late]
    sent = jnp.concatenate([{**early, **late}[owner] for owner in group], axis=1)
    if hold is not None:
        sent = after(sent, jnp.tile(hold[:1], (1, len(group))))
    for place, owner in enumerate(group):
        places[owner | 1 << len(middle) + 1] = (len(arrays), place)
    arrays.append(partner(sent, *last))
    return arrays, places


def shards(initial, block_values, block_index, bond_sites, *column_operands):
    state = initial[0, 0]
    columns, states = state.shape
    sixteenth = states // 16
    splits = [[6 * sixteenth], [3 * sixteenth, 5 * sixteenth], [2 * sixteenth]]
    ends = [sum(sum(widths) for widths in splits[: number + 1]) for number in range(3)]
    spins, spin_of_bond = device_spins()
    terms, summed = [], []

    def pieces_of(number, first, holds):
        start = ends[number] - sum(splits[number])
        found = []
        inside = 0
        for width, hold in zip(splits[number], holds):
            own_parts = {owner: piece[start + inside : start + inside + width] for owner, piece in early.items()}
            found.append(gathered(own_parts, first[inside : inside + width], spins[1:-1], spins[-1], hold))
            inside += width
        return found

    def run(number, pieces, ahead):
        tokens = []
        for (arrays, places), width in zip(pieces, splits[number]):
            start = sum(term.shape[0] for term in terms)
            total, term, token = chunk_terms(
                start, width, turned, product, high, low, dense, arrays, places, summed, ahead
            )
            summed[:] = [total]
            terms.append(term)
            tokens.append(token)
        return tokens

    turned, rounded, part = prepare(state, ends[0])
    first = partner(part, *spins[0])
    early = {0: rounded}
    for at, spin in enumerate(spins[1:-1], 1):
        for owner in sorted(early):
            early[owner | 1 << at] = partner(early[owner], *spin)
    dense, product, part, token = low_operator(block_values, block_index, rounded, (ends[0], ends[1]))
    second = partner(part, *spins[0])
    first = after(first, token)
    high, low, part, token = polynomial_columns(
        spins, spin_of_bond, 4, (bond_sites.T, *column_operands), rounded, (ends[1], ends[2]), first
    )
    third = partner(part, *spins[0])
    first_pieces = pieces_of(0, first, [token])
    second = after(after(second, token), first_pieces[0][0][1][:1, :columns] * 0)
    (token,) = run(0, first_pieces, [])
    second_pieces = pieces_of(1, second, [None, token])
    third = after(after(third, token), second_pieces[0][0][1][:1, :columns] * 0)
    tokens = run(1, second_pieces, [third])
    run(2, pieces_of(2, third, tokens[:1]), [])
    previous, current = final_vectors(*summed, dense, terms)
    return previous[None, None], current[None, None]


def solution(mesh):
    vector = P("wide", "narrow", None, None)
    return jax.shard_map(
        shards,
        mesh=mesh,
        in_specs=(vector,) + (P(),) * 10,
        out_specs=(vector, vector),
        check_vma=False,
    )
```

```python
import functools

import jax
import jax.numpy as jnp
from jax import lax
from jax.experimental import pallas as pl
from jax.experimental.pallas import tpu as pltpu
from jax.sharding import PartitionSpec as P

TILE = 256
ROWS = 512
F32 = jnp.float32
BF16 = jnp.bfloat16


def partner(block, axis, position):
    count = lax.axis_size(axis)
    return lax.ppermute(block, axis, [(at, at ^ (1 << position)) for at in range(count)])


def split(value):
    high = value.astype(BF16)
    return high, (value - high.astype(F32)).astype(BF16)


def dot(left, right):
    return jnp.dot(left, right, preferred_element_type=F32)


def prepare_kernel(state_ref, turned_ref, whole_ref, first_ref):
    turned = state_ref[...].T
    turned_ref[...] = turned
    rounded = turned.astype(BF16)
    whole_ref[...] = rounded
    first_ref[...] = rounded[: first_ref.shape[0]]


def prepare(state, first):
    columns, states = state.shape
    full = pl.BlockSpec(memory_space=pltpu.VMEM)
    return pl.pallas_call(
        prepare_kernel,
        in_specs=[full],
        out_specs=[full] * 3,
        out_shape=[
            jax.ShapeDtypeStruct((states, columns), F32),
            jax.ShapeDtypeStruct((states, columns), BF16),
            jax.ShapeDtypeStruct((first, columns), BF16),
        ],
        compiler_params=pltpu.CompilerParams(vmem_limit_bytes=8 * 2**20),
        name="prepare",
    )(state)


def low_kernel(part, index_hbm, values_hbm, state_ref, dense_ref, product_ref, part_ref, token_ref, values, index_ref, sems, index_sem):
    brows, kept, size, _ = values.shape
    part_ref[...] = state_ref[part[0] : part[1], :]
    token_ref[...] = jnp.zeros(token_ref.shape, token_ref.dtype)
    rows = TILE // size

    def copy(first):
        at = pl.ds(first, rows)
        return pltpu.make_async_copy(values_hbm.at[at], values.at[at], sems.at[first // rows])

    index_copy = pltpu.make_async_copy(index_hbm, index_ref, index_sem)
    index_copy.start()
    for first in range(0, brows, rows):
        copy(first).start()
    index_copy.wait()
    for first in range(0, brows, rows):
        copy(first).wait()
        tile = slice(first * size, (first + rows) * size)
        dense_ref[tile, :] = jnp.zeros((rows * size, dense_ref.shape[1]), BF16)
        for row in range(first, first + rows):
            for at in range(kept):
                start = pl.multiple_of(index_ref[row, at] * size, size)
                dense_ref[row * size : (row + 1) * size, pl.ds(start, size)] = values[row, at].T
        product_ref[tile, :] = dot(dense_ref[tile, :], state_ref[...])


def low_operator(block_values, block_index, rounded, part):
    brows, kept, size, _ = block_values.shape
    width = brows * size
    columns = rounded.shape[1]
    full = pl.BlockSpec(memory_space=pltpu.VMEM)
    return pl.pallas_call(
        functools.partial(low_kernel, part),
        in_specs=[pl.BlockSpec(memory_space=pltpu.HBM), pl.BlockSpec(memory_space=pltpu.HBM), full],
        out_specs=[full] * 4,
        out_shape=[
            jax.ShapeDtypeStruct((width, width), BF16),
            jax.ShapeDtypeStruct((width, columns), F32),
            jax.ShapeDtypeStruct((part[1] - part[0], columns), BF16),
            jax.ShapeDtypeStruct((16, columns), BF16),
        ],
        scratch_shapes=[
            pltpu.VMEM(block_values.shape, BF16),
            pltpu.SMEM(block_index.shape, jnp.int32),
            pltpu.SemaphoreType.DMA((brows * size // TILE,)),
            pltpu.SemaphoreType.DMA,
        ],
        compiler_params=pltpu.CompilerParams(vmem_limit_bytes=2 * block_values.size + 4 * 2**20),
        name="low_operator",
    )(
        pltpu.with_memory_space_constraint(block_index, pltpu.HBM),
        pltpu.with_memory_space_constraint(block_values, pltpu.HBM),
        rounded,
    )


def bit_of(values, position):
    return jnp.bitwise_and(jnp.right_shift(values, position), 1)


def polynomial_kernel(
    spins,
    spin_of_bond,
    part,
    sites_ref,
    coupling_ref,
    pin_sites_ref,
    pin_partner_ref,
    pinned_ref,
    pin_coupling_ref,
    cross_sites_ref,
    cross_coupling_ref,
    state_ref,
    before_ref,
    high_ref,
    low_ref,
    part_ref,
    token_ref,
    op_high,
    op_low,
    poly_ref,
):
    part_ref[...] = state_ref[part[0] : part[1], :]
    token_ref[...] = jnp.zeros(token_ref.shape, token_ref.dtype)
    whole, size = poly_ref.shape[1:]
    blocks = whole // size
    row = lax.broadcasted_iota(jnp.int32, (size, size), 0)
    col = lax.broadcasted_iota(jnp.int32, (size, size), 1)
    same = row == col
    zero = jnp.zeros((size, size), F32)
    matrix = zero
    field = zero
    for bond in range(sites_ref.shape[1]):
        one, two = sites_ref[0, bond], sites_ref[1, bond]
        strength = coupling_ref[bond]
        differ = jnp.bitwise_xor(bit_of(row, one), bit_of(row, two)).astype(F32)
        flips = jnp.bitwise_xor(
            jnp.left_shift(jnp.int32(1), one), jnp.left_shift(jnp.int32(1), two)
        )
        matrix += jnp.where(col == jnp.bitwise_xor(row, flips), strength * 0.5 * differ, 0.0)
        field += strength * (1.0 - 2.0 * differ) * 0.25
    for pin in range(pin_sites_ref.shape[0]):
        pinned = pinned_ref[pin_partner_ref[pin]]
        aligned = jnp.bitwise_xor(bit_of(row, pin_sites_ref[pin]), pinned).astype(F32)
        field += pin_coupling_ref[pin] * (1.0 - 2.0 * aligned) * 0.25
    own_bits = [bit_of(lax.axis_index(axis), position) for axis, position in spins]
    fields = [[zero, zero] for _ in spins]
    hops = [[zero, zero] for _ in spins]
    for bond, spin in enumerate(spin_of_bond):
        site = cross_sites_ref[bond]
        strength = cross_coupling_ref[bond]
        target = jnp.bitwise_xor(row, jnp.left_shift(jnp.int32(1), site))
        for turned in range(2):
            own = jnp.bitwise_xor(own_bits[spin], turned)
            parity = jnp.bitwise_xor(bit_of(row, site), own).astype(F32)
            fields[spin][turned] += strength * (1.0 - 2.0 * parity) * 0.25
            hops[spin][turned] += jnp.where(col == target, strength * 0.5 * parity, 0.0)
    hop_parts = [[split(hops[spin][turned]) for turned in range(2)] for spin in range(len(spins))]
    op_high[...] = jnp.zeros(op_high.shape, BF16)
    op_low[...] = jnp.zeros(op_low.shape, BF16)
    poly_ref[0] = jnp.zeros((whole, size), F32)
    poly_ref[1] = jnp.zeros((whole, size), F32)
    poly_ref[0, :size, :] = jnp.where(same, 1.0, 0.0)
    for block in range(blocks):
        at = slice(block * size, (block + 1) * size)
        own_field = field
        for spin in range(len(spins)):
            turned = block >> spin & 1
            own_field = own_field + fields[spin][turned]
            other = block ^ 1 << spin
            high, low = hop_parts[spin][turned]
            op_high[at, other * size : (other + 1) * size] = high
            op_low[at, other * size : (other + 1) * size] = low
            if other == 0:
                poly_ref[1, at, :] = hops[spin][turned]
        diagonal = matrix + jnp.where(same, own_field, 0.0)
        high, low = split(diagonal)
        op_high[at, at] = high
        op_low[at, at] = low
        if block == 0:
            poly_ref[1, at, :] = diagonal
    orders = high_ref.shape[1] // size
    tile = min(2 * TILE, whole)
    for order in range(1, orders + 1):
        high, low = split(poly_ref[order])
        high_ref[:, (order - 1) * size : order * size] = high
        low_ref[:, (order - 1) * size : order * size] = low
        if order == orders:
            break
        both = jnp.concatenate([high, low], axis=1)
        for start in range(0, whole, tile):
            at = slice(start, start + tile)
            product = dot(op_high[at, :], both)
            product = product[:, :size] + product[:, size:] + dot(op_low[at, :], high)
            poly_ref[order + 1, at, :] = 2.0 * product - poly_ref[order - 1, at, :]


def polynomial_columns(spins, spin_of_bond, orders, operands, state, part, before):
    columns = state.shape[1]
    whole = columns << len(spins)
    out = jax.ShapeDtypeStruct((whole, orders * columns), BF16)
    return pl.pallas_call(
        functools.partial(polynomial_kernel, spins, spin_of_bond, part),
        in_specs=[pl.BlockSpec(memory_space=pltpu.SMEM)] * len(operands)
        + [pl.BlockSpec(memory_space=pltpu.VMEM), pl.BlockSpec(memory_space=pl.ANY)],
        out_specs=[pl.BlockSpec(memory_space=pltpu.VMEM)] * 4,
        out_shape=[out, out, jax.ShapeDtypeStruct((part[1] - part[0], columns), BF16), jax.ShapeDtypeStruct((16, columns), BF16)],
        scratch_shapes=[
            pltpu.VMEM((whole, whole), BF16),
            pltpu.VMEM((whole, whole), BF16),
            pltpu.VMEM((orders + 1, whole, columns), F32),
        ],
        compiler_params=pltpu.CompilerParams(vmem_limit_bytes=4 * whole * whole + 24 * whole * columns + 4 * 2**20),
        name="polynomial_columns",
    )(*operands, state, before)


def chunk_kernel(start, places, arrays, summed, *refs):
    state_ref, product_ref, high_ref, low_ref, dense_ref = refs[:5]
    piece_refs = refs[5 : 5 + arrays]
    sum_ref, terms_ref, token_ref = refs[-3:]
    token_ref[...] = jnp.zeros(token_ref.shape, token_ref.dtype)
    width = terms_ref.shape[0]
    size = state_ref.shape[1]
    state = state_ref[start : start + width, :]
    product = product_ref[start : start + width, :]
    own, rest = split(state)
    pieces = [own]
    for owner in sorted(places):
        number, place = places[owner]
        pieces.append(piece_refs[number][:, place * size : (place + 1) * size])
    gathered = jnp.concatenate(pieces, axis=1)
    powers = dot(gathered, high_ref[...]) + dot(gathered, low_ref[...]) + dot(rest, high_ref[:size, :])
    one, two, three, four = (powers[:, k * size : (k + 1) * size] for k in range(4))
    both = jnp.concatenate([8.0 * product + 32.0 * one, 4.0 * product + 12.0 * one], axis=1).astype(BF16)
    terms_ref[:, :size] = 24.0 * two + 16.0 * state
    terms_ref[:, size : 2 * size] = 6.0 * two + 3.0 * state
    terms_ref[:, 2 * size : 3 * size] = 8.0 * (three + one)
    terms_ref[:, 3 * size : 4 * size] = three
    terms_ref[:, 4 * size :] = four
    for at in range(0, sum_ref.shape[0], ROWS):
        share = dot(dense_ref[at : at + ROWS, start : start + width], both)
        sum_ref[at : at + ROWS, :] = refs[5 + arrays][at : at + ROWS, :] + share if summed else share


def chunk_terms(start, width, state, product, high, low, dense, arrays, places, summed, ahead):
    states, columns = state.shape
    full = pl.BlockSpec(memory_space=pltpu.VMEM)
    operands = [state, product, high, low, dense, *arrays, *summed]
    return pl.pallas_call(
        functools.partial(chunk_kernel, start, places, len(arrays), len(summed)),
        in_specs=[full] * len(operands) + [pl.BlockSpec(memory_space=pl.ANY)] * len(ahead),
        out_specs=[full] * 3,
        out_shape=[
            jax.ShapeDtypeStruct((states, 2 * columns), F32),
            jax.ShapeDtypeStruct((width, 5 * columns), F32),
            jax.ShapeDtypeStruct((16, columns), BF16),
        ],
        compiler_params=pltpu.CompilerParams(vmem_limit_bytes=12 * 2**20),
        cost_estimate=pl.CostEstimate(flops=4 * 10**9, bytes_accessed=0, transcendentals=0),
        name="chunk_terms",
    )(*operands, *ahead)


def final_kernel(chunks, sum_ref, dense, *refs):
    term_refs = refs[:chunks]
    third_hbm, fourth_hbm, third, fourth, second, last, sems = refs[chunks:]
    size = third.shape[0]
    tiles = []
    row = 0
    for terms in term_refs:
        width = terms.shape[0]
        at = slice(row, row + width)
        second[at, :] = (sum_ref[at, :] + terms[:, : 2 * size]).astype(BF16)
        tiles.append((at, terms))
        row += width
    copies = []

    def give(source, target, at):
        copies.append(pltpu.make_async_copy(source.at[:, at], target.at[:, at], sems.at[len(copies)]))
        copies[-1].start()

    for at, terms in tiles:
        product = dot(dense[at, :], second[...])
        high, low = split(product[:, :size] + terms[:, 2 * size : 3 * size])
        last[at, :size] = high
        last[at, size:] = low
        third[:, at] = (product[:, size:] + terms[:, 3 * size : 4 * size]).T
        give(third, third_hbm, at)
    for at, terms in tiles:
        product = dot(dense[at, :], last[...])
        fourth[:, at] = (product[:, :size] + product[:, size:] + terms[:, 4 * size :]).T
        give(fourth, fourth_hbm, at)
    for copy in copies:
        copy.wait()


def final_vectors(summed, dense, terms):
    states, two = summed.shape
    columns = two // 2
    full = pl.BlockSpec(memory_space=pltpu.VMEM)
    operands = [summed, dense, *terms]
    out = jax.ShapeDtypeStruct((columns, states), F32)
    return pl.pallas_call(
        functools.partial(final_kernel, len(terms)),
        in_specs=[full] * len(operands),
        out_specs=[pl.BlockSpec(memory_space=pltpu.HBM)] * 2,
        out_shape=[out, out],
        scratch_shapes=[
            pltpu.VMEM((columns, states), F32),
            pltpu.VMEM((columns, states), F32),
            pltpu.VMEM((states, two), BF16),
            pltpu.VMEM((states, two), BF16),
            pltpu.SemaphoreType.DMA((2 * len(terms),)),
        ],
        compiler_params=pltpu.CompilerParams(vmem_limit_bytes=12 * 2**20),
        name="final_vectors",
    )(*operands)


def device_spins():
    wide_log = lax.axis_size("wide").bit_length() - 1
    narrow_log = lax.axis_size("narrow").bit_length() - 1
    of_bond = [("wide", wide_log - 1), ("wide", 0), ("narrow", narrow_log - 1), ("narrow", 0)]
    spins = []
    for bond in (0, 2, 3, 1):
        if of_bond[bond] not in spins:
            spins.append(of_bond[bond])
    return spins, [spins.index(spin) for spin in of_bond]


def after(value, token):
    return value + token[0, : value.shape[-1]].astype(value.dtype)


def gathered(early, first, middle, last, hold):
    late = {1: first}
    for at, spin in enumerate(middle, 1):
        for owner in sorted(late):
            late[owner | 1 << at] = partner(late[owner], *spin)
    arrays = [late[owner] for owner in late] + [early[owner] for owner in early if owner]
    owners = [owner for owner in late] + [owner for owner in early if owner]
    places = {owner: (number, 0) for number, owner in enumerate(owners)}
    group = [*early, *late]
    sent = jnp.concatenate([{**early, **late}[owner] for owner in group], axis=1)
    if hold is not None:
        sent = after(sent, jnp.tile(hold[:1], (1, len(group))))
    for place, owner in enumerate(group):
        places[owner | 1 << len(middle) + 1] = (len(arrays), place)
    arrays.append(partner(sent, *last))
    return arrays, places


def shards(initial, block_values, block_index, bond_sites, *column_operands):
    state = initial[0, 0]
    columns, states = state.shape
    sixteenth = states // 16
    splits = [[6 * sixteenth], [2 * sixteenth, 5 * sixteenth], [3 * sixteenth]]
    ends = [sum(sum(widths) for widths in splits[: number + 1]) for number in range(3)]
    spins, spin_of_bond = device_spins()
    terms, summed = [], []

    def pieces_of(number, first, holds):
        start = ends[number] - sum(splits[number])
        found = []
        inside = 0
        for width, hold in zip(splits[number], holds):
            own_parts = {owner: piece[start + inside : start + inside + width] for owner, piece in early.items()}
            found.append(gathered(own_parts, first[inside : inside + width], spins[1:-1], spins[-1], hold))
            inside += width
        return found

    def run(number, pieces, ahead):
        tokens = []
        for (arrays, places), width in zip(pieces, splits[number]):
            start = sum(term.shape[0] for term in terms)
            total, term, token = chunk_terms(
                start, width, turned, product, high, low, dense, arrays, places, summed, ahead
            )
            summed[:] = [total]
            terms.append(term)
            tokens.append(token)
        return tokens

    turned, rounded, part = prepare(state, ends[0])
    first = partner(part, *spins[0])
    early = {0: rounded}
    for at, spin in enumerate(spins[1:-1], 1):
        for owner in sorted(early):
            early[owner | 1 << at] = partner(early[owner], *spin)
    dense, product, part, token = low_operator(block_values, block_index, rounded, (ends[0], ends[1]))
    second = partner(part, *spins[0])
    first = after(first, token)
    high, low, part, token = polynomial_columns(
        spins, spin_of_bond, 4, (bond_sites.T, *column_operands), rounded, (ends[1], ends[2]), first
    )
    third = partner(part, *spins[0])
    first_pieces = pieces_of(0, first, [token])
    second = after(after(second, token), first_pieces[0][0][1][:1, :columns] * 0)
    (token,) = run(0, first_pieces, [])
    second_pieces = pieces_of(1, second, [None, token])
    third = after(after(third, token), second_pieces[0][0][1][:1, :columns] * 0)
    tokens = run(1, second_pieces, [third])
    run(2, pieces_of(2, third, tokens[:1]), [])
    previous, current = final_vectors(*summed, dense, terms)
    return previous[None, None], current[None, None]


def solution(mesh):
    vector = P("wide", "narrow", None, None)
    return jax.shard_map(
        shards,
        mesh=mesh,
        in_specs=(vector,) + (P(),) * 10,
        out_specs=(vector, vector),
        check_vma=False,
    )
```

```python
import functools

import jax
import jax.numpy as jnp
from jax import lax
from jax.experimental import pallas as pl
from jax.experimental.pallas import tpu as pltpu
from jax.sharding import PartitionSpec as P

TILE = 256
ROWS = 512
FINAL_ROWS = 1024
F32 = jnp.float32
BF16 = jnp.bfloat16


def partner(block, axis, position):
    count = lax.axis_size(axis)
    return lax.ppermute(block, axis, [(at, at ^ (1 << position)) for at in range(count)])


def split(value):
    high = value.astype(BF16)
    return high, (value - high.astype(F32)).astype(BF16)


def dot(left, right):
    return jnp.dot(left, right, preferred_element_type=F32)


def prepare_kernel(state_ref, turned_ref, whole_ref, first_ref):
    turned = state_ref[...].T
    turned_ref[...] = turned
    rounded = turned.astype(BF16)
    whole_ref[...] = rounded
    first_ref[...] = rounded[: first_ref.shape[0]]


def prepare(state, first):
    columns, states = state.shape
    full = pl.BlockSpec(memory_space=pltpu.VMEM)
    return pl.pallas_call(
        prepare_kernel,
        in_specs=[full],
        out_specs=[full] * 3,
        out_shape=[
            jax.ShapeDtypeStruct((states, columns), F32),
            jax.ShapeDtypeStruct((states, columns), BF16),
            jax.ShapeDtypeStruct((first, columns), BF16),
        ],
        compiler_params=pltpu.CompilerParams(vmem_limit_bytes=8 * 2**20),
        name="prepare",
    )(state)


def low_kernel(part, index_hbm, values_hbm, state_ref, dense_ref, product_ref, part_ref, token_ref, values, index_ref, sems, index_sem):
    brows, kept, size, _ = values.shape
    part_ref[...] = state_ref[part[0] : part[1], :]
    token_ref[...] = jnp.zeros(token_ref.shape, token_ref.dtype)
    rows = TILE // size

    def copy(first):
        at = pl.ds(first, rows)
        return pltpu.make_async_copy(values_hbm.at[at], values.at[at], sems.at[first // rows])

    index_copy = pltpu.make_async_copy(index_hbm, index_ref, index_sem)
    index_copy.start()
    for first in range(0, brows, rows):
        copy(first).start()
    index_copy.wait()
    for first in range(0, brows, rows):
        copy(first).wait()
        tile = slice(first * size, (first + rows) * size)
        dense_ref[tile, :] = jnp.zeros((rows * size, dense_ref.shape[1]), BF16)
        for row in range(first, first + rows):
            for at in range(kept):
                start = pl.multiple_of(index_ref[row, at] * size, size)
                dense_ref[row * size : (row + 1) * size, pl.ds(start, size)] = values[row, at].T
        product_ref[tile, :] = dot(dense_ref[tile, :], state_ref[...])


def low_operator(block_values, block_index, rounded, part):
    brows, kept, size, _ = block_values.shape
    width = brows * size
    columns = rounded.shape[1]
    full = pl.BlockSpec(memory_space=pltpu.VMEM)
    return pl.pallas_call(
        functools.partial(low_kernel, part),
        in_specs=[pl.BlockSpec(memory_space=pltpu.HBM), pl.BlockSpec(memory_space=pltpu.HBM), full],
        out_specs=[full] * 4,
        out_shape=[
            jax.ShapeDtypeStruct((width, width), BF16),
            jax.ShapeDtypeStruct((width, columns), F32),
            jax.ShapeDtypeStruct((part[1] - part[0], columns), BF16),
            jax.ShapeDtypeStruct((16, columns), BF16),
        ],
        scratch_shapes=[
            pltpu.VMEM(block_values.shape, BF16),
            pltpu.SMEM(block_index.shape, jnp.int32),
            pltpu.SemaphoreType.DMA((brows * size // TILE,)),
            pltpu.SemaphoreType.DMA,
        ],
        compiler_params=pltpu.CompilerParams(vmem_limit_bytes=2 * block_values.size + 4 * 2**20),
        name="low_operator",
    )(
        pltpu.with_memory_space_constraint(block_index, pltpu.HBM),
        pltpu.with_memory_space_constraint(block_values, pltpu.HBM),
        rounded,
    )


def bit_of(values, position):
    return jnp.bitwise_and(jnp.right_shift(values, position), 1)


def polynomial_kernel(
    spins,
    spin_of_bond,
    part,
    sites_ref,
    coupling_ref,
    pin_sites_ref,
    pin_partner_ref,
    pinned_ref,
    pin_coupling_ref,
    cross_sites_ref,
    cross_coupling_ref,
    state_ref,
    before_ref,
    high_ref,
    low_ref,
    part_ref,
    token_ref,
    op_high,
    op_low,
    poly_ref,
):
    part_ref[...] = state_ref[part[0] : part[1], :]
    token_ref[...] = jnp.zeros(token_ref.shape, token_ref.dtype)
    whole, size = poly_ref.shape[1:]
    blocks = whole // size
    row = lax.broadcasted_iota(jnp.int32, (size, size), 0)
    col = lax.broadcasted_iota(jnp.int32, (size, size), 1)
    same = row == col
    zero = jnp.zeros((size, size), F32)
    matrix = zero
    field = zero
    for bond in range(sites_ref.shape[1]):
        one, two = sites_ref[0, bond], sites_ref[1, bond]
        strength = coupling_ref[bond]
        differ = jnp.bitwise_xor(bit_of(row, one), bit_of(row, two)).astype(F32)
        flips = jnp.bitwise_xor(
            jnp.left_shift(jnp.int32(1), one), jnp.left_shift(jnp.int32(1), two)
        )
        matrix += jnp.where(col == jnp.bitwise_xor(row, flips), strength * 0.5 * differ, 0.0)
        field += strength * (1.0 - 2.0 * differ) * 0.25
    for pin in range(pin_sites_ref.shape[0]):
        pinned = pinned_ref[pin_partner_ref[pin]]
        aligned = jnp.bitwise_xor(bit_of(row, pin_sites_ref[pin]), pinned).astype(F32)
        field += pin_coupling_ref[pin] * (1.0 - 2.0 * aligned) * 0.25
    own_bits = [bit_of(lax.axis_index(axis), position) for axis, position in spins]
    fields = [[zero, zero] for _ in spins]
    hops = [[zero, zero] for _ in spins]
    for bond, spin in enumerate(spin_of_bond):
        site = cross_sites_ref[bond]
        strength = cross_coupling_ref[bond]
        target = jnp.bitwise_xor(row, jnp.left_shift(jnp.int32(1), site))
        for turned in range(2):
            own = jnp.bitwise_xor(own_bits[spin], turned)
            parity = jnp.bitwise_xor(bit_of(row, site), own).astype(F32)
            fields[spin][turned] += strength * (1.0 - 2.0 * parity) * 0.25
            hops[spin][turned] += jnp.where(col == target, strength * 0.5 * parity, 0.0)
    hop_parts = [[split(hops[spin][turned]) for turned in range(2)] for spin in range(len(spins))]
    op_high[...] = jnp.zeros(op_high.shape, BF16)
    op_low[...] = jnp.zeros(op_low.shape, BF16)
    poly_ref[0] = jnp.zeros((whole, size), F32)
    poly_ref[1] = jnp.zeros((whole, size), F32)
    poly_ref[0, :size, :] = jnp.where(same, 1.0, 0.0)
    for block in range(blocks):
        at = slice(block * size, (block + 1) * size)
        own_field = field
        for spin in range(len(spins)):
            turned = block >> spin & 1
            own_field = own_field + fields[spin][turned]
            other = block ^ 1 << spin
            high, low = hop_parts[spin][turned]
            op_high[at, other * size : (other + 1) * size] = high
            op_low[at, other * size : (other + 1) * size] = low
            if other == 0:
                poly_ref[1, at, :] = hops[spin][turned]
        diagonal = matrix + jnp.where(same, own_field, 0.0)
        high, low = split(diagonal)
        op_high[at, at] = high
        op_low[at, at] = low
        if block == 0:
            poly_ref[1, at, :] = diagonal
    orders = high_ref.shape[1] // size
    tile = min(2 * TILE, whole)
    for order in range(1, orders + 1):
        high, low = split(poly_ref[order])
        high_ref[:, (order - 1) * size : order * size] = high
        low_ref[:, (order - 1) * size : order * size] = low
        if order == orders:
            break
        both = jnp.concatenate([high, low], axis=1)
        for start in range(0, whole, tile):
            at = slice(start, start + tile)
            product = dot(op_high[at, :], both)
            product = product[:, :size] + product[:, size:] + dot(op_low[at, :], high)
            poly_ref[order + 1, at, :] = 2.0 * product - poly_ref[order - 1, at, :]


def polynomial_columns(spins, spin_of_bond, orders, operands, state, part, before):
    columns = state.shape[1]
    whole = columns << len(spins)
    out = jax.ShapeDtypeStruct((whole, orders * columns), BF16)
    return pl.pallas_call(
        functools.partial(polynomial_kernel, spins, spin_of_bond, part),
        in_specs=[pl.BlockSpec(memory_space=pltpu.SMEM)] * len(operands)
        + [pl.BlockSpec(memory_space=pltpu.VMEM), pl.BlockSpec(memory_space=pl.ANY)],
        out_specs=[pl.BlockSpec(memory_space=pltpu.VMEM)] * 4,
        out_shape=[out, out, jax.ShapeDtypeStruct((part[1] - part[0], columns), BF16), jax.ShapeDtypeStruct((16, columns), BF16)],
        scratch_shapes=[
            pltpu.VMEM((whole, whole), BF16),
            pltpu.VMEM((whole, whole), BF16),
            pltpu.VMEM((orders + 1, whole, columns), F32),
        ],
        compiler_params=pltpu.CompilerParams(vmem_limit_bytes=4 * whole * whole + 24 * whole * columns + 4 * 2**20),
        name="polynomial_columns",
    )(*operands, state, before)


def chunk_kernel(start, places, arrays, summed, *refs):
    state_ref, product_ref, high_ref, low_ref, dense_ref = refs[:5]
    piece_refs = refs[5 : 5 + arrays]
    sum_ref, terms_ref, token_ref = refs[-3:]
    token_ref[...] = jnp.zeros(token_ref.shape, token_ref.dtype)
    width = terms_ref.shape[0]
    size = state_ref.shape[1]
    state = state_ref[start : start + width, :]
    product = product_ref[start : start + width, :]
    own, rest = split(state)
    pieces = [own]
    for owner in sorted(places):
        number, place = places[owner]
        pieces.append(piece_refs[number][:, place * size : (place + 1) * size])
    gathered = jnp.concatenate(pieces, axis=1)
    powers = dot(gathered, high_ref[...]) + dot(gathered, low_ref[...]) + dot(rest, high_ref[:size, :])
    one, two, three, four = (powers[:, k * size : (k + 1) * size] for k in range(4))
    both = jnp.concatenate([8.0 * product + 32.0 * one, 4.0 * product + 12.0 * one], axis=1).astype(BF16)
    terms_ref[:, :size] = 24.0 * two + 16.0 * state
    terms_ref[:, size : 2 * size] = 6.0 * two + 3.0 * state
    terms_ref[:, 2 * size : 3 * size] = 8.0 * (three + one)
    terms_ref[:, 3 * size : 4 * size] = three
    terms_ref[:, 4 * size :] = four
    for at in range(0, sum_ref.shape[0], ROWS):
        share = dot(dense_ref[at : at + ROWS, start : start + width], both)
        sum_ref[at : at + ROWS, :] = refs[5 + arrays][at : at + ROWS, :] + share if summed else share


def chunk_terms(start, width, state, product, high, low, dense, arrays, places, summed, ahead):
    states, columns = state.shape
    full = pl.BlockSpec(memory_space=pltpu.VMEM)
    operands = [state, product, high, low, dense, *arrays, *summed]
    return pl.pallas_call(
        functools.partial(chunk_kernel, start, places, len(arrays), len(summed)),
        in_specs=[full] * len(operands) + [pl.BlockSpec(memory_space=pl.ANY)] * len(ahead),
        out_specs=[full] * 3,
        out_shape=[
            jax.ShapeDtypeStruct((states, 2 * columns), F32),
            jax.ShapeDtypeStruct((width, 5 * columns), F32),
            jax.ShapeDtypeStruct((16, columns), BF16),
        ],
        compiler_params=pltpu.CompilerParams(vmem_limit_bytes=12 * 2**20),
        cost_estimate=pl.CostEstimate(flops=4 * 10**9, bytes_accessed=0, transcendentals=0),
        name="chunk_terms",
    )(*operands, *ahead)


def final_kernel(chunks, sum_ref, dense, *refs):
    term_refs = refs[:chunks]
    third_hbm, fourth_hbm, third, fourth, second, last, sems = refs[chunks:]
    size = third.shape[0]
    states = dense.shape[0]
    tiles = {start: [] for start in range(0, states, FINAL_ROWS)}
    row = 0
    for terms in term_refs:
        width = terms.shape[0]
        second[row : row + width, :] = (sum_ref[row : row + width, :] + terms[:, : 2 * size]).astype(BF16)
        for start, pieces in tiles.items():
            low, high = max(row, start), min(row + width, start + FINAL_ROWS)
            if low < high:
                pieces.append((low, high, (terms, low - row)))
        row += width
    copies = []

    def give(source, target, at):
        copies.append(pltpu.make_async_copy(source.at[:, at], target.at[:, at], sems.at[len(copies)]))
        copies[-1].start()

    for start, pieces in tiles.items():
        product = dot(dense[start : start + FINAL_ROWS, :], second[...])
        for low, high, (terms_ref, inside) in pieces:
            at = slice(low, high)
            terms = terms_ref[inside : inside + high - low, :]
            here = product[low - start : high - start]
            large, small = split(here[:, :size] + terms[:, 2 * size : 3 * size])
            last[at, :size] = large
            last[at, size:] = small
            third[:, at] = (here[:, size:] + terms[:, 3 * size : 4 * size]).T
            give(third, third_hbm, at)
    for start, pieces in tiles.items():
        product = dot(dense[start : start + FINAL_ROWS, :], last[...])
        for low, high, (terms_ref, inside) in pieces:
            at = slice(low, high)
            terms = terms_ref[inside : inside + high - low, :]
            here = product[low - start : high - start]
            fourth[:, at] = (here[:, :size] + here[:, size:] + terms[:, 4 * size :]).T
            give(fourth, fourth_hbm, at)
    for copy in copies:
        copy.wait()


def final_vectors(summed, dense, terms):
    states, two = summed.shape
    columns = two // 2
    full = pl.BlockSpec(memory_space=pltpu.VMEM)
    operands = [summed, dense, *terms]
    out = jax.ShapeDtypeStruct((columns, states), F32)
    return pl.pallas_call(
        functools.partial(final_kernel, len(terms)),
        in_specs=[full] * len(operands),
        out_specs=[pl.BlockSpec(memory_space=pltpu.HBM)] * 2,
        out_shape=[out, out],
        scratch_shapes=[
            pltpu.VMEM((columns, states), F32),
            pltpu.VMEM((columns, states), F32),
            pltpu.VMEM((states, two), BF16),
            pltpu.VMEM((states, two), BF16),
            pltpu.SemaphoreType.DMA((2 * (len(terms) + states // FINAL_ROWS),)),
        ],
        compiler_params=pltpu.CompilerParams(vmem_limit_bytes=12 * 2**20),
        name="final_vectors",
    )(*operands)


def device_spins():
    wide_log = lax.axis_size("wide").bit_length() - 1
    narrow_log = lax.axis_size("narrow").bit_length() - 1
    of_bond = [("wide", wide_log - 1), ("wide", 0), ("narrow", narrow_log - 1), ("narrow", 0)]
    spins = []
    for bond in (0, 2, 3, 1):
        if of_bond[bond] not in spins:
            spins.append(of_bond[bond])
    return spins, [spins.index(spin) for spin in of_bond]


def after(value, token):
    return value + token[0, : value.shape[-1]].astype(value.dtype)


def gathered(early, first, middle, last, hold):
    late = {1: first}
    for at, spin in enumerate(middle, 1):
        for owner in sorted(late):
            late[owner | 1 << at] = partner(late[owner], *spin)
    arrays = [late[owner] for owner in late] + [early[owner] for owner in early if owner]
    owners = [owner for owner in late] + [owner for owner in early if owner]
    places = {owner: (number, 0) for number, owner in enumerate(owners)}
    group = [*early, *late]
    sent = jnp.concatenate([{**early, **late}[owner] for owner in group], axis=1)
    if hold is not None:
        sent = after(sent, jnp.tile(hold[:1], (1, len(group))))
    for place, owner in enumerate(group):
        places[owner | 1 << len(middle) + 1] = (len(arrays), place)
    arrays.append(partner(sent, *last))
    return arrays, places


def shards(initial, block_values, block_index, bond_sites, *column_operands):
    state = initial[0, 0]
    columns, states = state.shape
    sixteenth = states // 16
    splits = [[6 * sixteenth], [2 * sixteenth, 5 * sixteenth], [3 * sixteenth]]
    ends = [sum(sum(widths) for widths in splits[: number + 1]) for number in range(3)]
    spins, spin_of_bond = device_spins()
    terms, summed = [], []

    def pieces_of(number, first, holds):
        start = ends[number] - sum(splits[number])
        found = []
        inside = 0
        for width, hold in zip(splits[number], holds):
            own_parts = {owner: piece[start + inside : start + inside + width] for owner, piece in early.items()}
            found.append(gathered(own_parts, first[inside : inside + width], spins[1:-1], spins[-1], hold))
            inside += width
        return found

    def run(number, pieces, ahead):
        tokens = []
        for (arrays, places), width in zip(pieces, splits[number]):
            start = sum(term.shape[0] for term in terms)
            total, term, token = chunk_terms(
                start, width, turned, product, high, low, dense, arrays, places, summed, ahead
            )
            summed[:] = [total]
            terms.append(term)
            tokens.append(token)
        return tokens

    turned, rounded, part = prepare(state, ends[0])
    first = partner(part, *spins[0])
    early = {0: rounded}
    for at, spin in enumerate(spins[1:-1], 1):
        for owner in sorted(early):
            early[owner | 1 << at] = partner(early[owner], *spin)
    dense, product, part, token = low_operator(block_values, block_index, rounded, (ends[0], ends[1]))
    second = partner(part, *spins[0])
    first = after(first, token)
    high, low, part, token = polynomial_columns(
        spins, spin_of_bond, 4, (bond_sites.T, *column_operands), rounded, (ends[1], ends[2]), first
    )
    third = partner(part, *spins[0])
    first_pieces = pieces_of(0, first, [token])
    second = after(after(second, token), first_pieces[0][0][1][:1, :columns] * 0)
    (token,) = run(0, first_pieces, [])
    second_pieces = pieces_of(1, second, [None, token])
    third = after(after(third, token), second_pieces[0][0][1][:1, :columns] * 0)
    tokens = run(1, second_pieces, [third])
    run(2, pieces_of(2, third, tokens[:1]), [])
    previous, current = final_vectors(*summed, dense, terms)
    return previous[None, None], current[None, None]


def solution(mesh):
    vector = P("wide", "narrow", None, None)
    return jax.shard_map(
        shards,
        mesh=mesh,
        in_specs=(vector,) + (P(),) * 10,
        out_specs=(vector, vector),
        check_vma=False,
    )
```
